32 devices in a mesh: dp: 8 (over z, x), ctx: 4 (over y, core).
Axes of the slice: x: 2, y: 2, z: 4, core: 2. Of those that a mesh axis runs over, the one named last changes fastest.
Arguments:
- tokens: bfloat16 [16, 2048, 576], P('dp', 'ctx'), may hold values from -6 to 6
- segments: int32 [16, 2048], P('dp', 'ctx'), may hold values from 0 to 2, as said below
- attn_gain: bfloat16 [576], P('dp'), may hold values from 0.5 to 1.5
- query_weight: bfloat16 [576, 576], P('dp', 'ctx'), may hold values from -0.375 to 0.375
- key_matrix: bfloat16 [576, 192], P('dp', 'ctx'), may hold values from -0.375 to 0.375
- value_matrix: bfloat16 [576, 192], P('dp', 'ctx'), may hold values from -0.25 to 0.25
- out_weight: bfloat16 [576, 576], P('dp', 'ctx'), may hold values from -0.75 to 0.75
- mlp_gain: bfloat16 [576], P('dp'), may hold values from 0.5 to 1.5
- gate_weight: bfloat16 [576, 1536], P('dp', 'ctx'), may hold values from -0.25 to 0.25
- up_weight: bfloat16 [576, 1536], P('dp', 'ctx'), may hold values from -0.25 to 0.25
- down_weight: bfloat16 [1536, 576], P('dp', 'ctx'), may hold values from -0.21875 to 0.21875
- cotangent: bfloat16 [16, 2048, 576], P('dp', 'ctx'), may hold values from -6 to 6
Outputs:
- output: bfloat16 [16, 2048, 576], P('dp', 'ctx')
- token_grad: bfloat16 [16, 2048, 576], P('dp', 'ctx')
- attn_gain_grad: float32 [576], P('dp')
- query_grad: float32 [576, 576], P('dp', 'ctx')
- key_grad: float32 [576, 192], P('dp', 'ctx')
- value_grad: float32 [576, 192], P('dp', 'ctx')
- out_grad: float32 [576, 576], P('dp', 'ctx')
- mlp_gain_grad: float32 [576], P('dp')
- gate_grad: float32 [576, 1536], P('dp', 'ctx')
- up_grad: float32 [576, 1536], P('dp', 'ctx')
- down_grad: float32 [1536, 576], P('dp', 'ctx')
The draws below stay inside these ranges and needn't reach their ends.
Inputs may be any that keep to these rules, and one draw needn't show every extreme that they name: `segments`: each sequence holds three documents numbered 0, 1, 2 in order; document 0 ends and document 1 starts within the first 512 tokens, document 1 ends and document 2 starts within the last 512 tokens, and no document is empty.
All inputs are finite; a program needn't handle non-finite values.
Results may differ from the reference program's by a relative error of at most 0.018.
Values may be sent and summed in bfloat16 or wider, within the bound.
No kernel may reach another device: no remote copies, remote signals or barrier semaphores. Data moves between devices by JAX's collectives and lax.ppermute only.
A program may use at most 192 MiB of HBM per device.

```python
import math
import jax
import jax.numpy as jnp
from jax import lax

MODEL_WIDTH = 576
QUERY_HEADS = 9
KEY_VALUE_HEADS = 3
HEAD_SIZE = 64
FF = 1536
SEQ_TOK = 512
LEN = 2048
SEQS = 16


def draw_segments(key, part):
    key = jax.random.fold_in(key, 11)
    key_start, key_stop = jax.random.split(key, 2)
    index = jnp.arange(LEN, dtype=jnp.int32)[None, :]
    begin = jax.random.randint(key_start, (SEQS, 1), 1, SEQ_TOK)
    finish = jax.random.randint(key_stop, (SEQS, 1), LEN - SEQ_TOK + 1, LEN)
    return ((index >= begin).astype(jnp.int32) + (index >= finish).astype(jnp.int32)).astype(jnp.int32)


def strengthened(result, stream_key, source, target, shards_of, factor):
    def block_of(axis_at):
        return (jnp.arange(result.shape[axis_at]) // (result.shape[axis_at] // shards_of)).reshape((-1,) + (1,) * (result.ndim - 1 - axis_at))

    one_side = jax.random.permutation(stream_key, shards_of)[block_of(target)]
    other_side = (block_of(target) + shards_of // 2) % shards_of
    return jnp.where((block_of(source) == one_side) | (block_of(source) == other_side), factor * result, result)


def shard_levels(stream_key, extent, cuts, least, high):
    factor_of, own = 1.0, jax.random.fold_in(stream_key, 6)
    for dim, parts in cuts:
        heights = jnp.exp(jax.random.uniform(jax.random.fold_in(own, dim), (parts,), jnp.float32, least / len(cuts), high / len(cuts)))
        factor_of = factor_of * jnp.repeat(heights, extent[dim] // parts).reshape([-1 if axis == dim else 1 for axis in range(len(extent))])
    return factor_of


def noise(stream_key, extent, deviation, reach, pieces=(), held_as=jnp.bfloat16):
    level = shard_levels(stream_key, extent, pieces, -0.22, 0.18) if pieces else 1.0
    result = jax.random.normal(stream_key, extent, jnp.float32) * deviation * level
    return jnp.minimum(jnp.maximum(result, -reach), reach).astype(held_as)


def noise_with(rng, extent, width, limit, cuts, heavy, kind=jnp.bfloat16):
    values = width * jax.random.normal(rng, extent, jnp.float32)
    if cuts:
        values = values * shard_levels(rng, extent, cuts, -0.22, 0.18)
    return jnp.clip(strengthened(values, jax.random.fold_in(rng, 3), *heavy), -limit, limit).astype(kind)


def setup_inputs(seed: int = 0) -> dict:
    streams_of = jax.random.split(jax.random.key(seed), 13)
    tokens = noise_with(streams_of[0], (SEQS, LEN, MODEL_WIDTH), 1.0, 6.0, ((0, 8), (1, 4)), (0, 2, 8, 2.0))
    segments = draw_segments(jax.random.fold_in(streams_of[12], 71), 0)
    attn_gain = jnp.clip(1.0 + 0.1 * jax.random.normal(streams_of[2], (MODEL_WIDTH,), jnp.float32), 0.5, 1.5).astype(jnp.bfloat16)
    query_weight = noise(streams_of[3], (MODEL_WIDTH, QUERY_HEADS * HEAD_SIZE), (MODEL_WIDTH // 2) ** -0.5, 0.375, ((0, 8), (1, 4)))
    key_matrix = noise(streams_of[4], (MODEL_WIDTH, KEY_VALUE_HEADS * HEAD_SIZE), (MODEL_WIDTH // 2) ** -0.5, 0.375, ((0, 8), (1, 4)))
    value_matrix = noise(streams_of[5], (MODEL_WIDTH, KEY_VALUE_HEADS * HEAD_SIZE), MODEL_WIDTH ** -0.5, 0.25, ((0, 8), (1, 4)))
    out_weight = noise(streams_of[6], (QUERY_HEADS * HEAD_SIZE, MODEL_WIDTH), HEAD_SIZE ** -0.5, 0.75, ((0, 8), (1, 4)))
    mlp_gain = jnp.clip(1.0 + 0.1 * jax.random.normal(streams_of[7], (MODEL_WIDTH,), jnp.float32), 0.5, 1.5).astype(jnp.bfloat16)
    gate_weight = noise(streams_of[8], (MODEL_WIDTH, FF), MODEL_WIDTH ** -0.5, 0.25, ((0, 8), (1, 4)))
    up_weight = noise(streams_of[9], (MODEL_WIDTH, FF), MODEL_WIDTH ** -0.5, 0.25, ((0, 8), (1, 4)))
    down_weight = noise(streams_of[10], (FF, MODEL_WIDTH), (FF // 2) ** -0.5, 0.21875, ((0, 8), (1, 4)))
    cotangent = noise(streams_of[11], (SEQS, LEN, MODEL_WIDTH), 1.0, 6.0, ((0, 8), (1, 4)))
    return {"tokens": tokens, "segments": segments, "attn_gain": attn_gain, "query_weight": query_weight, "key_matrix": key_matrix, "value_matrix": value_matrix, "out_weight": out_weight, "mlp_gain": mlp_gain, "gate_weight": gate_weight, "up_weight": up_weight, "down_weight": down_weight, "cotangent": cotangent}


@jax.custom_vjp
def low(v):
    return lax.optimization_barrier(v.astype(jnp.bfloat16)).astype(jnp.float32)

@jax.custom_vjp
def low_back(v):
    return v

def low_keep(v):
    return (low(v), None)

def low_pass(kept, grad):
    return (grad,)

def back_keep(v):
    return (v, None)

def back_low(kept, grad):
    return (low(grad),)
low.defvjp(low_keep, low_pass)
low_back.defvjp(back_keep, back_low)
epsilon = 1e-05
rope_base = 100000.0

def precise_product(left, right):
    return jnp.dot(left, right, precision=lax.Precision.HIGHEST)

def rms_norm(hidden_in, gain):
    return hidden_in * lax.rsqrt(lax.optimization_barrier(jnp.mean(hidden_in * hidden_in, axis=-1, keepdims=True)) + epsilon) * gain

def angles(positions):
    half_index = jnp.arange(HEAD_SIZE // 2).astype(jnp.float32)
    inverse = rope_base ** (-2.0 * half_index / HEAD_SIZE)
    phase = positions.astype(jnp.float32)[:, None] * inverse[None, :]
    phase = jnp.concatenate([phase, phase], axis=-1)
    return (jnp.cos(phase), jnp.sin(phase))

def apply_rotation(flat, cosine_table, sine_table, heads):
    row_count = flat.shape[0]
    split_heads = flat.reshape(row_count, heads, HEAD_SIZE)
    half_width = HEAD_SIZE // 2
    turned = jnp.concatenate([-split_heads[..., half_width:], split_heads[..., :half_width]], axis=-1)
    return (split_heads * cosine_table[:, None, :] + turned * sine_table[:, None, :]).reshape(row_count, heads * HEAD_SIZE)

def doc_positions(local_ids, all_ids, row_start):
    index = row_start + jnp.arange(local_ids.shape[0], dtype=jnp.int32)
    before = lax.optimization_barrier(jnp.sum((all_ids[None, :] < local_ids[:, None]).astype(jnp.int32), axis=1)).astype(jnp.int32)
    return index - before

def decoder_layer(hidden_in, doc_ids, attn_gain, query_weight, key_matrix, value_matrix, out_weight, mlp_gain, gate_weight, up_weight, down_weight):
    sequence_length = hidden_in.shape[0]
    cosine_table, sine_table = angles(doc_positions(doc_ids, doc_ids, 0))
    normalized_input = low(rms_norm(hidden_in, attn_gain))
    queries = low(apply_rotation(low_back(precise_product(normalized_input, query_weight)), cosine_table, sine_table, QUERY_HEADS))
    rotated_keys = low(apply_rotation(low_back(precise_product(normalized_input, key_matrix)), cosine_table, sine_table, KEY_VALUE_HEADS))
    value_rows = low(low_back(precise_product(normalized_input, value_matrix)))
    position = jnp.arange(sequence_length, dtype=jnp.int32)
    allowed = (doc_ids[:, None] == doc_ids[None, :]) & (position[None, :] <= position[:, None])
    query_heads = queries.reshape(sequence_length, QUERY_HEADS, HEAD_SIZE).transpose(1, 0, 2)
    key_head_rows = jnp.repeat(rotated_keys.reshape(sequence_length, KEY_VALUE_HEADS, HEAD_SIZE).transpose(1, 0, 2), QUERY_HEADS // KEY_VALUE_HEADS, axis=0)
    value_head_rows = jnp.repeat(value_rows.reshape(sequence_length, KEY_VALUE_HEADS, HEAD_SIZE).transpose(1, 0, 2), QUERY_HEADS // KEY_VALUE_HEADS, axis=0)
    inv_root = 1.0 / math.sqrt(HEAD_SIZE)

    def one_head(operands):
        query_one, key_one, value_one = operands
        scores = low_back(precise_product(query_one, key_one.T) * inv_root)
        scores = jnp.where(allowed, scores, -1e+30)
        row_max = lax.optimization_barrier(jnp.max(scores, axis=-1, keepdims=True))
        weights = jnp.exp(scores - row_max)
        probability = weights / lax.optimization_barrier(jnp.sum(weights, axis=-1, keepdims=True))
        return precise_product(low(probability), value_one)
    head_out = lax.map(jax.checkpoint(one_head), (query_heads, key_head_rows, value_head_rows))
    attended = low(low_back(head_out.transpose(1, 0, 2).reshape(sequence_length, QUERY_HEADS * HEAD_SIZE)))
    middle = hidden_in + low_back(precise_product(attended, out_weight))
    mixed = low(rms_norm(middle, mlp_gain))
    gate_out = low_back(precise_product(mixed, gate_weight))
    up_out = low_back(precise_product(mixed, up_weight))
    inner_act = low(jax.nn.silu(gate_out) * up_out)
    return middle + low_back(precise_product(inner_act, down_weight))

def reference(tokens, segments, attn_gain, query_weight, key_matrix, value_matrix, out_weight, mlp_gain, gate_weight, up_weight, down_weight, cotangent):
    params = tuple((element.astype(jnp.float32) for element in (attn_gain, query_weight, key_matrix, value_matrix, out_weight, mlp_gain, gate_weight, up_weight, down_weight)))
    inputs = tokens.astype(jnp.float32)

    def forward(stacked, *weights_all):

        def advance(carried, element):
            sequence, doc_ids = element

            def run(seq_in, *weights_in):
                return decoder_layer(seq_in, doc_ids, *weights_in)
            return (carried, jax.checkpoint(run)(sequence, *weights_all))
        unused, results = lax.scan(advance, jnp.zeros((), jnp.float32), (stacked, segments))
        return results
    outputs, pullback = jax.vjp(forward, inputs, *params)
    gradients = pullback(cotangent.astype(jnp.float32))
    return (outputs.astype(jnp.bfloat16), gradients[0].astype(jnp.bfloat16), gradients[1], gradients[2], gradients[3], gradients[4], gradients[5], gradients[6], gradients[7], gradients[8], gradients[9])
```

```python
import functools
import math

import jax
import jax.numpy as jnp
import numpy as np
from jax import lax
from jax.experimental import pallas as pl
from jax.experimental.pallas import tpu as pltpu
from jax.sharding import PartitionSpec as P

HEADS = 9
GROUPS = 3
SHARE = HEADS // GROUPS
HEAD = 64
HALF = HEAD // 2
AUG = HEAD + 16
EPS = 1e-05
ROPE_BASE = 100000.0
VMEM = 56 << 20
BF = jnp.bfloat16
F32 = jnp.float32


def params(semantics=None):
    return pltpu.CompilerParams(vmem_limit_bytes=VMEM, dimension_semantics=semantics)


def dot(a, b, dims):
    return lax.dot_general(a, b, (dims, ((), ())), preferred_element_type=F32)


NN = ((1,), (0,))
NT = ((1,), (1,))
TN = ((0,), (0,))


def swap(x, axis, size, mask):
    return lax.ppermute(x, axis, [(i, i ^ mask) for i in range(size)])


def bits_of(size):
    return [1 << k for k in range(size.bit_length() - 1)]


def spread(x, steps, sizes):
    x = x[None]
    for axis, bit in steps:
        x = jnp.concatenate([x, swap(x, axis, sizes[axis], bit)], axis=0)
    return x


def gather_up(x, steps, sizes):
    for axis, bit in reversed(steps):
        half = x.shape[0] // 2
        other = swap(x[half:], axis, sizes[axis], bit)
        x = (x[:half].astype(F32) + other.astype(F32)).astype(x.dtype)
    return x[0]


def slot_table(steps, axis, size, me):
    order = [bit for a, bit in steps if a == axis]
    rel = jnp.arange(size, dtype=jnp.int32) ^ me
    place = jnp.zeros_like(rel)
    for k, bit in enumerate(order):
        place = place | jnp.where((rel & bit) != 0, 1 << k, 0)
    return place


Z_MASKS = (2, 4, 6)


def stack_z(x, sizes):
    return jnp.stack([x] + [swap(x, "dp", sizes["dp"], m) for m in Z_MASKS])


def grow(x, axis, mask, sizes):
    return jnp.concatenate([x, swap(x, axis, sizes[axis], mask)], axis=0)


def fold(keep, send, axis, mask, sizes):
    other = swap(send, axis, sizes[axis], mask)
    half = keep.shape[0] // 2
    add = lambda a, b: (a.astype(F32) + b.astype(F32)).astype(BF)
    return add(keep[:half], other[:half]), add(keep[half:], other[half:])


def fold_z(lo, hi, sizes):
    parts = [lo[0], swap(lo[1], "dp", sizes["dp"], 2), swap(hi[0], "dp", sizes["dp"], 4), swap(hi[1], "dp", sizes["dp"], 6)]
    return sum(p.astype(F32) for p in parts)


def collect_box(x, order, sizes):
    x = stack_z(x, sizes)
    for axis, mask in order:
        x = grow(x, axis, mask, sizes)
    return x, swap(x, "ctx", sizes["ctx"], 1)


def settle_box(keep, send, order, sizes):
    for axis, mask in (("ctx", 1),) + tuple(reversed(order)):
        keep, send = fold(keep, send, axis, mask, sizes)
    return fold_z(keep, send, sizes)


X_THEN_Y = (("dp", 1), ("ctx", 2))
Y_THEN_X = (("ctx", 2), ("dp", 1))


def place_table(order, me_d, me_c):
    d = (jnp.arange(8, dtype=jnp.int32) ^ me_d)[:, None]
    c = (jnp.arange(4, dtype=jnp.int32) ^ me_c)[None, :]
    x, z, y = d & 1, d >> 1, c >> 1
    if order == X_THEN_Y:
        at = y * 8 + x * 4 + z
    else:
        at = x * 8 + y * 4 + z
    return at.reshape(-1), jnp.broadcast_to(c & 1, (8, 4)).reshape(-1)


def fold_down(d):
    r = d.shape[0] // 8
    n = d.shape[0] * 3 // 8
    main, rest = d[:, :128], d[:, 128:]
    rest = jnp.concatenate([rest[i * r : (i + 1) * r] for i in range(8)], axis=1)
    tall = jnp.concatenate([main, rest], axis=0)
    return jnp.concatenate([tall[i * n : (i + 1) * n] for i in range(3)], axis=1)


def unfold_down(p):
    n = p.shape[0]
    r = n // 3
    tall = jnp.concatenate([p[:, i * 128 : (i + 1) * 128] for i in range(3)], axis=0)
    main, rest = tall[: 8 * r], tall[8 * r :]
    rest = jnp.concatenate([rest[:, i * 16 : (i + 1) * 16] for i in range(8)], axis=0)
    return jnp.concatenate([main, rest], axis=1)


def per_device(sizes, tokens, segments, attn_gain, query_weight, key_matrix, value_matrix,
               out_weight, mlp_gain, gate_weight, up_weight, down_weight, cotangent):
    nd, nc = sizes["dp"], sizes["ctx"]
    seqs, rows, width = tokens.shape
    blk = rows // 2
    me_d = lax.axis_index("dp")
    me_c = lax.axis_index("ctx")
    last = nc - 1
    kvd = GROUPS * HEAD
    qd = HEADS * HEAD
    qn, kn, fn = query_weight.shape[1], key_matrix.shape[1], gate_weight.shape[1]
    ff = fn * nc
    shard = width // nd
    box = nd == 8 and nc == 4
    csteps = [("ctx", b) for b in reversed(bits_of(nc))]
    wsteps = [("dp", b) for b in reversed(bits_of(nd))] + csteps

    pad = lambda n: jnp.zeros((shard, n), BF)
    a_own = jnp.concatenate([query_weight, key_matrix, value_matrix, attn_gain[:, None], pad(15)], axis=1)
    b1_own = jnp.concatenate([gate_weight, up_weight], axis=1)
    b2_own = jnp.concatenate([out_weight, mlp_gain[:, None], pad(111)], axis=1)
    if box:
        b2_own = jnp.concatenate([b2_own, fold_down(down_weight)], axis=1)
        a_parts = collect_box(a_own, X_THEN_Y, sizes)
        at1, other1 = place_table(X_THEN_Y, me_d, me_c)
        at2, _ = place_table(Y_THEN_X, me_d, me_c)
        places = jnp.concatenate([at1, at2, other1, me_c[None] & 1, me_c[None]])
        w_all = pl.pallas_call(
            unpack_a_kernel,
            in_specs=[pl.BlockSpec(memory_space=pltpu.SMEM)] + [pl.BlockSpec(memory_space=pltpu.VMEM)] * 2,
            out_specs=pl.BlockSpec(memory_space=pltpu.VMEM),
            out_shape=jax.ShapeDtypeStruct((nd, shard, 1024), BF),
            compiler_params=params(),
            name="unpack_a",
        )(places, *a_parts).reshape(width, 1024)
        b = jnp.concatenate([b1_own, b2_own], axis=1)
        b = stack_z(b, sizes)
        b1, b2 = b[..., : 2 * fn], b[..., 2 * fn :]
        b1, b2 = grow(b1, "dp", 1, sizes), grow(b2, "ctx", 2, sizes)
        b1, b2 = grow(b1, "ctx", 2, sizes), grow(b2, "dp", 1, sizes)
        b1x, b2x = swap(b1, "ctx", nc, 1), swap(b2, "ctx", nc, 1)
        piece = lambda n: pl.BlockSpec((2, 1, shard, n), lambda d, t: (0, t[d * 4] % 8, 0, 0))
        b1, b1x = (v.reshape(2, 8, shard, 2 * fn) for v in (b1, b1x))
        b2, b2x = (v.reshape(2, 2, 4, shard, 640).transpose(1, 0, 2, 3, 4).reshape(2, 8, shard, 640) for v in (b2, b2x))
        wide = lambda r, n: pl.BlockSpec((1, r, n), lambda d, t: (d, 0, 0))
        wg, wu, wo, wd = pl.pallas_call(
            unpack_b_kernel,
            grid_spec=pltpu.PrefetchScalarGridSpec(
                num_scalar_prefetch=1,
                grid=(nd,),
                in_specs=[piece(2 * fn), piece(2 * fn), piece(640), piece(640)],
                out_specs=[wide(shard, ff), wide(shard, ff), wide(shard, 640), wide(ff // nd, width)],
            ),
            out_shape=[jax.ShapeDtypeStruct((nd, shard, ff), BF), jax.ShapeDtypeStruct((nd, shard, ff), BF),
                       jax.ShapeDtypeStruct((nd, shard, 640), BF), jax.ShapeDtypeStruct((nd, ff // nd, width), BF)],
            compiler_params=params(),
            name="unpack_b",
        )(places, b1, b1x, b2, b2x)
        wg, wu, wo, wd = wg.reshape(width, ff), wu.reshape(width, ff), wo.reshape(width, 640), wd.reshape(ff, width)
    else:
        dslot = slot_table(wsteps, "dp", nd, me_d)
        cslot = slot_table(wsteps, "ctx", nc, me_c)

        def whole(own):
            x = spread(own, wsteps, sizes)
            x = x.reshape((nc, nd) + own.shape)
            return jnp.take(jnp.take(x, cslot, axis=0), dslot, axis=1)

        def join(x):
            return x.transpose(1, 2, 0, 3).reshape(nd * x.shape[2], nc * x.shape[3])

        a = whole(a_own)
        w_all = jnp.concatenate(
            [join(a[..., :qn]), join(a[..., qn : qn + kn]), join(a[..., qn + kn : qn + 2 * kn]),
             a[0, :, :, 240:241].reshape(width, 1), jnp.zeros((width, 63), BF)], axis=1)
        b1 = whole(b1_own)
        b2 = whole(b2_own)
        wg, wu = join(b1[..., :fn]), join(b1[..., fn:])
        wo = jnp.concatenate([join(b2[..., :qn]), b2[0, :, :, qn : qn + 1].reshape(width, 1), jnp.zeros((width, 63), BF)], axis=1)
        wd = join(whole(down_weight))
        places = jnp.zeros((98,), jnp.int32)

    ctx_bits = [b for _, b in csteps]

    def piece_rel(i):
        return sum(b for k, b in enumerate(ctx_bits) if i >> k & 1)

    place = {piece_rel(i): i for i in range(nc)}

    def balanced(all_pieces):
        rel = [all_pieces[place[r]] for r in range(nc)]
        return jnp.stack([jnp.concatenate([rel[r][:blk], rel[r ^ last][blk:]], axis=0) for r in range(nc)])

    seg_all = spread(segments, csteps, sizes)
    owner = me_c ^ jnp.arange(nc, dtype=jnp.int32)
    lane = jnp.arange(blk, dtype=jnp.int32)
    index = jnp.concatenate(
        [owner[:, None] * rows + lane[None], (last - owner[:, None]) * rows + blk + lane[None]], axis=1)
    inverse = ROPE_BASE ** (-2.0 * jnp.arange(HALF).astype(F32) / HEAD)
    table = jnp.asarray(pair_table(nc))[me_c].reshape(-1)
    pairs = 2 * nc + 1
    wide_q = SHARE * blk

    cot_swapped = swap(cotangent[:, blk:], "ctx", nc, last)
    cot = jnp.concatenate([cotangent[:, :blk], cot_swapped], axis=1)

    saved = []
    for s in range(seqs):
        zig = balanced(spread(tokens[s], csteps, sizes))
        zseg = balanced(seg_all[:, s])
        before = jnp.where(zseg == 0, 0, jnp.where(zseg == 1, jnp.sum(zseg < 1), jnp.sum(zseg < 2)))
        phase = (index - before).astype(F32)[:, None, :] * inverse[None, :, None]
        cos_t, sin_t = jnp.cos(phase), jnp.sin(phase)

        piece = lambda *tail: pl.BlockSpec((1,) + tail, lambda r: (r,) + (0,) * len(tail))
        fixed = lambda *shape: pl.BlockSpec(shape, lambda r: (0,) * len(shape))
        h1, k_t, v_t, q_t, w_t = pl.pallas_call(
            pre_kernel,
            grid=(nc,),
            in_specs=[piece(rows, width), fixed(width, 1024), piece(HALF, rows), piece(HALF, rows), piece(1, rows)],
            out_specs=[piece(rows, width),
                       pl.BlockSpec((GROUPS, 1, AUG, rows), lambda r: (0, r, 0, 0)),
                       pl.BlockSpec((GROUPS, 1, AUG, rows), lambda r: (0, r, 0, 0)),
                       fixed(GROUPS, 2, AUG, wide_q), fixed(1024, width)],
            out_shape=[jax.ShapeDtypeStruct((nc, rows, width), BF),
                       jax.ShapeDtypeStruct((GROUPS, nc, AUG, rows), BF),
                       jax.ShapeDtypeStruct((GROUPS, nc, AUG, rows), BF),
                       jax.ShapeDtypeStruct((GROUPS, 2, AUG, wide_q), BF),
                       jax.ShapeDtypeStruct((1024, width), BF)],
            compiler_params=params(),
            cost_estimate=pl.CostEstimate(flops=4_500_000_000, bytes_accessed=10_000_000, transcendentals=0),
            name="pre",
        )(zig, w_all, cos_t, sin_t, zseg[:, None, :])

        att = lambda *tail: pl.BlockSpec((1,) + tail, lambda g, t: (g,) + (0,) * len(tail))
        prob, o_t, inv_l = pl.pallas_call(
            functools.partial(attend_kernel, pairs),
            grid_spec=pltpu.PrefetchScalarGridSpec(
                num_scalar_prefetch=1,
                grid=(GROUPS,),
                in_specs=[att(2, AUG, wide_q), att(nc, AUG, rows), att(nc, AUG, rows)],
                out_specs=[att(pairs, blk, wide_q), att(2, HEAD, wide_q), att(2, 1, wide_q)],
                scratch_shapes=[pltpu.VMEM((pairs, blk, wide_q), F32), pltpu.VMEM((2, 8, wide_q), F32),
                                pltpu.VMEM((2, AUG, wide_q), F32)],
            ),
            out_shape=[jax.ShapeDtypeStruct((GROUPS, pairs, blk, wide_q), BF),
                       jax.ShapeDtypeStruct((GROUPS, 2, HEAD, wide_q), BF),
                       jax.ShapeDtypeStruct((GROUPS, 2, 1, wide_q), F32)],
            compiler_params=params(),
            cost_estimate=pl.CostEstimate(flops=12_000_000_000, bytes_accessed=12_000_000, transcendentals=0),
            name="attend",
        )(table, q_t, k_t, v_t)
        saved.append((zig, cos_t, sin_t, h1, k_t, v_t, q_t, w_t, prob, o_t, inv_l))

    x_own = jnp.stack([v[0][0] for v in saved]).reshape(seqs * rows, width)
    total = seqs * rows
    o_pair = jnp.stack([v[9] for v in saved])
    steps = nc
    fstep = ff // steps
    fixed = lambda *shape: pl.BlockSpec(shape, lambda f, t: (0,) * len(shape))
    if box:
        grad_specs = [fixed(16, shard, 2 * fn)] * 2 + [fixed(16, shard, 640)] * 2
        grad_shapes = [jax.ShapeDtypeStruct((16, shard, 2 * fn), BF)] * 2 + [jax.ShapeDtypeStruct((16, shard, 640), BF)] * 2
    else:
        grad_specs = [pl.BlockSpec((width, fstep), lambda f, t: (0, f))] * 2
        grad_specs += [pl.BlockSpec((fstep, width), lambda f, t: (f, 0)), fixed(width, 640)]
        grad_shapes = [jax.ShapeDtypeStruct((width, ff), BF)] * 2
        grad_shapes += [jax.ShapeDtypeStruct((ff, width), BF), jax.ShapeDtypeStruct((width, 640), BF)]
    output, d_middle, do_t, *grads = pl.pallas_call(
        functools.partial(middle_kernel, box, nd, nc),
        grid_spec=pltpu.PrefetchScalarGridSpec(
            num_scalar_prefetch=1,
            grid=(steps,),
            in_specs=[fixed(total, width), fixed(total, width), fixed(seqs, GROUPS, 2, HEAD, wide_q),
                      pl.BlockSpec((width, fstep), lambda f, t: (0, f)), pl.BlockSpec((width, fstep), lambda f, t: (0, f)),
                      pl.BlockSpec((fstep, width), lambda f, t: (f, 0)), fixed(width, 640)],
            out_specs=[fixed(total, width), fixed(total, width), fixed(seqs, GROUPS, 2, HEAD, wide_q)] + grad_specs,
            scratch_shapes=[pltpu.VMEM((qd, total), BF), pltpu.VMEM((total, width), F32), pltpu.VMEM((total, width), BF),
                            pltpu.VMEM((total, width), F32), pltpu.VMEM((total, width), F32)],
        ),
        out_shape=[jax.ShapeDtypeStruct((total, width), BF), jax.ShapeDtypeStruct((total, width), F32),
                   jax.ShapeDtypeStruct((seqs, GROUPS, 2, HEAD, wide_q), BF)] + grad_shapes,
        compiler_params=params(),
        cost_estimate=pl.CostEstimate(flops=36_000_000_000, bytes_accessed=20_000_000, transcendentals=0),
        name="middle",
    )(places, x_own, cot.reshape(total, width), o_pair, wg, wu, wd, wo)

    def settle(pieces):
        x = jnp.take(jnp.take(pieces, jnp.argsort(dslot), axis=0), jnp.argsort(cslot), axis=1)
        x = jnp.swapaxes(x, 0, 1).reshape((nc * nd,) + pieces.shape[2:])
        return gather_up(x, wsteps, sizes).astype(F32)

    def cut(g):
        r, c = g.shape
        return g.reshape(nd, r // nd, nc, c // nc).transpose(0, 2, 1, 3)

    def repeat(column):
        return jnp.broadcast_to(column.reshape(nd, 1, shard, 1), (nd, nc, shard, 1))

    if box:
        b1_sum = settle_box(grads[0], grads[1], X_THEN_Y, sizes)
        b2_sum = settle_box(grads[2], grads[3], Y_THEN_X, sizes)
        gate_sum, up_sum = b1_sum[:, :fn], b1_sum[:, fn:]
        out_sum, gain2_sum, down_sum = b2_sum[:, :qn], b2_sum[:, qn], unfold_down(b2_sum[:, 256:])
    else:
        gate_sum, up_sum, down_sum = settle(cut(grads[0])), settle(cut(grads[1])), settle(cut(grads[2]))
        b2_sum = settle(jnp.concatenate([cut(grads[3][:, :qd]), repeat(grads[3][:, qd])], axis=-1))
        out_sum, gain2_sum = b2_sum[:, :qn], b2_sum[:, qn]

    token_grads = []
    a_grads = None
    for s in range(seqs):
        zig, cos_t, sin_t, h1, k_t, v_t, q_t, w_t, prob, o_t, inv_l = saved[s]
        att = lambda *tail: pl.BlockSpec((1,) + tail, lambda g, t: (g,) + (0,) * len(tail))
        pair_of = pl.BlockSpec((1, 1, 2, HEAD, wide_q), lambda g, t: (s, g, 0, 0, 0))
        kv_out = pl.BlockSpec((nc, 1, HEAD, rows), lambda g, t: (0, g, 0, 0))
        dq_t, dk_t, dv_t = pl.pallas_call(
            functools.partial(attend_back_kernel, pairs),
            grid_spec=pltpu.PrefetchScalarGridSpec(
                num_scalar_prefetch=1,
                grid=(GROUPS,),
                in_specs=[att(pairs, blk, wide_q), att(2, AUG, wide_q), att(nc, AUG, rows),
                          att(nc, AUG, rows), att(2, HEAD, wide_q), pair_of, att(2, 1, wide_q)],
                out_specs=[att(2, HEAD, wide_q), kv_out, kv_out],
                scratch_shapes=[pltpu.VMEM((2, AUG, wide_q), BF), pltpu.VMEM((2 * nc, HEAD, blk), F32),
                                pltpu.VMEM((2 * nc, HEAD, blk), F32), pltpu.VMEM((2, HEAD, wide_q), F32)],
            ),
            out_shape=[jax.ShapeDtypeStruct((GROUPS, 2, HEAD, wide_q), F32),
                       jax.ShapeDtypeStruct((nc, GROUPS, HEAD, rows), F32),
                       jax.ShapeDtypeStruct((nc, GROUPS, HEAD, rows), F32)],
            compiler_params=params(),
            cost_estimate=pl.CostEstimate(flops=20_000_000_000, bytes_accessed=12_000_000, transcendentals=0),
            name="attend_back",
        )(table, prob, q_t, k_t, v_t, o_t, do_t, inv_l)

        piece = lambda *tail: pl.BlockSpec((1,) + tail, lambda r, t: (r,) + (0,) * len(tail))
        fixed = lambda *shape: pl.BlockSpec(shape, lambda r, t: (0,) * len(shape))
        final = s == seqs - 1
        if box and final:
            a_specs = [fixed(16, shard, 256)] * 2
            a_shapes = [jax.ShapeDtypeStruct((16, shard, 256), BF)] * 2
        elif final:
            a_specs, a_shapes = [fixed(width, 1024)], [jax.ShapeDtypeStruct((width, 1024), BF)]
        else:
            a_specs, a_shapes = [fixed(1024, width)], [jax.ShapeDtypeStruct((1024, width), F32)]
        before_args = [] if a_grads is None else [a_grads]
        dkv_t, dqr_t, *a_out = pl.pallas_call(
            functools.partial(post_kernel, box, nd, nc, len(before_args), final),
            grid_spec=pltpu.PrefetchScalarGridSpec(
                num_scalar_prefetch=1,
                grid=(nc,),
                in_specs=[piece(GROUPS, HEAD, rows), piece(GROUPS, HEAD, rows), fixed(GROUPS, 2, HEAD, wide_q),
                          piece(HALF, rows), piece(HALF, rows), piece(rows, width), fixed(width, 1024)]
                + [fixed(1024, width)] * len(before_args),
                out_specs=[piece(2 * kvd, rows), fixed(qd, rows)] + a_specs,
                scratch_shapes=[pltpu.VMEM((1024, width), F32)],
            ),
            out_shape=[jax.ShapeDtypeStruct((nc, 2 * kvd, rows), BF), jax.ShapeDtypeStruct((qd, rows), BF)] + a_shapes,
            compiler_params=params(),
            cost_estimate=pl.CostEstimate(flops=4_500_000_000, bytes_accessed=10_000_000, transcendentals=0),
            name="post",
        )(places, dk_t, dv_t, dq_t, cos_t, sin_t, h1, w_all, *before_args)
        a_grads = a_out[0]

        dkv_places = jnp.stack([dkv_t[piece_rel(i)] for i in range(nc)])
        dkv_own = gather_up(dkv_places, csteps, sizes)
        token_grads.append(pl.pallas_call(
            token_kernel,
            out_shape=jax.ShapeDtypeStruct((rows, width), BF),
            compiler_params=params(),
            cost_estimate=pl.CostEstimate(flops=2_000_000_000, bytes_accessed=5_000_000, transcendentals=0),
            name="token",
        )(dqr_t, dkv_own, w_t, x_own[s * rows : (s + 1) * rows], d_middle[s * rows : (s + 1) * rows]))

    if box:
        a_sum = settle_box(a_out[0], a_out[1], X_THEN_Y, sizes)
    else:
        a = a_out[0]
        a_sum = settle(jnp.concatenate(
            [cut(a[:, :qd]), cut(a[:, qd : qd + kvd]), cut(a[:, qd + kvd : qd + 2 * kvd]), repeat(a[:, 960])], axis=-1))

    def home(y):
        y = y.reshape(seqs, rows, width)
        return jnp.concatenate([y[:, :blk], swap(y[:, blk:], "ctx", nc, last)], axis=1)

    return (
        home(output),
        home(jnp.stack(token_grads)),
        a_sum[:, 2 * kn + qn],
        a_sum[:, :qn],
        a_sum[:, qn : qn + kn],
        a_sum[:, qn + kn : qn + 2 * kn],
        out_sum,
        gain2_sum,
        gate_sum,
        up_sum,
        down_sum,
    )


def pair_table(nc):
    out = []
    for me in range(nc):
        spots = {}
        for r in range(nc):
            d = me ^ r
            spots[2 * d] = 2 * r
            spots[2 * (nc - 1 - d) + 1] = 2 * r + 1
        mine = [2 * me, 2 * (nc - 1 - me) + 1]
        rows = [(i, spots[mine[i]]) for i in range(2)]
        rows += [(i, spots[k]) for i in range(2) for k in range(mine[i])]
        out.append(rows)
    return np.array(out, np.int32)


def turn(x, cos, sin, heads, sign):
    parts = []
    for h in range(heads):
        lo, hi = x[h * HEAD : h * HEAD + HALF], x[h * HEAD + HALF : (h + 1) * HEAD]
        parts += [lo * cos - sign * hi * sin, hi * cos + sign * lo * sin]
    return jnp.concatenate(parts, axis=0)


def unpack_a_kernel(places, own_ref, other_ref, w_ref):
    nd = w_ref.shape[0]
    nc = 4
    qn, kn = 144, 48
    qd, kvd = qn * nc, kn * nc

    def write(cores):
        for d in range(nd):
            for c in range(nc):
                p = cores[c % 2][places[d * nc + c]].astype(F32)
                if c == 0:
                    cols = [[], [], []]
                    gain = p[:, 240:256]
                cols[0].append(p[:, :qn])
                cols[1].append(p[:, qn : qn + kn])
                cols[2].append(p[:, qn + kn : qn + 2 * kn])
            row = cols[0] + cols[1] + cols[2] + [gain, jnp.zeros((p.shape[0], 48), F32)]
            w_ref[d] = jnp.concatenate(row, axis=1).astype(BF)

    core = places[96]
    pl.when(core == 0)(lambda: write((own_ref, other_ref)))
    pl.when(core == 1)(lambda: write((other_ref, own_ref)))


def unpack_b_kernel(places, b1_ref, b1x_ref, b2_ref, b2x_ref, g_ref, u_ref, o_ref, w_ref):
    nc = 4
    fn = b1_ref.shape[-1] // 2
    me_y = places[97] // 2

    def write(one, two):
        outs, downs = [], []
        for c in range(nc):
            y = jnp.bitwise_xor(me_y, c // 2)
            p = one[c % 2][y, 0]
            g_ref[0, :, c * fn : (c + 1) * fn] = p[:, :fn]
            u_ref[0, :, c * fn : (c + 1) * fn] = p[:, fn:]
            p = two[c % 2][y, 0].astype(F32)
            outs.append(p[:, :144])
            downs.append(unfold_down(p[:, 256:]))
            if c == 0:
                gain = p[:, 144:160]
        o_ref[0] = jnp.concatenate(outs + [gain, jnp.zeros((gain.shape[0], 48), F32)], axis=1).astype(BF)
        w_ref[0] = jnp.concatenate(downs, axis=1).astype(BF)

    core = places[96]
    pl.when(core == 0)(lambda: write((b1_ref, b1x_ref), (b2_ref, b2x_ref)))
    pl.when(core == 1)(lambda: write((b1x_ref, b1_ref), (b2x_ref, b2_ref)))


def pre_kernel(x_ref, w_ref, cos_ref, sin_ref, seg_ref, h_ref, k_ref, v_ref, q_ref, wt_ref):
    @pl.when(pl.program_id(0) == 0)
    def _():
        wt_ref[...] = w_ref[...].T

    x = x_ref[0].astype(F32)
    inv = lax.rsqrt(jnp.mean(x * x, axis=-1, keepdims=True) + EPS)
    qd, kvd = HEADS * HEAD, GROUPS * HEAD
    gain = wt_ref[qd + 2 * kvd : qd + 2 * kvd + 16].astype(F32)[0:1]
    h = ((x * inv) * gain).astype(BF)
    h_ref[0] = h
    cos, sin, seg = cos_ref[0], sin_ref[0], seg_ref[0]
    rows = x.shape[0]
    blk = rows // 2
    kv = dot(wt_ref[qd : qd + 2 * kvd], h, NT)
    keys = turn(kv[:kvd], cos, sin, GROUPS, 1.0).astype(BF)
    values = kv[kvd:].astype(BF)
    row = lax.broadcasted_iota(jnp.int32, (AUG - HEAD, rows), 0)
    other = jnp.where((row < 3) & (row != seg), -1e30, 0.0).astype(BF)
    ones = (row < 3).astype(BF)
    for g in range(GROUPS):
        k_ref[g, 0, :HEAD] = keys[g * HEAD : (g + 1) * HEAD]
        k_ref[g, 0, HEAD:] = other
        v_ref[g, 0, :HEAD] = values[g * HEAD : (g + 1) * HEAD]
        v_ref[g, 0, HEAD:] = ones

    @pl.when(pl.program_id(0) == 0)
    def _():
        q = turn(dot(wt_ref[:qd], h, NT), cos, sin, HEADS, 1.0).astype(BF) * (1.0 / math.sqrt(HEAD))
        same = (row == seg).astype(BF)
        for g in range(GROUPS):
            for b in range(2):
                for j in range(SHARE):
                    n = g * SHARE + j
                    q_ref[g, b, :HEAD, j * blk : (j + 1) * blk] = q[n * HEAD : (n + 1) * HEAD, b * blk : (b + 1) * blk]
                    q_ref[g, b, HEAD:, j * blk : (j + 1) * blk] = same[:, b * blk : (b + 1) * blk]


def middle_kernel(box, nd, nc, places, x_ref, cot_ref, ot_ref, wg_ref, wu_ref, wd_ref, wo_ref,
                  out_ref, dm_ref, do_ref, *rest):
    grads, (att_ref, mid_ref, h_ref, acc_ref, dh_ref) = rest[:4], rest[4:]
    f = pl.program_id(0)
    seqs, _, _, _, wide = ot_ref.shape
    blk = wide // SHARE
    rows = 2 * blk
    qd, width = HEADS * HEAD, x_ref.shape[1]
    shard = width // nd
    fn = wg_ref.shape[1]

    def norm():
        m = mid_ref[...]
        inv = lax.rsqrt(jnp.mean(m * m, axis=-1, keepdims=True) + EPS)
        return m, inv, m * inv

    def gain_row():
        return wo_ref[:, 512:640].astype(F32).T[qd - 512 : qd - 512 + 1]

    def blocks():
        for s in range(seqs):
            for g in range(GROUPS):
                for b in range(2):
                    for j in range(SHARE):
                        n = g * SHARE + j
                        yield (s, g, b, slice(None), slice(j * blk, (j + 1) * blk)), (
                            slice(n * HEAD, (n + 1) * HEAD), slice(s * rows + b * blk, s * rows + (b + 1) * blk))

    @pl.when(f == 0)
    def _():
        for there, here in blocks():
            att_ref[here] = ot_ref[there]
        mid_ref[...] = x_ref[...].astype(F32) + dot(att_ref[...], wo_ref[:, :qd], TN)
        _, _, n2 = norm()
        h_ref[...] = (n2 * gain_row()).astype(BF)

    h = h_ref[...]
    cot = cot_ref[...]
    gate = dot(h, wg_ref[...], NN)
    up = dot(h, wu_ref[...], NN)
    sig = jax.nn.sigmoid(gate)
    act = gate * sig
    inner = (act * up).astype(BF)
    part = dot(inner, wd_ref[...], NN)
    d_inner = dot(cot, wd_ref[...], NT)
    d_gate = (d_inner * up * (sig + act * (1.0 - sig))).astype(BF)
    d_up = (d_inner * act).astype(BF)
    d_part = dot(d_gate, wg_ref[...], NT) + dot(d_up, wu_ref[...], NT)

    @pl.when(f == 0)
    def _():
        acc_ref[...] = part
        dh_ref[...] = d_part

    @pl.when(f > 0)
    def _():
        acc_ref[...] += part
        dh_ref[...] += d_part

    grad_gate = dot(h, d_gate, TN)
    grad_up = dot(h, d_up, TN)
    grad_down = dot(inner, cot, TN)
    if box:
        b1, b1x, b2, b2x = grads

        def put(near, far, c, at, lanes, value):
            @pl.when(places[64 + c] == 0)
            def _():
                near[at, :, lanes] = value

            @pl.when(places[64 + c] == 1)
            def _():
                far[at, :, lanes] = value

        for d in range(nd):
            part_rows = slice(d * shard, (d + 1) * shard)
            at = places[d * nc + f]
            put(b1, b1x, f, at, slice(0, fn), grad_gate[part_rows].astype(BF))
            put(b1, b1x, f, at, slice(fn, 2 * fn), grad_up[part_rows].astype(BF))
        per = fn * nc // nd
        for i in range(fn // per):
            for c in range(nc):
                p = fold_down(grad_down[i * per : (i + 1) * per, c * 144 : (c + 1) * 144]).astype(BF)
                put(b2, b2x, c, places[32 + (f * (fn // per) + i) * nc + c], slice(256, 640), p)
    else:
        grads[0][...] = grad_gate.astype(BF)
        grads[1][...] = grad_up.astype(BF)
        grads[2][...] = grad_down.astype(BF)

    @pl.when(f == pl.num_programs(0) - 1)
    def _():
        m, inv, n2 = norm()
        out_ref[...] = (m + acc_ref[...]).astype(BF)
        d_h2 = dh_ref[...]
        e2 = d_h2 * gain_row()
        d_middle = cot_ref[...].astype(F32) + inv * (e2 - n2 * jnp.mean(e2 * n2, axis=-1, keepdims=True))
        dm_ref[...] = d_middle
        branch = d_middle.astype(BF)
        d_att = dot(wo_ref[:, :qd], branch, NT).astype(BF)
        for there, here in blocks():
            do_ref[there] = d_att[here]
        grad_out = dot(att_ref[...], branch, NN)
        gain = jnp.broadcast_to(jnp.sum(d_h2 * n2, axis=0, keepdims=True), (128, width)).T
        if box:
            for d in range(nd):
                part_rows = slice(d * shard, (d + 1) * shard)
                for c in range(nc):
                    p = jnp.concatenate([grad_out[part_rows, c * 144 : (c + 1) * 144], gain[part_rows, :112]], axis=1)
                    put(b2, b2x, c, places[32 + d * nc + c], slice(0, 256), p.astype(BF))
        else:
            grads[3][...] = jnp.concatenate([grad_out, gain[:, :64]], axis=1).astype(BF)


def post_kernel(box, nd, nc, carried, final, places, dk_ref, dv_ref, dq_ref, cos_ref, sin_ref, h_ref, w_ref, *rest):
    before = rest[:carried]
    dkv_ref, dqr_ref, *outs, acc_ref = rest[carried:]
    cos, sin = cos_ref[0], sin_ref[0]
    h = h_ref[0]
    rows = h.shape[0]
    blk = rows // 2
    kvd, qd = GROUPS * HEAD, HEADS * HEAD
    dk = turn(dk_ref[0].reshape(kvd, rows), cos, sin, GROUPS, -1.0).astype(BF)
    dv = dv_ref[0].reshape(kvd, rows).astype(BF)
    dkv_ref[0, :kvd] = dk
    dkv_ref[0, kvd:] = dv

    @pl.when(pl.program_id(0) == 0)
    def _():
        if carried:
            acc_ref[...] = before[0][...]
        else:
            acc_ref[...] = jnp.zeros_like(acc_ref)
        heads = []
        for g in range(GROUPS):
            for j in range(SHARE):
                heads.append(jnp.concatenate([dq_ref[g, b, :, j * blk : (j + 1) * blk] for b in range(2)], axis=1))
        dq = turn(jnp.concatenate(heads, axis=0), cos, sin, HEADS, -1.0).astype(BF)
        dqr_ref[...] = dq
        acc_ref[:qd] += dot(dq, h, NN)

    acc_ref[qd : qd + kvd] += dot(dk, h, NN)
    acc_ref[qd + kvd : qd + 2 * kvd] += dot(dv, h, NN)

    @pl.when(pl.program_id(0) == pl.num_programs(0) - 1)
    def _():
        if not final:
            outs[0][...] = acc_ref[...]
            return
        g = acc_ref[...].T
        w = w_ref[...].astype(F32)
        used = qd + 2 * kvd
        gain = jnp.sum(g[:, :used] * w[:, :used], axis=1, keepdims=True) / w[:, used : used + 1]
        if not box:
            outs[0][...] = jnp.concatenate([g[:, :used], jnp.broadcast_to(gain, (g.shape[0], 64))], axis=1).astype(BF)
            return
        shard = g.shape[0] // nd
        gain = jnp.broadcast_to(gain, (g.shape[0], 16))
        qn, kn = qd // nc, kvd // nc
        for d in range(nd):
            r = slice(d * shard, (d + 1) * shard)
            for c in range(nc):
                p = jnp.concatenate(
                    [g[r, c * qn : (c + 1) * qn], g[r, qd + c * kn : qd + (c + 1) * kn],
                     g[r, qd + kvd + c * kn : qd + kvd + (c + 1) * kn], gain[r]], axis=1).astype(BF)
                at = places[d * nc + c]

                @pl.when(places[64 + c] == 0)
                def _():
                    outs[0][at] = p

                @pl.when(places[64 + c] == 1)
                def _():
                    outs[1][at] = p


def token_kernel(dq_ref, dkv_ref, wt_ref, x_ref, dm_ref, out_ref):
    qd, kvd = HEADS * HEAD, GROUPS * HEAD
    x = x_ref[...].astype(F32)
    inv = lax.rsqrt(jnp.mean(x * x, axis=-1, keepdims=True) + EPS)
    n1 = x * inv
    d_h1 = dot(dq_ref[...], wt_ref[:qd], TN) + dot(dkv_ref[...], wt_ref[qd : qd + 2 * kvd], TN)
    e1 = d_h1 * wt_ref[qd + 2 * kvd : qd + 2 * kvd + 16].astype(F32)[0:1]
    out_ref[...] = (dm_ref[...] + inv * (e1 - n1 * jnp.mean(e1 * n1, axis=-1, keepdims=True))).astype(BF)


def key_block(ref, loc, blk, rows=None):
    r, half = loc // 2, loc % 2
    lanes = pl.ds(pl.multiple_of(half * blk, blk), blk)
    if rows is None:
        return ref[0, r, :, lanes]
    return ref[0, r, :rows, lanes]


def attend_kernel(pairs, table, q_ref, k_ref, v_ref, p_ref, o_ref, l_ref, s_ref, m_ref, acc_ref):
    wide = q_ref.shape[-1]
    blk = wide // SHARE

    def score(t, diagonal):
        qb, loc = table[2 * t], table[2 * t + 1]
        s = dot(key_block(k_ref, loc, blk), q_ref[0, qb], TN)
        if diagonal:
            k_at = lax.broadcasted_iota(jnp.int32, (blk, wide), 0)
            q_at = lax.broadcasted_iota(jnp.int32, (blk, wide), 1) % blk
            s = jnp.where(k_at <= q_at, s, -1e30)
        s_ref[t] = s
        top = jnp.max(s.reshape(blk // 8, 8, wide), axis=0)
        if diagonal:
            m_ref[qb] = top
        else:
            m_ref[qb] = jnp.maximum(m_ref[qb], top)

    for t in range(2):
        score(t, True)
    lax.fori_loop(2, pairs, lambda t, c: (score(t, False), c)[1], 0)
    for b in range(2):
        m_ref[b] = jnp.broadcast_to(jnp.max(m_ref[b], axis=0, keepdims=True), m_ref.shape[1:])
    acc_ref[...] = jnp.zeros_like(acc_ref)

    def weigh(t, c):
        qb, loc = table[2 * t], table[2 * t + 1]
        p = jnp.exp(s_ref[t] - m_ref[qb, 0:1]).astype(BF)
        p_ref[0, t] = p
        acc_ref[qb] += dot(key_block(v_ref, loc, blk), p, NN)
        return c

    lax.fori_loop(0, pairs, weigh, 0)
    for b in range(2):
        inv = 1.0 / acc_ref[b, HEAD : HEAD + 1]
        l_ref[0, b] = inv
        o_ref[0, b] = (acc_ref[b, :HEAD] * inv).astype(BF)


def attend_back_kernel(pairs, table, p_ref, q_ref, k_ref, v_ref, o_ref, do_ref, l_ref, dq_ref, dk_ref, dv_ref,
                       da_ref, dka_ref, dva_ref, dqa_ref):
    wide = q_ref.shape[-1]
    blk = wide // SHARE
    row = lax.broadcasted_iota(jnp.int32, (AUG - HEAD, wide), 0)
    for b in range(2):
        d = (do_ref[0, 0, b].astype(F32) * l_ref[0, b]).astype(BF)
        delta = -jnp.sum(d.astype(F32) * o_ref[0, b].astype(F32), axis=0, keepdims=True)
        hi = delta.astype(BF).astype(F32)
        mid = (delta - hi).astype(BF).astype(F32)
        low = delta - hi - mid
        da_ref[b, :HEAD] = d
        da_ref[b, HEAD:] = jnp.where(row == 0, hi, jnp.where(row == 1, mid, jnp.where(row == 2, low, 0.0))).astype(BF)
    dka_ref[...] = jnp.zeros_like(dka_ref)
    dva_ref[...] = jnp.zeros_like(dva_ref)
    dqa_ref[...] = jnp.zeros_like(dqa_ref)

    def step(t, c):
        qb, loc = table[2 * t], table[2 * t + 1]
        p = p_ref[0, t]
        dp = dot(key_block(v_ref, loc, blk), da_ref[qb], TN)
        ds = (p.astype(F32) * dp).astype(BF)
        dqa_ref[qb] += dot(key_block(k_ref, loc, blk, HEAD), ds, NN)
        dka_ref[loc] += dot(q_ref[0, qb, :HEAD], ds, NT)
        dva_ref[loc] += dot(da_ref[qb, :HEAD], p, NT)
        return c

    lax.fori_loop(0, pairs, step, 0)
    dq_ref[0] = dqa_ref[...] * (1.0 / math.sqrt(HEAD))
    for r in range(dk_ref.shape[0]):
        for half in range(2):
            dk_ref[r, 0, :, half * blk : (half + 1) * blk] = dka_ref[2 * r + half]
            dv_ref[r, 0, :, half * blk : (half + 1) * blk] = dva_ref[2 * r + half]


def solution(mesh):
    sizes = {name: mesh.shape[name] for name in ("dp", "ctx")}
    rows = P("dp", "ctx", None)
    grid = P("dp", "ctx")
    line = P("dp")
    return jax.shard_map(
        functools.partial(per_device, sizes),
        mesh=mesh,
        in_specs=(rows, grid, line, grid, grid, grid, grid, line, grid, grid, grid, rows),
        out_specs=(rows, rows, line, grid, grid, grid, grid, line, grid, grid, grid),
        check_vma=False,
    )
```

```python
import functools
import math

import jax
import jax.numpy as jnp
import numpy as np
from jax import lax
from jax.experimental import pallas as pl
from jax.experimental.pallas import tpu as pltpu
from jax.sharding import PartitionSpec as P

HEADS = 9
GROUPS = 3
SHARE = HEADS // GROUPS
HEAD = 64
HALF = HEAD // 2
AUG = HEAD + 16
EPS = 1e-05
ROPE_BASE = 100000.0
VMEM = 56 << 20
BF = jnp.bfloat16
F32 = jnp.float32


def params(semantics=None):
    return pltpu.CompilerParams(vmem_limit_bytes=VMEM, dimension_semantics=semantics)


def dot(a, b, dims):
    return lax.dot_general(a, b, (dims, ((), ())), preferred_element_type=F32)


NN = ((1,), (0,))
NT = ((1,), (1,))
TN = ((0,), (0,))


def swap(x, axis, size, mask):
    return lax.ppermute(x, axis, [(i, i ^ mask) for i in range(size)])


def bits_of(size):
    return [1 << k for k in range(size.bit_length() - 1)]


def spread(x, steps, sizes):
    x = x[None]
    for axis, bit in steps:
        x = jnp.concatenate([x, swap(x, axis, sizes[axis], bit)], axis=0)
    return x


def gather_up(x, steps, sizes):
    for axis, bit in reversed(steps):
        half = x.shape[0] // 2
        other = swap(x[half:], axis, sizes[axis], bit)
        x = (x[:half].astype(F32) + other.astype(F32)).astype(x.dtype)
    return x[0]


def slot_table(steps, axis, size, me):
    order = [bit for a, bit in steps if a == axis]
    rel = jnp.arange(size, dtype=jnp.int32) ^ me
    place = jnp.zeros_like(rel)
    for k, bit in enumerate(order):
        place = place | jnp.where((rel & bit) != 0, 1 << k, 0)
    return place


Z_MASKS = (2, 4, 6)


def stack_z(x, sizes):
    return jnp.stack([x] + [swap(x, "dp", sizes["dp"], m) for m in Z_MASKS])


def grow(x, axis, mask, sizes):
    return jnp.concatenate([x, swap(x, axis, sizes[axis], mask)], axis=0)


def add(keep, other):
    half = keep.shape[0] // 2
    plus = lambda a, b: (a.astype(F32) + b.astype(F32)).astype(BF)
    return plus(keep[:half], other[:half]), plus(keep[half:], other[half:])


def fold(keep, send, axis, mask, sizes):
    return add(keep, swap(send, axis, sizes[axis], mask))


def fold_z(lo, hi, sizes):
    parts = [lo[0], swap(lo[1], "dp", sizes["dp"], 2), swap(hi[0], "dp", sizes["dp"], 4), swap(hi[1], "dp", sizes["dp"], 6)]
    return sum(p.astype(F32) for p in parts)


def place_table(me_d, me_c):
    d = (jnp.arange(8, dtype=jnp.int32) ^ me_d)[:, None]
    c = (jnp.arange(4, dtype=jnp.int32) ^ me_c)[None, :]
    x, z, y = d & 1, d >> 1, c >> 1
    return (x * 8 + y * 4 + z).reshape(-1), (x * 8 + z * 2 + y).reshape(-1), jnp.broadcast_to(c & 1, (8, 4)).reshape(-1)


def fold_down(d):
    n = d.shape[0] // 2
    return jnp.concatenate([d[:n], d[n:]], axis=1)


def unfold_down(p):
    m = p.shape[1] // 2
    return jnp.concatenate([p[:, :m], p[:, m:]], axis=0)


def after_all(xs, *others):
    return lax.optimization_barrier(tuple(xs) + others)[: len(xs)]


def after(x, *others):
    return lax.optimization_barrier((x,) + others)[0]


def per_device(sizes, tokens, segments, attn_gain, query_weight, key_matrix, value_matrix,
               out_weight, mlp_gain, gate_weight, up_weight, down_weight, cotangent):
    nd, nc = sizes["dp"], sizes["ctx"]
    tokens, cotangent = jnp.swapaxes(tokens, 1, 2), jnp.swapaxes(cotangent, 1, 2)
    seqs, width, rows = tokens.shape
    blk = rows // 2
    me_d = lax.axis_index("dp")
    me_c = lax.axis_index("ctx")
    last = nc - 1
    kvd = GROUPS * HEAD
    qd = HEADS * HEAD
    qn, kn, fn = query_weight.shape[1], key_matrix.shape[1], gate_weight.shape[1]
    ff = fn * nc
    shard = width // nd
    box = nd == 8 and nc == 4
    csteps = [("ctx", b) for b in reversed(bits_of(nc))]
    wsteps = [("dp", b) for b in reversed(bits_of(nd))] + csteps

    pad = lambda n: jnp.zeros((shard, n), BF)
    a_own = jnp.concatenate([query_weight, key_matrix, value_matrix, attn_gain[:, None], pad(15)], axis=1)
    b1_own = jnp.concatenate([gate_weight, up_weight], axis=1)
    b2_own = jnp.concatenate([out_weight, mlp_gain[:, None], pad(111)], axis=1)
    if box:
        b2_own = jnp.concatenate([b2_own, fold_down(down_weight.T)], axis=1)
        ab = stack_z(jnp.concatenate([a_own, b1_own], axis=1), sizes)
        b2_y = grow(b2_own[None], "ctx", 2, sizes)
        tok0_y = grow(tokens[0][None], "ctx", 2, sizes)
        ab, b2_y, tok0_y = lax.optimization_barrier((ab, b2_y, tok0_y))
        a_z, b1_z = ab[..., :256], ab[..., 256:]
        a_y = grow(a_z, "ctx", 2, sizes)
        b1_got = swap(after(b1_z, a_z), "ctx", nc, 2)
        b2_z = [swap(b2_y, "dp", nd, m) for m in Z_MASKS]
        tokens_all = [grow(tok0_y, "ctx", 1, sizes)]
        a_x = grow(a_y, "dp", 1, sizes)
        a_parts = a_x, swap(a_x, "ctx", nc, 1)
        b1_y = jnp.concatenate([b1_z, after(b1_got, a_x)], axis=0)
        b1_got = swap(b1_y, "dp", nd, 1)
        tok1_got = swap(after(tokens[1][None], a_x), "ctx", nc, 2)
        at1, at2, other1 = place_table(me_d, me_c)
        places = jnp.concatenate([at1, at2, other1, me_c[None] & 1, me_c[None], me_d[None]])
        w_all = pl.pallas_call(
            unpack_a_kernel,
            in_specs=[pl.BlockSpec(memory_space=pltpu.SMEM)] + [pl.BlockSpec(memory_space=pltpu.VMEM)] * 2,
            out_specs=pl.BlockSpec(memory_space=pltpu.VMEM),
            out_shape=jax.ShapeDtypeStruct((nd, shard, 1024), BF),
            compiler_params=params(),
            name="unpack_a",
        )(places, *a_parts).reshape(width, 1024)
        b2_z = jnp.stack([b2_y] + list(after_all(b2_z, w_all))).reshape(8, shard, 640)
        b2_got = swap(b2_z, "dp", nd, 1)

    def unpack_b(b1, b1x, b2, b2x):
        b1, b1x = (v.reshape(2, 2, 4, shard, 2 * fn) for v in (b1, b1x))
        b2, b2x = (v.reshape(2, 4, 2, shard, 640) for v in (b2, b2x))
        piece1 = pl.BlockSpec((2, 2, 1, shard, 2 * fn), lambda z, t: (0, 0, jnp.bitwise_xor(z, t[98] // 2), 0, 0))
        piece2 = pl.BlockSpec((2, 1, 2, shard, 640), lambda z, t: (0, jnp.bitwise_xor(z, t[98] // 2), 0, 0, 0))
        duo = lambda n: pl.BlockSpec((2, shard, n), lambda z, t: (z, 0, 0))
        wg, wu, wo, wd = pl.pallas_call(
            unpack_b_kernel,
            grid_spec=pltpu.PrefetchScalarGridSpec(
                num_scalar_prefetch=1,
                grid=(4,),
                in_specs=[piece1, piece1, piece2, piece2],
                out_specs=[duo(ff), duo(ff), duo(640), pl.BlockSpec((nd, shard, ff // 4), lambda z, t: (0, 0, z))],
            ),
            out_shape=[jax.ShapeDtypeStruct((nd, shard, ff), BF), jax.ShapeDtypeStruct((nd, shard, ff), BF),
                       jax.ShapeDtypeStruct((nd, shard, 640), BF), jax.ShapeDtypeStruct((nd, shard, ff), BF)],
            compiler_params=params(),
            name="unpack_b",
        )(places, b1, b1x, b2, b2x)
        return wg.reshape(width, ff), wu.reshape(width, ff), wo.reshape(width, 640), wd.reshape(width, ff)

    if not box:
        dslot = slot_table(wsteps, "dp", nd, me_d)
        cslot = slot_table(wsteps, "ctx", nc, me_c)

        def whole(own):
            x = spread(own, wsteps, sizes)
            x = x.reshape((nc, nd) + own.shape)
            return jnp.take(jnp.take(x, cslot, axis=0), dslot, axis=1)

        def join(x):
            return x.transpose(1, 2, 0, 3).reshape(nd * x.shape[2], nc * x.shape[3])

        a = whole(a_own)
        w_all = jnp.concatenate(
            [join(a[..., :qn]), join(a[..., qn : qn + kn]), join(a[..., qn + kn : qn + 2 * kn]),
             a[0, :, :, 240:241].reshape(width, 1), jnp.zeros((width, 63), BF)], axis=1)
        b1 = whole(b1_own)
        b2 = whole(b2_own)
        wg, wu = join(b1[..., :fn]), join(b1[..., fn:])
        wo = jnp.concatenate([join(b2[..., :qn]), b2[0, :, :, qn : qn + 1].reshape(width, 1), jnp.zeros((width, 63), BF)], axis=1)
        wd = join(whole(down_weight)).T
        places = jnp.zeros((99,), jnp.int32)
        tokens_all = [spread(tokens[s], csteps, sizes) for s in range(seqs)]
        cot_got = swap(cotangent[..., blk:], "ctx", nc, last)

    ctx_bits = [b for _, b in csteps]

    def piece_rel(i):
        return sum(b for k, b in enumerate(ctx_bits) if i >> k & 1)

    place = {piece_rel(i): i for i in range(nc)}

    def balanced(all_pieces):
        rel = [all_pieces[place[r]] for r in range(nc)]
        return jnp.stack([jnp.concatenate([rel[r][..., :blk], rel[r ^ last][..., blk:]], axis=-1) for r in range(nc)])

    seg_all = spread(segments, csteps, sizes)
    owner = me_c ^ jnp.arange(nc, dtype=jnp.int32)
    lane = jnp.arange(blk, dtype=jnp.int32)
    index = jnp.concatenate(
        [owner[:, None] * rows + lane[None], (last - owner[:, None]) * rows + blk + lane[None]], axis=1)
    inverse = ROPE_BASE ** (-2.0 * jnp.arange(HALF).astype(F32) / HEAD)
    table = jnp.asarray(pair_table(nc))[me_c].reshape(-1)
    pairs = 2 * nc + 1
    wide_q = SHARE * blk

    saved = []
    for s in range(seqs):
        zig = balanced(tokens_all[s])
        zseg = balanced(seg_all[:, s])
        before = jnp.where(zseg == 0, 0, jnp.where(zseg == 1, jnp.sum(zseg < 1), jnp.sum(zseg < 2)))
        phase = (index - before).astype(F32)[:, None, :] * inverse[None, :, None]
        cos_t, sin_t = jnp.cos(phase), jnp.sin(phase)

        piece = lambda *tail: pl.BlockSpec((1,) + tail, lambda r: (r,) + (0,) * len(tail))
        fixed = lambda *shape: pl.BlockSpec(shape, lambda r: (0,) * len(shape))
        if s:
            zig = after(zig, prob)
        if s and box:
            zig = after(zig, b1_x)
        h1, k_t, v_t, q_t = pl.pallas_call(
            pre_kernel,
            grid=(nc,),
            in_specs=[piece(width, rows), fixed(width, 1024), piece(HALF, rows), piece(HALF, rows), piece(1, rows)],
            out_specs=[piece(width, rows),
                       pl.BlockSpec((GROUPS, 1, AUG, rows), lambda r: (0, r, 0, 0)),
                       pl.BlockSpec((GROUPS, 1, AUG, rows), lambda r: (0, r, 0, 0)),
                       fixed(GROUPS, 2, AUG, wide_q)],
            out_shape=[jax.ShapeDtypeStruct((nc, width, rows), BF),
                       jax.ShapeDtypeStruct((GROUPS, nc, AUG, rows), BF),
                       jax.ShapeDtypeStruct((GROUPS, nc, AUG, rows), BF),
                       jax.ShapeDtypeStruct((GROUPS, 2, AUG, wide_q), BF)],
            compiler_params=params(),
            cost_estimate=pl.CostEstimate(flops=4_500_000_000, bytes_accessed=10_000_000, transcendentals=0),
            name="pre",
        )(zig, w_all, cos_t, sin_t, zseg[:, None, :])

        if box and s == 0:
            tok1_y = jnp.concatenate([tokens[1][None], after(tok1_got, q_t)], axis=0)
            tokens_all.append(grow(tok1_y, "ctx", 1, sizes))
        if box and s == 1:
            b2_x = jnp.concatenate([b2_z, after(b2_got, q_t)], axis=0)
            b2_far = swap(b2_x, "ctx", nc, 1)
            q_t = after(q_t, b2_x)
        att = lambda *tail: pl.BlockSpec((1,) + tail, lambda g, t: (g,) + (0,) * len(tail))
        prob, o_t, inv_l = pl.pallas_call(
            functools.partial(attend_kernel, pairs),
            grid_spec=pltpu.PrefetchScalarGridSpec(
                num_scalar_prefetch=1,
                grid=(GROUPS,),
                in_specs=[att(2, AUG, wide_q), att(nc, AUG, rows), att(nc, AUG, rows)],
                out_specs=[att(pairs, blk, wide_q), att(2, HEAD, wide_q), att(2, 1, wide_q)],
                scratch_shapes=[pltpu.VMEM((pairs, blk, wide_q), F32), pltpu.VMEM((2, 8, wide_q), F32),
                                pltpu.VMEM((2, AUG, wide_q), F32)],
            ),
            out_shape=[jax.ShapeDtypeStruct((GROUPS, pairs, blk, wide_q), BF),
                       jax.ShapeDtypeStruct((GROUPS, 2, HEAD, wide_q), BF),
                       jax.ShapeDtypeStruct((GROUPS, 2, 1, wide_q), F32)],
            compiler_params=params(),
            cost_estimate=pl.CostEstimate(flops=12_000_000_000, bytes_accessed=12_000_000, transcendentals=0),
            name="attend",
        )(table, q_t, k_t, v_t)
        if box and s == 0:
            b1_x = jnp.concatenate([b1_y, after(b1_got, prob)], axis=0)
            b1_far = swap(b1_x, "ctx", nc, 1)
            cot_got = swap(after(cotangent[..., blk:], prob), "ctx", nc, last)
        if box and s == 1:
            b1_far, b2_far, cot_got = after_all((b1_far, b2_far, cot_got), prob)
            wg, wu, wo, wd = unpack_b(b1_x, b1_far, b2_x, b2_far)
        saved.append((zig, cos_t, sin_t, h1, k_t, v_t, q_t, prob, o_t, inv_l))

    cot = jnp.concatenate([cotangent[..., :blk], cot_got], axis=-1)

    x_own = jnp.stack([v[0][0] for v in saved])
    total = seqs * rows
    o_pair = jnp.stack([v[8] for v in saved])
    steps = nc
    fstep = ff // steps
    fixed = lambda *shape: pl.BlockSpec(shape, lambda f, t: (0,) * len(shape))
    if box:
        grad_specs = [fixed(16, shard, 2 * fn)] * 2 + [fixed(16, shard, 640)] * 2
        grad_shapes = [jax.ShapeDtypeStruct((16, shard, 2 * fn), BF)] * 2 + [jax.ShapeDtypeStruct((16, shard, 640), BF)] * 2
    else:
        grad_specs = [pl.BlockSpec((width, fstep), lambda f, t: (0, f))] * 2
        grad_specs += [pl.BlockSpec((width, fstep), lambda f, t: (0, f)), fixed(width, 640)]
        grad_shapes = [jax.ShapeDtypeStruct((width, ff), BF)] * 3 + [jax.ShapeDtypeStruct((width, 640), BF)]
    output, d_middle, do_t, *grads = pl.pallas_call(
        functools.partial(middle_kernel, box, nd, nc),
        grid_spec=pltpu.PrefetchScalarGridSpec(
            num_scalar_prefetch=1,
            grid=(steps,),
            in_specs=[fixed(seqs, width, rows), fixed(seqs, width, rows), fixed(seqs, GROUPS, 2, HEAD, wide_q)]
            + [pl.BlockSpec((width, fstep), lambda f, t: (0, f))] * 3 + [fixed(width, 640)],
            out_specs=[fixed(seqs, width, rows), fixed(seqs, width, rows), fixed(seqs, GROUPS, 2, HEAD, wide_q)] + grad_specs,
            scratch_shapes=[pltpu.VMEM((qd, total), BF), pltpu.VMEM((width, total), F32), pltpu.VMEM((width, total), BF),
                            pltpu.VMEM((width, total), BF), pltpu.VMEM((width, total), F32), pltpu.VMEM((width, total), F32)],
        ),
        out_shape=[jax.ShapeDtypeStruct((seqs, width, rows), BF), jax.ShapeDtypeStruct((seqs, width, rows), F32),
                   jax.ShapeDtypeStruct((seqs, GROUPS, 2, HEAD, wide_q), BF)] + grad_shapes,
        compiler_params=params(),
        cost_estimate=pl.CostEstimate(flops=36_000_000_000, bytes_accessed=20_000_000, transcendentals=0),
        name="middle",
    )(places, x_own, cot, o_pair, wg, wu, wd, wo)

    def settle(pieces):
        x = jnp.take(jnp.take(pieces, jnp.argsort(dslot), axis=0), jnp.argsort(cslot), axis=1)
        x = jnp.swapaxes(x, 0, 1).reshape((nc * nd,) + pieces.shape[2:])
        return gather_up(x, wsteps, sizes).astype(F32)

    def cut(g):
        r, c = g.shape
        return g.reshape(nd, r // nd, nc, c // nc).transpose(0, 2, 1, 3)

    def repeat(column):
        return jnp.broadcast_to(column.reshape(nd, 1, shard, 1), (nd, nc, shard, 1))

    if box:
        b1_got = swap(grads[1], "ctx", nc, 1)
        b2_got = swap(grads[3], "ctx", nc, 1)
    else:
        gate_sum, up_sum, down_sum = settle(cut(grads[0])), settle(cut(grads[1])), settle(cut(grads[2].T))
        b2_sum = settle(jnp.concatenate([cut(grads[3][:, :qd]), repeat(grads[3][:, qd])], axis=-1))
        out_sum, gain2_sum = b2_sum[:, :qn], b2_sum[:, qn]

    out_away = swap(output[..., blk:], "ctx", nc, last)
    half = nc // 2
    backs, dkv_owns = [], []
    for s in range(seqs):
        zig, cos_t, sin_t, h1, k_t, v_t, q_t, prob, o_t, inv_l = saved[s]
        if s:
            q_t = after(q_t, backs[0][1], *((b1 + b2) if box else ()))
        att = lambda *tail: pl.BlockSpec((1,) + tail, lambda g, t: (g,) + (0,) * len(tail))
        fixed = lambda *shape: pl.BlockSpec(shape, lambda g, t: (0,) * len(shape))
        pair_of = pl.BlockSpec((1, 1, 2, HEAD, wide_q), lambda g, t: (s, g, 0, 0, 0))
        kv_out = pl.BlockSpec((half, 2, 1, HEAD, rows), lambda g, t: (0, 0, g, 0, 0))
        dq_t, near, far = pl.pallas_call(
            functools.partial(attend_back_kernel, pairs, tuple(place[r] for r in range(nc))),
            grid_spec=pltpu.PrefetchScalarGridSpec(
                num_scalar_prefetch=1,
                grid=(GROUPS,),
                in_specs=[att(pairs, blk, wide_q), att(2, AUG, wide_q), att(nc, AUG, rows), att(nc, AUG, rows),
                          att(2, HEAD, wide_q), pair_of, att(2, 1, wide_q), fixed(nc, HALF, rows), fixed(nc, HALF, rows)],
                out_specs=[att(SHARE, HEAD, rows), kv_out, kv_out],
                scratch_shapes=[pltpu.VMEM((2, AUG, wide_q), BF), pltpu.VMEM((2 * nc, HEAD, blk), F32),
                                pltpu.VMEM((2 * nc, HEAD, blk), F32), pltpu.VMEM((2, HEAD, wide_q), F32)],
            ),
            out_shape=[jax.ShapeDtypeStruct((GROUPS, SHARE, HEAD, rows), BF)]
            + [jax.ShapeDtypeStruct((half, 2, GROUPS, HEAD, rows), BF)] * 2,
            compiler_params=params(),
            cost_estimate=pl.CostEstimate(flops=20_000_000_000, bytes_accessed=12_000_000, transcendentals=0),
            name="attend_back",
        )(table, prob, q_t, k_t, v_t, o_t, do_t, inv_l, cos_t, sin_t)
        near, far = near.reshape(half, 2 * kvd, rows), far.reshape(half, 2 * kvd, rows)
        backs.append((dq_t.reshape(qd, rows), near, far, h1))
        dkv_got = swap(far, "ctx", nc, csteps[-1][1])
        if s == 0:
            first = near, dkv_got
            if box:
                b1_got, b2_got = after_all((b1_got, b2_got), near)
                b1, b2 = add(grads[0], b1_got), add(grads[2], b2_got)
                b1_got = swap(b1[1], "dp", nd, 1)
        else:
            if box:
                b1_got = after(b1_got, near)
                b1 = add(b1[0], b1_got)
                b2_got = swap(after(b2[1], b1_got), "dp", nd, 1)
                b1_got = swap(b1[1], "ctx", nc, 2)
            near0, got0 = after_all(first, near)
            for mine, got in ((near0, got0), (near, dkv_got)):
                low, high = add(mine, got)
                dkv_owns.append((low, swap(high, "ctx", nc, csteps[0][1])))

    spot = [place[r] for r in range(nc)]
    part_of = pl.BlockSpec((1, 2 * kvd, rows), lambda r, t: (r % half, 0, 0))
    hid_of = pl.BlockSpec((1, width, rows), lambda r, t: (t[99 + r], 0, 0))
    fixed = lambda *shape: pl.BlockSpec(shape, lambda r, t: (0,) * len(shape))
    if box:
        a_specs = [fixed(16, shard, 256)] * 2
        a_shapes = [jax.ShapeDtypeStruct((16, shard, 256), BF)] * 2
    else:
        a_specs, a_shapes = [fixed(width, 1024)], [jax.ShapeDtypeStruct((width, 1024), BF)]
    ops = [v for back in backs for v in back]
    ops[0] = after(ops[0], *[v for low, _ in dkv_owns for v in [low]], *((b1[0], b2[1]) if box else ()))
    places = jnp.concatenate([places, jnp.asarray([spot.index(i) for i in range(nc)], jnp.int32)])
    a_out = pl.pallas_call(
        functools.partial(post_kernel, box, nd, nc, seqs),
        grid_spec=pltpu.PrefetchScalarGridSpec(
            num_scalar_prefetch=1,
            grid=(nc,),
            in_specs=[fixed(qd, rows), part_of, part_of, hid_of] * seqs + [fixed(width, 1024)],
            out_specs=a_specs,
            scratch_shapes=[pltpu.VMEM((width, 1024), F32)],
        ),
        out_shape=a_shapes,
        compiler_params=params(),
        cost_estimate=pl.CostEstimate(flops=15_000_000_000, bytes_accessed=10_000_000, transcendentals=0),
        name="post",
    )(places, *ops, w_all)

    a_got = swap(a_out[1], "ctx", nc, 1) if box else None
    if box:
        b1_got, b2_got = after_all((b1_got, b2_got), a_out[0])
        b1, b2 = add(b1[0], b1_got), add(b2[0], b2_got)
        b1_parts = [b1[0][0]] + [swap(p, "dp", nd, m) for p, m in zip((b1[0][1], b1[1][0], b1[1][1]), Z_MASKS)]
        b2_parts = [b2[0][:2]] + [swap(p, "dp", nd, m) for p, m in zip((b2[0][2:], b2[1][:2], b2[1][2:]), Z_MASKS)]
    dkv_owns = [(low, after(got, a_out[0])) for low, got in dkv_owns]
    token_grads, token_away = [], []
    for s in range(seqs):
        dqr_t = after(backs[s][0], a_out[0])
        dkv_own = (dkv_owns[s][0][0].astype(F32) + dkv_owns[s][1][0].astype(F32)).astype(BF)
        token_grads.append(pl.pallas_call(
            token_kernel,
            out_shape=jax.ShapeDtypeStruct((width, rows), BF),
            compiler_params=params(),
            cost_estimate=pl.CostEstimate(flops=2_000_000_000, bytes_accessed=5_000_000, transcendentals=0),
            name="token",
        )(dqr_t, dkv_own, w_all, x_own[s], d_middle[s]))
        token_away.append(swap(token_grads[s][:, blk:], "ctx", nc, last))
    if box:
        b1_parts, b2_parts = after_all(b1_parts, token_grads[-1]), after_all(b2_parts, token_grads[-1])
        total_of = lambda parts: sum(p.astype(F32) for p in parts)
        b1_sum = total_of(b1_parts)
        b2 = total_of(b2_parts).astype(BF)
        b2_sum = b2[0].astype(F32) + swap(b2[1], "ctx", nc, 2).astype(F32)
        gate_sum, up_sum = b1_sum[:, :fn], b1_sum[:, fn:]
        out_sum, gain2_sum, down_sum = b2_sum[:, :qn], b2_sum[:, qn], unfold_down(b2_sum[:, 256:]).T

    if box:
        a = fold(*add(a_out[0], a_got), "dp", 1, sizes)
        a = fold(*a, "ctx", 2, sizes)
        a_sum = fold_z(*a, sizes)
    else:
        a = a_out[0]
        a_sum = settle(jnp.concatenate(
            [cut(a[:, :qd]), cut(a[:, qd : qd + kvd]), cut(a[:, qd + kvd : qd + 2 * kvd]), repeat(a[:, 960])], axis=-1))

    def home(mine, away):
        return jnp.swapaxes(jnp.concatenate([mine[..., :blk], away], axis=-1), 1, 2)

    return (
        home(output, out_away),
        home(jnp.stack(token_grads), jnp.stack(token_away)),
        a_sum[:, 2 * kn + qn],
        a_sum[:, :qn],
        a_sum[:, qn : qn + kn],
        a_sum[:, qn + kn : qn + 2 * kn],
        out_sum,
        gain2_sum,
        gate_sum,
        up_sum,
        down_sum,
    )


def pair_table(nc):
    out = []
    for me in range(nc):
        spots = {}
        for r in range(nc):
            d = me ^ r
            spots[2 * d] = 2 * r
            spots[2 * (nc - 1 - d) + 1] = 2 * r + 1
        mine = [2 * me, 2 * (nc - 1 - me) + 1]
        rows = [(i, spots[mine[i]]) for i in range(2)]
        rows += [(i, spots[k]) for i in range(2) for k in range(mine[i])]
        out.append(rows)
    return np.array(out, np.int32)


def turn(x, cos, sin, heads, sign):
    parts = []
    for h in range(heads):
        lo, hi = x[h * HEAD : h * HEAD + HALF], x[h * HEAD + HALF : (h + 1) * HEAD]
        parts += [lo * cos - sign * hi * sin, hi * cos + sign * lo * sin]
    return jnp.concatenate(parts, axis=0)


def unpack_a_kernel(places, own_ref, other_ref, w_ref):
    nd = w_ref.shape[0]
    nc = 4
    qn, kn = 144, 48
    qd, kvd = qn * nc, kn * nc

    def write(cores):
        for d in range(nd):
            for c in range(nc):
                p = cores[c % 2][places[d * nc + c]].astype(F32)
                if c == 0:
                    cols = [[], [], []]
                    gain = p[:, 240:256]
                cols[0].append(p[:, :qn])
                cols[1].append(p[:, qn : qn + kn])
                cols[2].append(p[:, qn + kn : qn + 2 * kn])
            row = cols[0] + cols[1] + cols[2] + [gain, jnp.zeros((p.shape[0], 48), F32)]
            w_ref[d] = jnp.concatenate(row, axis=1).astype(BF)

    core = places[96]
    pl.when(core == 0)(lambda: write((own_ref, other_ref)))
    pl.when(core == 1)(lambda: write((other_ref, own_ref)))


def unpack_b_kernel(places, b1_ref, b1x_ref, b2_ref, b2x_ref, g_ref, u_ref, o_ref, w_ref):
    nc = 4
    fn = b1_ref.shape[-1] // 2
    shard = b1_ref.shape[-2]
    me_y, me_x = places[97] // 2, places[98] % 2

    def write(one, two):
        for x in range(2):
            at_x = jnp.bitwise_xor(me_x, x)
            outs = []
            for c in range(nc):
                y = jnp.bitwise_xor(me_y, c // 2)
                p = one[c % 2][at_x, y, 0]
                g_ref[x, :, c * fn : (c + 1) * fn] = p[:, :fn]
                u_ref[x, :, c * fn : (c + 1) * fn] = p[:, fn:]
                p = two[c % 2][at_x, 0, y].astype(F32)
                outs.append(p[:, :144])
                for i in range(2):
                    w_ref[2 * c + i, :, x * 192 : (x + 1) * 192] = p[:, 256 + 192 * i : 448 + 192 * i].astype(BF)
                if c == 0:
                    gain = p[:, 144:160]
            o_ref[x] = jnp.concatenate(outs + [gain, jnp.zeros((shard, 48), F32)], axis=1).astype(BF)

    core = places[96]
    pl.when(core == 0)(lambda: write((b1_ref, b1x_ref), (b2_ref, b2x_ref)))
    pl.when(core == 1)(lambda: write((b1x_ref, b1_ref), (b2x_ref, b2_ref)))


def pre_kernel(x_ref, w_ref, cos_ref, sin_ref, seg_ref, h_ref, k_ref, v_ref, q_ref):
    x = x_ref[0].astype(F32)
    inv = lax.rsqrt(jnp.mean(x * x, axis=0, keepdims=True) + EPS)
    qd, kvd = HEADS * HEAD, GROUPS * HEAD
    gain = w_ref[:, qd + 2 * kvd : qd + 2 * kvd + 1].astype(F32)
    h = ((x * inv) * gain).astype(BF)
    h_ref[0] = h
    cos, sin, seg = cos_ref[0], sin_ref[0], seg_ref[0]
    rows = x.shape[1]
    blk = rows // 2
    kv = dot(w_ref[:, qd : qd + 2 * kvd], h, TN)
    keys = turn(kv[:kvd], cos, sin, GROUPS, 1.0).astype(BF)
    values = kv[kvd:].astype(BF)
    row = lax.broadcasted_iota(jnp.int32, (AUG - HEAD, rows), 0)
    other = jnp.where((row < 3) & (row != seg), -1e30, 0.0).astype(BF)
    ones = (row < 3).astype(BF)
    for g in range(GROUPS):
        k_ref[g, 0, :HEAD] = keys[g * HEAD : (g + 1) * HEAD]
        k_ref[g, 0, HEAD:] = other
        v_ref[g, 0, :HEAD] = values[g * HEAD : (g + 1) * HEAD]
        v_ref[g, 0, HEAD:] = ones

    @pl.when(pl.program_id(0) == 0)
    def _():
        q = turn(dot(w_ref[:, :qd], h, TN), cos, sin, HEADS, 1.0).astype(BF) * (1.0 / math.sqrt(HEAD))
        same = (row == seg).astype(BF)
        for g in range(GROUPS):
            for b in range(2):
                for j in range(SHARE):
                    n = g * SHARE + j
                    q_ref[g, b, :HEAD, j * blk : (j + 1) * blk] = q[n * HEAD : (n + 1) * HEAD, b * blk : (b + 1) * blk]
                    q_ref[g, b, HEAD:, j * blk : (j + 1) * blk] = same[:, b * blk : (b + 1) * blk]


def middle_kernel(box, nd, nc, places, x_ref, cot_ref, ot_ref, wg_ref, wu_ref, wd_ref, wo_ref,
                  out_ref, dm_ref, do_ref, *rest):
    grads, (att_ref, mid_ref, h_ref, cots_ref, acc_ref, dh_ref) = rest[:4], rest[4:]
    f = pl.program_id(0)
    seqs, _, _, _, wide = ot_ref.shape
    blk = wide // SHARE
    rows = 2 * blk
    qd, width = HEADS * HEAD, x_ref.shape[1]
    shard = width // nd
    fn = wg_ref.shape[1]

    def norm():
        m = mid_ref[...]
        inv = lax.rsqrt(jnp.mean(m * m, axis=0, keepdims=True) + EPS)
        return m, inv, m * inv

    def gain_column():
        return wo_ref[:, qd : qd + 1].astype(F32)

    def of(s):
        return slice(s * rows, (s + 1) * rows)

    def blocks():
        for s in range(seqs):
            for g in range(GROUPS):
                for b in range(2):
                    for j in range(SHARE):
                        n = g * SHARE + j
                        yield (s, g, b, slice(None), slice(j * blk, (j + 1) * blk)), (
                            slice(n * HEAD, (n + 1) * HEAD), slice(s * rows + b * blk, s * rows + (b + 1) * blk))

    @pl.when(f == 0)
    def _():
        for there, here in blocks():
            att_ref[here] = ot_ref[there]
        branch = dot(wo_ref[:, :qd], att_ref[...], TN)
        for s in range(seqs):
            mid_ref[:, of(s)] = x_ref[s].astype(F32) + branch[:, of(s)]
            cots_ref[:, of(s)] = cot_ref[s]
        _, _, n2 = norm()
        h_ref[...] = (n2 * gain_column()).astype(BF)

    h = h_ref[...]
    cot = cots_ref[...]
    gate = dot(wg_ref[...], h, TN)
    up = dot(wu_ref[...], h, TN)
    sig = jax.nn.sigmoid(gate)
    act = gate * sig
    inner = (act * up).astype(BF)
    part = dot(wd_ref[...], inner, NN)
    d_inner = dot(wd_ref[...], cot, TN)
    d_gate = (d_inner * up * (sig + act * (1.0 - sig))).astype(BF)
    d_up = (d_inner * act).astype(BF)
    d_part = dot(wg_ref[...], d_gate, NN) + dot(wu_ref[...], d_up, NN)

    @pl.when(f == 0)
    def _():
        acc_ref[...] = part
        dh_ref[...] = d_part

    @pl.when(f > 0)
    def _():
        acc_ref[...] += part
        dh_ref[...] += d_part

    grad_gate = dot(h, d_gate, NT)
    grad_up = dot(h, d_up, NT)
    grad_down = dot(cot, inner, NT)
    if box:
        b1, b1x, b2, b2x = grads

        def put(near, far, c, at, lanes, value):
            @pl.when(places[64 + c] == 0)
            def _():
                near[at, :, lanes] = value

            @pl.when(places[64 + c] == 1)
            def _():
                far[at, :, lanes] = value

        for d in range(nd):
            part_rows = slice(d * shard, (d + 1) * shard)
            at = places[d * nc + f]
            put(b1, b1x, f, at, slice(0, fn), grad_gate[part_rows].astype(BF))
            put(b1, b1x, f, at, slice(fn, 2 * fn), grad_up[part_rows].astype(BF))
        per = fn * nc // nd
        for i in range(fn // per):
            for c in range(nc):
                p = fold_down(grad_down[c * 144 : (c + 1) * 144, i * per : (i + 1) * per]).astype(BF)
                put(b2, b2x, c, places[32 + (f * (fn // per) + i) * nc + c], slice(256, 640), p)
    else:
        grads[0][...] = grad_gate.astype(BF)
        grads[1][...] = grad_up.astype(BF)
        grads[2][...] = grad_down.astype(BF)

    @pl.when(f == pl.num_programs(0) - 1)
    def _():
        m, inv, n2 = norm()
        out = (m + acc_ref[...]).astype(BF)
        d_h2 = dh_ref[...]
        e2 = d_h2 * gain_column()
        d_middle = cots_ref[...].astype(F32) + inv * (e2 - n2 * jnp.mean(e2 * n2, axis=0, keepdims=True))
        for s in range(seqs):
            out_ref[s] = out[:, of(s)]
            dm_ref[s] = d_middle[:, of(s)]
        branch = d_middle.astype(BF)
        d_att = dot(wo_ref[:, :qd], branch, NN).astype(BF)
        for there, here in blocks():
            do_ref[there] = d_att[here]
        grad_out = dot(att_ref[...], branch, NT)
        gain = jnp.broadcast_to(jnp.sum(d_h2 * n2, axis=1, keepdims=True), (width, 128))
        if box:
            for d in range(nd):
                part_rows = slice(d * shard, (d + 1) * shard)
                for c in range(nc):
                    p = jnp.concatenate([grad_out[part_rows, c * 144 : (c + 1) * 144], gain[part_rows, :112]], axis=1)
                    put(b2, b2x, c, places[32 + d * nc + c], slice(0, 256), p.astype(BF))
        else:
            grads[3][...] = jnp.concatenate([grad_out, gain[:, :64]], axis=1).astype(BF)


def post_kernel(box, nd, nc, seqs, places, *refs):
    ops, w_ref, outs, acc_ref = refs[: 4 * seqs], refs[4 * seqs], refs[4 * seqs + 1 : -1], refs[-1]
    kvd, qd = GROUPS * HEAD, HEADS * HEAD
    r = pl.program_id(0)

    @pl.when(r == 0)
    def _():
        acc_ref[...] = jnp.zeros_like(acc_ref)
        acc_ref[:, :qd] = sum(dot(ops[4 * s + 3][0], ops[4 * s][...], NT) for s in range(seqs))

    @pl.when(r < nc // 2)
    def _():
        acc_ref[:, qd : qd + 2 * kvd] += sum(dot(ops[4 * s + 3][0], ops[4 * s + 1][0], NT) for s in range(seqs))

    @pl.when(r >= nc // 2)
    def _():
        acc_ref[:, qd : qd + 2 * kvd] += sum(dot(ops[4 * s + 3][0], ops[4 * s + 2][0], NT) for s in range(seqs))

    @pl.when(r == nc - 1)
    def _():
        g = acc_ref[...]
        w = w_ref[...].astype(F32)
        used = qd + 2 * kvd
        gain = jnp.sum(g[:, :used] * w[:, :used], axis=1, keepdims=True) / w[:, used : used + 1]
        if not box:
            outs[0][...] = jnp.concatenate([g[:, :used], jnp.broadcast_to(gain, (g.shape[0], 64))], axis=1).astype(BF)
            return
        shard = g.shape[0] // nd
        gain = jnp.broadcast_to(gain, (g.shape[0], 16))
        qn, kn = qd // nc, kvd // nc
        for d in range(nd):
            r = slice(d * shard, (d + 1) * shard)
            for c in range(nc):
                p = jnp.concatenate(
                    [g[r, c * qn : (c + 1) * qn], g[r, qd + c * kn : qd + (c + 1) * kn],
                     g[r, qd + kvd + c * kn : qd + kvd + (c + 1) * kn], gain[r]], axis=1).astype(BF)
                at = places[d * nc + c]

                @pl.when(places[64 + c] == 0)
                def _():
                    outs[0][at] = p

                @pl.when(places[64 + c] == 1)
                def _():
                    outs[1][at] = p


def token_kernel(dq_ref, dkv_ref, w_ref, x_ref, dm_ref, out_ref):
    qd, kvd = HEADS * HEAD, GROUPS * HEAD
    x = x_ref[...].astype(F32)
    inv = lax.rsqrt(jnp.mean(x * x, axis=0, keepdims=True) + EPS)
    n1 = x * inv
    d_h1 = dot(w_ref[:, :qd], dq_ref[...], NN) + dot(w_ref[:, qd : qd + 2 * kvd], dkv_ref[...], NN)
    e1 = d_h1 * w_ref[:, qd + 2 * kvd : qd + 2 * kvd + 1].astype(F32)
    out_ref[...] = (dm_ref[...] + inv * (e1 - n1 * jnp.mean(e1 * n1, axis=0, keepdims=True))).astype(BF)


def key_block(ref, loc, blk, rows=None):
    r, half = loc // 2, loc % 2
    lanes = pl.ds(pl.multiple_of(half * blk, blk), blk)
    if rows is None:
        return ref[0, r, :, lanes]
    return ref[0, r, :rows, lanes]


def attend_kernel(pairs, table, q_ref, k_ref, v_ref, p_ref, o_ref, l_ref, s_ref, m_ref, acc_ref):
    wide = q_ref.shape[-1]
    blk = wide // SHARE

    def score(t, diagonal):
        qb, loc = table[2 * t], table[2 * t + 1]
        s = dot(key_block(k_ref, loc, blk), q_ref[0, qb], TN)
        if diagonal:
            k_at = lax.broadcasted_iota(jnp.int32, (blk, wide), 0)
            q_at = lax.broadcasted_iota(jnp.int32, (blk, wide), 1) % blk
            s = jnp.where(k_at <= q_at, s, -1e30)
        s_ref[t] = s
        top = jnp.max(s.reshape(blk // 8, 8, wide), axis=0)
        if diagonal:
            m_ref[qb] = top
        else:
            m_ref[qb] = jnp.maximum(m_ref[qb], top)

    for t in range(2):
        score(t, True)
    lax.fori_loop(2, pairs, lambda t, c: (score(t, False), c)[1], 0, unroll=pairs - 2)
    for b in range(2):
        m_ref[b] = jnp.broadcast_to(jnp.max(m_ref[b], axis=0, keepdims=True), m_ref.shape[1:])
    acc_ref[...] = jnp.zeros_like(acc_ref)

    def weigh(t, c):
        qb, loc = table[2 * t], table[2 * t + 1]
        p = jnp.exp(s_ref[t] - m_ref[qb, 0:1]).astype(BF)
        p_ref[0, t] = p
        acc_ref[qb] += dot(key_block(v_ref, loc, blk), p, NN)
        return c

    lax.fori_loop(0, pairs, weigh, 0, unroll=pairs)
    for b in range(2):
        inv = 1.0 / acc_ref[b, HEAD : HEAD + 1]
        l_ref[0, b] = inv
        o_ref[0, b] = (acc_ref[b, :HEAD] * inv).astype(BF)


def attend_back_kernel(pairs, order, table, p_ref, q_ref, k_ref, v_ref, o_ref, do_ref, l_ref, cos_ref, sin_ref,
                       dq_ref, near_ref, far_ref, da_ref, dka_ref, dva_ref, dqa_ref):
    wide = q_ref.shape[-1]
    blk = wide // SHARE
    row = lax.broadcasted_iota(jnp.int32, (AUG - HEAD, wide), 0)
    for b in range(2):
        d = (do_ref[0, 0, b].astype(F32) * l_ref[0, b]).astype(BF)
        delta = -jnp.sum(d.astype(F32) * o_ref[0, b].astype(F32), axis=0, keepdims=True)
        hi = delta.astype(BF).astype(F32)
        mid = (delta - hi).astype(BF).astype(F32)
        low = delta - hi - mid
        da_ref[b, :HEAD] = d
        da_ref[b, HEAD:] = jnp.where(row == 0, hi, jnp.where(row == 1, mid, jnp.where(row == 2, low, 0.0))).astype(BF)
    dka_ref[...] = jnp.zeros_like(dka_ref)
    dva_ref[...] = jnp.zeros_like(dva_ref)
    dqa_ref[...] = jnp.zeros_like(dqa_ref)

    def step(t, c):
        qb, loc = table[2 * t], table[2 * t + 1]
        p = p_ref[0, t]
        dp = dot(key_block(v_ref, loc, blk), da_ref[qb], TN)
        ds = (p.astype(F32) * dp).astype(BF)
        dqa_ref[qb] += dot(key_block(k_ref, loc, blk, HEAD), ds, NN)
        dka_ref[loc] += dot(q_ref[0, qb, :HEAD], ds, NT)
        dva_ref[loc] += dot(da_ref[qb, :HEAD], p, NT)
        return c

    lax.fori_loop(0, pairs, step, 0, unroll=pairs)
    scale = 1.0 / math.sqrt(HEAD)
    for b in range(2):
        lanes = slice(b * blk, (b + 1) * blk)
        cos, sin = cos_ref[0, :, lanes] * scale, sin_ref[0, :, lanes] * scale
        for j in range(SHARE):
            dq_ref[0, j, :, lanes] = turn(dqa_ref[b, :, j * blk : (j + 1) * blk], cos, sin, 1, -1.0).astype(BF)
    half = len(order) // 2
    for r, at in enumerate(order):
        out_ref = near_ref if at < half else far_ref
        for b in range(2):
            lanes = slice(b * blk, (b + 1) * blk)
            cos, sin = cos_ref[r, :, lanes], sin_ref[r, :, lanes]
            out_ref[at % half, 0, 0, :, lanes] = turn(dka_ref[2 * r + b], cos, sin, 1, -1.0).astype(BF)
            out_ref[at % half, 1, 0, :, lanes] = dva_ref[2 * r + b].astype(BF)


def solution(mesh):
    sizes = {name: mesh.shape[name] for name in ("dp", "ctx")}
    rows = P("dp", "ctx", None)
    grid = P("dp", "ctx")
    line = P("dp")
    return jax.shard_map(
        functools.partial(per_device, sizes),
        mesh=mesh,
        in_specs=(rows, grid, line, grid, grid, grid, grid, line, grid, grid, grid, rows),
        out_specs=(rows, rows, line, grid, grid, grid, grid, line, grid, grid, grid),
        check_vma=False,
    )
```

```python
import functools
import math

import jax
import jax.numpy as jnp
import numpy as np
from jax import lax
from jax.experimental import pallas as pl
from jax.experimental.pallas import tpu as pltpu
from jax.sharding import PartitionSpec as P

HEADS = 9
GROUPS = 3
SHARE = HEADS // GROUPS
HEAD = 64
HALF = HEAD // 2
AUG = HEAD + 16
EPS = 1e-05
ROPE_BASE = 100000.0
VMEM = 56 << 20
BF = jnp.bfloat16
F32 = jnp.float32


def params(semantics=None):
    return pltpu.CompilerParams(vmem_limit_bytes=VMEM, dimension_semantics=semantics)


def dot(a, b, dims):
    return lax.dot_general(a, b, (dims, ((), ())), preferred_element_type=F32)


NN = ((1,), (0,))
NT = ((1,), (1,))
TN = ((0,), (0,))


def swap(x, axis, size, mask):
    return lax.ppermute(x, axis, [(i, i ^ mask) for i in range(size)])


def bits_of(size):
    return [1 << k for k in range(size.bit_length() - 1)]


def spread(x, steps, sizes):
    x = x[None]
    for axis, bit in steps:
        x = jnp.concatenate([x, swap(x, axis, sizes[axis], bit)], axis=0)
    return x


def gather_up(x, steps, sizes):
    for axis, bit in reversed(steps):
        half = x.shape[0] // 2
        other = swap(x[half:], axis, sizes[axis], bit)
        x = (x[:half].astype(F32) + other.astype(F32)).astype(x.dtype)
    return x[0]


def slot_table(steps, axis, size, me):
    order = [bit for a, bit in steps if a == axis]
    rel = jnp.arange(size, dtype=jnp.int32) ^ me
    place = jnp.zeros_like(rel)
    for k, bit in enumerate(order):
        place = place | jnp.where((rel & bit) != 0, 1 << k, 0)
    return place


Z_MASKS = (2, 4, 6)


def stack_z(x, sizes):
    return jnp.stack([x] + [swap(x, "dp", sizes["dp"], m) for m in Z_MASKS])


def grow(x, axis, mask, sizes):
    return jnp.concatenate([x, swap(x, axis, sizes[axis], mask)], axis=0)


def add(keep, other):
    half = keep.shape[0] // 2
    plus = lambda a, b: (a.astype(F32) + b.astype(F32)).astype(BF)
    return plus(keep[:half], other[:half]), plus(keep[half:], other[half:])


def fold(keep, send, axis, mask, sizes):
    return add(keep, swap(send, axis, sizes[axis], mask))


def fold_z(lo, hi, sizes):
    parts = [lo[0], swap(lo[1], "dp", sizes["dp"], 2), swap(hi[0], "dp", sizes["dp"], 4), swap(hi[1], "dp", sizes["dp"], 6)]
    return sum(p.astype(F32) for p in parts)


def place_table(me_d, me_c):
    d = (jnp.arange(8, dtype=jnp.int32) ^ me_d)[:, None]
    c = (jnp.arange(4, dtype=jnp.int32) ^ me_c)[None, :]
    x, z, y = d & 1, d >> 1, c >> 1
    return (x * 8 + y * 4 + z).reshape(-1), (z * 4 + x * 2 + y).reshape(-1), jnp.broadcast_to(c & 1, (8, 4)).reshape(-1)


def fold_down(d):
    n = d.shape[0] // 2
    return jnp.concatenate([d[:n], d[n:]], axis=1)


def unfold_down(p):
    m = p.shape[1] // 2
    return jnp.concatenate([p[:, :m], p[:, m:]], axis=0)


def after_all(xs, *others):
    return lax.optimization_barrier(tuple(xs) + others)[: len(xs)]


def after(x, *others):
    return lax.optimization_barrier((x,) + others)[0]


def per_device(sizes, tokens, segments, attn_gain, query_weight, key_matrix, value_matrix,
               out_weight, mlp_gain, gate_weight, up_weight, down_weight, cotangent):
    nd, nc = sizes["dp"], sizes["ctx"]
    tokens, cotangent = jnp.swapaxes(tokens, 1, 2), jnp.swapaxes(cotangent, 1, 2)
    seqs, width, rows = tokens.shape
    blk = rows // 2
    me_d = lax.axis_index("dp")
    me_c = lax.axis_index("ctx")
    last = nc - 1
    kvd = GROUPS * HEAD
    qd = HEADS * HEAD
    qn, kn, fn = query_weight.shape[1], key_matrix.shape[1], gate_weight.shape[1]
    ff = fn * nc
    shard = width // nd
    box = nd == 8 and nc == 4
    csteps = [("ctx", b) for b in reversed(bits_of(nc))]
    wsteps = [("dp", b) for b in reversed(bits_of(nd))] + csteps

    pad = lambda n: jnp.zeros((shard, n), BF)
    a_own = jnp.concatenate([query_weight, key_matrix, value_matrix, attn_gain[:, None], pad(15)], axis=1)
    b1_own = jnp.concatenate([gate_weight, up_weight], axis=1)
    b2_own = jnp.concatenate([out_weight, mlp_gain[:, None], pad(111)], axis=1)
    if box:
        b2_own = jnp.concatenate([b2_own, fold_down(down_weight.T)], axis=1)
        ab = stack_z(jnp.concatenate([a_own, b1_own], axis=1), sizes)
        tok0 = tokens[0][None]
        tok0_y = grow(tok0, "ctx", 2, sizes)
        b2_y = grow(after(b2_own[None], tok0), "ctx", 2, sizes)
        ab, tok0_y, b2_y, segments = lax.optimization_barrier((ab, tok0_y, b2_y, segments))
        a_z, b1_z = ab[..., :256], ab[..., 256:]
        a_y = grow(a_z, "ctx", 2, sizes)
        seg_all = spread(segments, csteps, sizes)
        b1_got = swap(after(b1_z, a_y), "ctx", nc, 2)
        b2_got = swap(b2_y, "dp", nd, 1)
        tokens_all = [(tok0_y, swap(tok0_y, "ctx", nc, 1))]
        a_x = grow(a_y, "dp", 1, sizes)
        a_parts = a_x, swap(a_x, "ctx", nc, 1)
        tok1_got = swap(after(tokens[1][None], a_x), "ctx", nc, 2)
        at1, at2, other1 = place_table(me_d, me_c)
        places = jnp.concatenate([at1, at2, other1, me_c[None] & 1, me_c[None], me_d[None]])
        w_all = pl.pallas_call(
            unpack_a_kernel,
            in_specs=[pl.BlockSpec(memory_space=pltpu.SMEM)] + [pl.BlockSpec(memory_space=pltpu.VMEM)] * 2,
            out_specs=pl.BlockSpec(memory_space=pltpu.VMEM),
            out_shape=jax.ShapeDtypeStruct((nd, shard, 1024), BF),
            compiler_params=params(),
            name="unpack_a",
        )(places, *a_parts).reshape(width, 1024)
        b1_got, b2_got = after_all((b1_got, b2_got), w_all)
        b1_y = jnp.concatenate([b1_z, b1_got], axis=0)
        b1_got = swap(b1_y, "dp", nd, 1)
        b2_x = jnp.concatenate([b2_y, b2_got], axis=0)
        b2_got = [swap(b2_x, "dp", nd, m) for m in Z_MASKS]

    def unpack_b(b1, b1x, b2, b2x):
        b1, b1x = (v.reshape(2, 2, 4, shard, 2 * fn) for v in (b1, b1x))
        b2, b2x = (v.reshape(4, 2, 2, shard, 640) for v in (b2, b2x))
        piece1 = pl.BlockSpec((2, 2, 1, shard, 2 * fn), lambda z, t: (0, 0, jnp.bitwise_xor(z, t[98] // 2), 0, 0))
        piece2 = pl.BlockSpec((1, 2, 2, shard, 640), lambda z, t: (jnp.bitwise_xor(z, t[98] // 2), 0, 0, 0, 0))
        duo = lambda n: pl.BlockSpec((2, shard, n), lambda z, t: (z, 0, 0))
        wg, wu, wo, wd = pl.pallas_call(
            unpack_b_kernel,
            grid_spec=pltpu.PrefetchScalarGridSpec(
                num_scalar_prefetch=1,
                grid=(4,),
                in_specs=[piece1, piece1, piece2, piece2],
                out_specs=[duo(ff), duo(ff), duo(640), pl.BlockSpec((nd, shard, ff // 4), lambda z, t: (0, 0, z))],
            ),
            out_shape=[jax.ShapeDtypeStruct((nd, shard, ff), BF), jax.ShapeDtypeStruct((nd, shard, ff), BF),
                       jax.ShapeDtypeStruct((nd, shard, 640), BF), jax.ShapeDtypeStruct((nd, shard, ff), BF)],
            compiler_params=params(),
            name="unpack_b",
        )(places, b1, b1x, b2, b2x)
        return wg.reshape(width, ff), wu.reshape(width, ff), wo.reshape(width, 640), wd.reshape(width, ff)

    if not box:
        dslot = slot_table(wsteps, "dp", nd, me_d)
        cslot = slot_table(wsteps, "ctx", nc, me_c)

        def whole(own):
            x = spread(own, wsteps, sizes)
            x = x.reshape((nc, nd) + own.shape)
            return jnp.take(jnp.take(x, cslot, axis=0), dslot, axis=1)

        def join(x):
            return x.transpose(1, 2, 0, 3).reshape(nd * x.shape[2], nc * x.shape[3])

        a = whole(a_own)
        w_all = jnp.concatenate(
            [join(a[..., :qn]), join(a[..., qn : qn + kn]), join(a[..., qn + kn : qn + 2 * kn]),
             a[0, :, :, 240:241].reshape(width, 1), jnp.zeros((width, 63), BF)], axis=1)
        b1 = whole(b1_own)
        b2 = whole(b2_own)
        wg, wu = join(b1[..., :fn]), join(b1[..., fn:])
        wo = jnp.concatenate([join(b2[..., :qn]), b2[0, :, :, qn : qn + 1].reshape(width, 1), jnp.zeros((width, 63), BF)], axis=1)
        wd = join(whole(down_weight)).T
        places = jnp.zeros((99,), jnp.int32)
        tokens_all = [spread(tokens[s], csteps, sizes) for s in range(seqs)]
        seg_all = spread(segments, csteps, sizes)
        tokens_all = [(v[: nc // 2], v[nc // 2 :]) for v in tokens_all]
        cot_got = swap(cotangent[..., blk:], "ctx", nc, last)

    ctx_bits = [b for _, b in csteps]

    def piece_rel(i):
        return sum(b for k, b in enumerate(ctx_bits) if i >> k & 1)

    place = {piece_rel(i): i for i in range(nc)}

    def balanced(all_pieces):
        rel = [all_pieces[place[r]] for r in range(nc)]
        return jnp.stack([jnp.concatenate([rel[r][..., :blk], rel[r ^ last][..., blk:]], axis=-1) for r in range(nc)])

    owner = me_c ^ jnp.arange(nc, dtype=jnp.int32)
    lane = jnp.arange(blk, dtype=jnp.int32)
    index = jnp.concatenate(
        [owner[:, None] * rows + lane[None], (last - owner[:, None]) * rows + blk + lane[None]], axis=1)
    inverse = ROPE_BASE ** (-2.0 * jnp.arange(HALF).astype(F32) / HEAD)
    table = jnp.asarray(pair_table(nc))[me_c].reshape(-1)
    pairs = 2 * nc + 1
    wide_q = SHARE * blk

    saved = []
    for s in range(seqs):
        tok_own, tok_got = tokens_all[s]
        zseg = balanced(seg_all[:, s])
        before = jnp.where(zseg == 0, 0, jnp.where(zseg == 1, jnp.sum(zseg < 1), jnp.sum(zseg < 2)))
        phase = (index - before).astype(F32)[:, None, :] * inverse[None, :, None]
        cos_t, sin_t = jnp.cos(phase), jnp.sin(phase)

        piece = lambda *tail: pl.BlockSpec((1,) + tail, lambda r: (r,) + (0,) * len(tail))
        fixed = lambda *shape: pl.BlockSpec(shape, lambda r: (0,) * len(shape))
        if s:
            tok_own = after(tok_own, prob)
        if s and box:
            tok_own = after(tok_own, b1_x)
        half = lambda at: pl.BlockSpec((1, width, blk), at)
        near = half(lambda r: (r // 2, 0, 0))
        opposite = half(lambda r: ((nc - 1 - r) // 2, 0, 1))
        h1, k_t, v_t, q_t, x_own = pl.pallas_call(
            pre_kernel,
            grid=(nc,),
            in_specs=[near, near, opposite, opposite, fixed(width, 1024), piece(HALF, rows), piece(HALF, rows), piece(1, rows)],
            out_specs=[piece(width, rows),
                       pl.BlockSpec((GROUPS, 1, AUG, rows), lambda r: (0, r, 0, 0)),
                       pl.BlockSpec((GROUPS, 1, AUG, rows), lambda r: (0, r, 0, 0)),
                       fixed(GROUPS, 2, AUG, wide_q), fixed(width, rows)],
            out_shape=[jax.ShapeDtypeStruct((nc, width, rows), BF),
                       jax.ShapeDtypeStruct((GROUPS, nc, AUG, rows), BF),
                       jax.ShapeDtypeStruct((GROUPS, nc, AUG, rows), BF),
                       jax.ShapeDtypeStruct((GROUPS, 2, AUG, wide_q), BF),
                       jax.ShapeDtypeStruct((width, rows), BF)],
            compiler_params=params(),
            cost_estimate=pl.CostEstimate(flops=4_500_000_000, bytes_accessed=10_000_000, transcendentals=0),
            name="pre",
        )(tok_own, tok_got, tok_own, tok_got, w_all, cos_t, sin_t, zseg[:, None, :])

        if box and s == 0:
            tok1_y = jnp.concatenate([tokens[1][None], after(tok1_got, q_t)], axis=0)
            tokens_all.append((tok1_y, swap(tok1_y, "ctx", nc, 1)))
        if box and s == 1:
            b2_z = jnp.concatenate([b2_x] + list(after_all(b2_got, q_t)), axis=0)
            b2_far = swap(b2_z, "ctx", nc, 1)
            q_t = after(q_t, b2_z)
        att = lambda *tail: pl.BlockSpec((1,) + tail, lambda g, t: (g,) + (0,) * len(tail))
        prob, o_t, inv_l = pl.pallas_call(
            functools.partial(attend_kernel, pairs),
            grid_spec=pltpu.PrefetchScalarGridSpec(
                num_scalar_prefetch=1,
                grid=(GROUPS,),
                in_specs=[att(2, AUG, wide_q), att(nc, AUG, rows), att(nc, AUG, rows)],
                out_specs=[att(pairs, blk, wide_q), att(2, HEAD, wide_q), att(2, 1, wide_q)],
                scratch_shapes=[pltpu.VMEM((pairs, blk, wide_q), F32), pltpu.VMEM((2, 8, wide_q), F32),
                                pltpu.VMEM((2, AUG, wide_q), F32)],
            ),
            out_shape=[jax.ShapeDtypeStruct((GROUPS, pairs, blk, wide_q), BF),
                       jax.ShapeDtypeStruct((GROUPS, 2, HEAD, wide_q), BF),
                       jax.ShapeDtypeStruct((GROUPS, 2, 1, wide_q), F32)],
            compiler_params=params(),
            cost_estimate=pl.CostEstimate(flops=12_000_000_000, bytes_accessed=12_000_000, transcendentals=0),
            name="attend",
        )(table, q_t, k_t, v_t)
        if box and s == 0:
            prob, o_t, inv_l, b1_got = lax.optimization_barrier((prob, o_t, inv_l, b1_got))
            b1_x = jnp.concatenate([b1_y, b1_got], axis=0)
            b1_far = swap(b1_x, "ctx", nc, 1)
            cot_got = swap(after(cotangent[..., blk:], prob), "ctx", nc, last)
        if box and s == 1:
            b1_far, b2_far, cot_got = after_all((b1_far, b2_far, cot_got), prob)
            wg, wu, wo, wd = unpack_b(b1_x, b1_far, b2_z, b2_far)
        saved.append((x_own, cos_t, sin_t, h1, k_t, v_t, q_t, prob, o_t, inv_l))

    total = seqs * rows
    steps = 2
    fstep = ff // steps
    fixed = lambda *shape: pl.BlockSpec(shape, lambda f, t: (0,) * len(shape))
    if box:
        grad_specs = [fixed(16, shard, 2 * fn)] * 2 + [fixed(16, shard, 640)] * 2
        grad_shapes = [jax.ShapeDtypeStruct((16, shard, 2 * fn), BF)] * 2 + [jax.ShapeDtypeStruct((16, shard, 640), BF)] * 2
    else:
        grad_specs = [pl.BlockSpec((width, fstep), lambda f, t: (0, f))] * 2
        grad_specs += [pl.BlockSpec((width, fstep), lambda f, t: (0, f)), fixed(width, 640)]
        grad_shapes = [jax.ShapeDtypeStruct((width, ff), BF)] * 3 + [jax.ShapeDtypeStruct((width, 640), BF)]
    out_near, out_far, d_middle, do_t, *grads = pl.pallas_call(
        functools.partial(middle_kernel, box, nd, nc, seqs),
        grid_spec=pltpu.PrefetchScalarGridSpec(
            num_scalar_prefetch=1,
            grid=(steps,),
            in_specs=[fixed(width, rows), fixed(GROUPS, 2, HEAD, wide_q)] * seqs
            + [fixed(seqs, width, rows), fixed(seqs, width, blk)] + [pl.BlockSpec((width, fstep), lambda f, t: (0, f))] * 3 + [fixed(width, 640)],
            out_specs=[fixed(seqs, width, blk), fixed(seqs, width, blk), fixed(seqs, width, rows), fixed(seqs, GROUPS, 2, HEAD, wide_q)] + grad_specs,
            scratch_shapes=[pltpu.VMEM((qd, total), BF), pltpu.VMEM((width, total), F32), pltpu.VMEM((width, total), BF),
                            pltpu.VMEM((width, total), BF), pltpu.VMEM((width, total), F32), pltpu.VMEM((width, total), F32)],
        ),
        out_shape=[jax.ShapeDtypeStruct((seqs, width, blk), BF), jax.ShapeDtypeStruct((seqs, width, blk), BF),
                   jax.ShapeDtypeStruct((seqs, width, rows), F32),
                   jax.ShapeDtypeStruct((seqs, GROUPS, 2, HEAD, wide_q), BF)] + grad_shapes,
        compiler_params=params(),
        cost_estimate=pl.CostEstimate(flops=36_000_000_000, bytes_accessed=20_000_000, transcendentals=0),
        name="middle",
    )(places, *[v[k] for v in saved for k in (0, 8)], cotangent, cot_got, wg, wu, wd, wo)

    def settle(pieces):
        x = jnp.take(jnp.take(pieces, jnp.argsort(dslot), axis=0), jnp.argsort(cslot), axis=1)
        x = jnp.swapaxes(x, 0, 1).reshape((nc * nd,) + pieces.shape[2:])
        return gather_up(x, wsteps, sizes).astype(F32)

    def cut(g):
        r, c = g.shape
        return g.reshape(nd, r // nd, nc, c // nc).transpose(0, 2, 1, 3)

    def repeat(column):
        return jnp.broadcast_to(column.reshape(nd, 1, shard, 1), (nd, nc, shard, 1))

    if box:
        b1_got = swap(grads[1], "ctx", nc, 1)
        b2_got = swap(grads[3], "ctx", nc, 1)
    else:
        gate_sum, up_sum, down_sum = settle(cut(grads[0])), settle(cut(grads[1])), settle(cut(grads[2].T))
        b2_sum = settle(jnp.concatenate([cut(grads[3][:, :qd]), repeat(grads[3][:, qd])], axis=-1))
        out_sum, gain2_sum = b2_sum[:, :qn], b2_sum[:, qn]

    out_away = swap(out_far, "ctx", nc, last)
    half = nc // 2
    backs, dkv_owns = [], []
    for s in range(seqs):
        _, cos_t, sin_t, h1, k_t, v_t, q_t, prob, o_t, inv_l = saved[s]
        if s:
            q_t = after(q_t, backs[0][0], *((b1 + b2) if box else ()))
        att = lambda *tail: pl.BlockSpec((1,) + tail, lambda g, t: (g,) + (0,) * len(tail))
        fixed = lambda *shape: pl.BlockSpec(shape, lambda g, t: (0,) * len(shape))
        pair_of = pl.BlockSpec((1, 1, 2, HEAD, wide_q), lambda g, t: (s, g, 0, 0, 0))
        count = 1 if box and s == 0 else half
        kv_out = pl.BlockSpec((count, 2, 1, HEAD, rows), lambda g, t: (0, 0, g, 0, 0))
        dq_t, *kvs = pl.pallas_call(
            functools.partial(attend_back_kernel, pairs, tuple(place[r] for r in range(nc))),
            grid_spec=pltpu.PrefetchScalarGridSpec(
                num_scalar_prefetch=1,
                grid=(GROUPS,),
                in_specs=[att(pairs, blk, wide_q), att(2, AUG, wide_q), att(nc, AUG, rows), att(nc, AUG, rows),
                          att(2, HEAD, wide_q), pair_of, att(2, 1, wide_q), fixed(nc, HALF, rows), fixed(nc, HALF, rows)],
                out_specs=[att(SHARE, HEAD, rows)] + [kv_out] * (nc // count),
                scratch_shapes=[pltpu.VMEM((2, AUG, wide_q), BF), pltpu.VMEM((2 * nc, HEAD, blk), F32),
                                pltpu.VMEM((2 * nc, HEAD, blk), F32), pltpu.VMEM((2, HEAD, wide_q), F32)],
            ),
            out_shape=[jax.ShapeDtypeStruct((GROUPS, SHARE, HEAD, rows), BF)]
            + [jax.ShapeDtypeStruct((count, 2, GROUPS, HEAD, rows), BF)] * (nc // count),
            compiler_params=params(),
            cost_estimate=pl.CostEstimate(flops=20_000_000_000, bytes_accessed=12_000_000, transcendentals=0),
            name="attend_back",
        )(table, prob, q_t, k_t, v_t, o_t, do_t, inv_l, cos_t, sin_t)
        if box and s == 0:
            dq_t, b1_got, b2_got, out_away, *kvs = lax.optimization_barrier((dq_t, b1_got, b2_got, out_away, *kvs))
        if box and s == 1:
            dq_t, b1_got, z_got, dkv0, *kvs = lax.optimization_barrier((dq_t, b1_got, z_got, dkv0, *kvs))
            dkv_owns[0] = [dkv_owns[0][0]] + list(dkv0)
        kvs = [v.reshape(count, 2 * kvd, rows) for v in kvs]
        backs.append([dq_t.reshape(qd, rows), h1] + kvs)
        if box and s == 0:
            dkv0 = [swap(v, "ctx", nc, piece_rel(k)) for k, v in enumerate(kvs) if k]
            dkv_owns.append(kvs[:1])
            b1, b2 = add(grads[0], b1_got), add(grads[2], b2_got)
            b1_got = swap(b1[1], "dp", nd, 1)
            z_got = swap(b2[1][:4], "dp", nd, 4)
        else:
            dkv_got = swap(kvs[1], "ctx", nc, csteps[-1][1])
            if box:
                b1 = add(b1[0], b1_got)
                b1_got = swap(b1[1], "ctx", nc, 2)
                b2_parts = [b2[0][:4], z_got] + [swap(p, "dp", nd, m) for p, m in ((b2[0][4:], 2), (b2[1][4:], 6))]
            low, high = add(kvs[0], dkv_got)
            dkv_owns.append([low, swap(high, "ctx", nc, csteps[0][1])])

    def token(s, dqr_t):
        return pl.pallas_call(
            token_kernel,
            grid=(1,),
            in_specs=[pl.BlockSpec((1, 2 * kvd, rows), lambda i: (0, 0, 0))] * len(dkv_owns[s])
            + [pl.BlockSpec((qd, rows), lambda i: (0, 0)), pl.BlockSpec((width, 1024), lambda i: (0, 0)),
               pl.BlockSpec((width, rows), lambda i: (0, 0)), pl.BlockSpec((1, width, rows), lambda i: (s, 0, 0))],
            out_specs=[pl.BlockSpec((width, blk), lambda i: (0, 0))] * 2,
            out_shape=[jax.ShapeDtypeStruct((width, blk), BF)] * 2,
            compiler_params=params(),
            cost_estimate=pl.CostEstimate(flops=4_000_000_000, bytes_accessed=5_000_000, transcendentals=0),
            name="token",
        )(*dkv_owns[s], dqr_t, w_all, saved[s][0], d_middle)

    near0, far0 = token(0, after(backs[0][0], backs[1][0], dkv_owns[1][0], *((b1[0],) if box else ())))
    away0 = swap(far0, "ctx", nc, last)
    spot = [place[r] for r in range(nc)]
    hid_of = pl.BlockSpec((1, width, rows), lambda r, t: (t[99 + r], 0, 0))
    fixed = lambda *shape: pl.BlockSpec(shape, lambda r, t: (0,) * len(shape))
    if box:
        a_specs = [fixed(16, shard, 256)] * 2
        a_shapes = [jax.ShapeDtypeStruct((16, shard, 256), BF)] * 2
    else:
        a_specs, a_shapes = [fixed(width, 1024)], [jax.ShapeDtypeStruct((width, 1024), BF)]
    ops = [v for back in backs for v in back]
    ops[0] = after(ops[0], near0)
    places = jnp.concatenate([places, jnp.asarray([spot.index(i) for i in range(nc)], jnp.int32)])
    a_out = pl.pallas_call(
        functools.partial(post_kernel, box, nd, nc, tuple(len(v) for v in backs)),
        grid_spec=pltpu.PrefetchScalarGridSpec(
            num_scalar_prefetch=1,
            grid=(nc,),
            in_specs=[sp for back in backs for sp in [fixed(qd, rows), hid_of] + [fixed(*v.shape) for v in back[2:]]] + [fixed(width, 1024)],
            out_specs=a_specs,
            scratch_shapes=[pltpu.VMEM((width, 1024), F32)],
        ),
        out_shape=a_shapes,
        compiler_params=params(),
        cost_estimate=pl.CostEstimate(flops=15_000_000_000, bytes_accessed=10_000_000, transcendentals=0),
        name="post",
    )(places, *ops, w_all)

    if box:
        *a_out, b1_got, b2_parts, away0 = lax.optimization_barrier((*a_out, b1_got, b2_parts, away0))
        a_got = swap(a_out[1], "ctx", nc, 1)
        a_got, dkv_owns[1] = lax.optimization_barrier((a_got, dkv_owns[1]))
        total_of = lambda parts: sum(p.astype(F32) for p in parts)
        b2 = total_of(b2_parts).astype(BF)
        b2_got = swap(b2[2:], "dp", nd, 1)
        b1 = add(b1[0], b1_got)
        a = add(a_out[0], a_got)
        a_got = swap(a[1], "dp", nd, 1)
        b1_parts = [b1[0][0]] + [swap(p, "dp", nd, m) for p, m in zip((b1[0][1], b1[1][0], b1[1][1]), Z_MASKS)]
    mine, away = token(1, after(backs[1][0], *((a[0], b2[0]) if box else ())))
    if box:
        mine, away, a_got, b1_parts, b2_got = lax.optimization_barrier((mine, away, a_got, b1_parts, b2_got))
    token_near, token_away = [near0, mine], [away0, swap(away, "ctx", nc, last)]
    if box:
        a = add(a[0], a_got)
        b2 = (b2[:2].astype(F32) + b2_got.astype(F32)).astype(BF)
        b2_got = swap(b2[1], "ctx", nc, 2)
        a = fold(*a, "ctx", 2, sizes)
        a, token_away, b2_got = lax.optimization_barrier((a, token_away, b2_got))
        b1_sum = total_of(b1_parts)
        b2_sum = b2[0].astype(F32) + b2_got.astype(F32)
        gate_sum, up_sum = b1_sum[:, :fn], b1_sum[:, fn:]
        out_sum, gain2_sum, down_sum = b2_sum[:, :qn], b2_sum[:, qn], unfold_down(b2_sum[:, 256:]).T

    if box:
        a_sum = fold_z(*a, sizes)
    else:
        a = a_out[0]
        a_sum = settle(jnp.concatenate(
            [cut(a[:, :qd]), cut(a[:, qd : qd + kvd]), cut(a[:, qd + kvd : qd + 2 * kvd]), repeat(a[:, 960])], axis=-1))

    def home(mine, away):
        return jnp.swapaxes(jnp.concatenate([mine, away], axis=-1), 1, 2)

    return (
        home(out_near, out_away),
        home(jnp.stack(token_near), jnp.stack(token_away)),
        a_sum[:, 2 * kn + qn],
        a_sum[:, :qn],
        a_sum[:, qn : qn + kn],
        a_sum[:, qn + kn : qn + 2 * kn],
        out_sum,
        gain2_sum,
        gate_sum,
        up_sum,
        down_sum,
    )


def pair_table(nc):
    out = []
    for me in range(nc):
        spots = {}
        for r in range(nc):
            d = me ^ r
            spots[2 * d] = 2 * r
            spots[2 * (nc - 1 - d) + 1] = 2 * r + 1
        mine = [2 * me, 2 * (nc - 1 - me) + 1]
        rows = [(i, spots[mine[i]]) for i in range(2)]
        rows += [(i, spots[k]) for i in range(2) for k in range(mine[i])]
        out.append(rows)
    return np.array(out, np.int32)


def turn(x, cos, sin, heads, sign):
    parts = []
    for h in range(heads):
        lo, hi = x[h * HEAD : h * HEAD + HALF], x[h * HEAD + HALF : (h + 1) * HEAD]
        parts += [lo * cos - sign * hi * sin, hi * cos + sign * lo * sin]
    return jnp.concatenate(parts, axis=0)


def unpack_a_kernel(places, own_ref, other_ref, w_ref):
    nd = w_ref.shape[0]
    nc = 4
    qn, kn = 144, 48
    qd, kvd = qn * nc, kn * nc

    def write(cores):
        for d in range(nd):
            for c in range(nc):
                p = cores[c % 2][places[d * nc + c]].astype(F32)
                if c == 0:
                    cols = [[], [], []]
                    gain = p[:, 240:256]
                cols[0].append(p[:, :qn])
                cols[1].append(p[:, qn : qn + kn])
                cols[2].append(p[:, qn + kn : qn + 2 * kn])
            row = cols[0] + cols[1] + cols[2] + [gain, jnp.zeros((p.shape[0], 48), F32)]
            w_ref[d] = jnp.concatenate(row, axis=1).astype(BF)

    core = places[96]
    pl.when(core == 0)(lambda: write((own_ref, other_ref)))
    pl.when(core == 1)(lambda: write((other_ref, own_ref)))


def unpack_b_kernel(places, b1_ref, b1x_ref, b2_ref, b2x_ref, g_ref, u_ref, o_ref, w_ref):
    nc = 4
    fn = b1_ref.shape[-1] // 2
    shard = b1_ref.shape[-2]
    me_y, me_x = places[97] // 2, places[98] % 2

    def write(one, two):
        for x in range(2):
            at_x = jnp.bitwise_xor(me_x, x)
            outs = []
            for c in range(nc):
                y = jnp.bitwise_xor(me_y, c // 2)
                p = one[c % 2][at_x, y, 0]
                g_ref[x, :, c * fn : (c + 1) * fn] = p[:, :fn]
                u_ref[x, :, c * fn : (c + 1) * fn] = p[:, fn:]
                p = two[c % 2][0, at_x, y].astype(F32)
                outs.append(p[:, :144])
                for i in range(2):
                    w_ref[2 * c + i, :, x * 192 : (x + 1) * 192] = p[:, 256 + 192 * i : 448 + 192 * i].astype(BF)
                if c == 0:
                    gain = p[:, 144:160]
            o_ref[x] = jnp.concatenate(outs + [gain, jnp.zeros((shard, 48), F32)], axis=1).astype(BF)

    core = places[96]
    pl.when(core == 0)(lambda: write((b1_ref, b1x_ref), (b2_ref, b2x_ref)))
    pl.when(core == 1)(lambda: write((b1x_ref, b1_ref), (b2x_ref, b2_ref)))


def pre_kernel(own_ref, got_ref, own2_ref, got2_ref, w_ref, cos_ref, sin_ref, seg_ref, h_ref, k_ref, v_ref, q_ref, x_ref):
    mine = lax.rem(pl.program_id(0), 2) == 0
    x = jnp.concatenate([jnp.where(mine, own_ref[0].astype(F32), got_ref[0].astype(F32)),
                         jnp.where(mine, got2_ref[0].astype(F32), own2_ref[0].astype(F32))], axis=1)
    inv = lax.rsqrt(jnp.mean(x * x, axis=0, keepdims=True) + EPS)
    qd, kvd = HEADS * HEAD, GROUPS * HEAD
    gain = w_ref[:, qd + 2 * kvd : qd + 2 * kvd + 1].astype(F32)
    h = ((x * inv) * gain).astype(BF)
    h_ref[0] = h
    cos, sin, seg = cos_ref[0], sin_ref[0], seg_ref[0]
    rows = x.shape[1]
    blk = rows // 2
    kv = dot(w_ref[:, qd : qd + 2 * kvd], h, TN)
    keys = turn(kv[:kvd], cos, sin, GROUPS, 1.0).astype(BF)
    values = kv[kvd:].astype(BF)
    row = lax.broadcasted_iota(jnp.int32, (AUG - HEAD, rows), 0)
    other = jnp.where((row < 3) & (row != seg), -1e30, 0.0).astype(BF)
    ones = (row < 3).astype(BF)
    for g in range(GROUPS):
        k_ref[g, 0, :HEAD] = keys[g * HEAD : (g + 1) * HEAD]
        k_ref[g, 0, HEAD:] = other
        v_ref[g, 0, :HEAD] = values[g * HEAD : (g + 1) * HEAD]
        v_ref[g, 0, HEAD:] = ones

    @pl.when(pl.program_id(0) == 0)
    def _():
        q = turn(dot(w_ref[:, :qd], h, TN), cos, sin, HEADS, 1.0).astype(BF) * (1.0 / math.sqrt(HEAD))
        x_ref[...] = x.astype(BF)
        same = (row == seg).astype(BF)
        for g in range(GROUPS):
            for b in range(2):
                for j in range(SHARE):
                    n = g * SHARE + j
                    q_ref[g, b, :HEAD, j * blk : (j + 1) * blk] = q[n * HEAD : (n + 1) * HEAD, b * blk : (b + 1) * blk]
                    q_ref[g, b, HEAD:, j * blk : (j + 1) * blk] = same[:, b * blk : (b + 1) * blk]


def by_core(core, refs, write):
    pairs = [refs[i : i + 2] for i in range(0, len(refs), 2)]
    pl.when(core == 0)(lambda: write(*pairs))
    pl.when(core == 1)(lambda: write(*[p[::-1] for p in pairs]))


def middle_kernel(box, nd, nc, seqs, places, *refs):
    xs, refs = refs[: 2 * seqs], refs[2 * seqs :]
    cot_ref, got_ref, wg_ref, wu_ref, wd_ref, wo_ref, near_ref, far_ref, dm_ref, do_ref, *rest = refs
    grads, (att_ref, mid_ref, h_ref, cots_ref, acc_ref, dh_ref) = rest[:4], rest[4:]
    f = pl.program_id(0)
    blk = got_ref.shape[2]
    rows = 2 * blk
    qd, width = HEADS * HEAD, cot_ref.shape[1]
    shard = width // nd
    fn = wg_ref.shape[1]
    steps = 2
    part_fn = fn * steps // nc

    def norm():
        m = mid_ref[...]
        inv = lax.rsqrt(jnp.mean(m * m, axis=0, keepdims=True) + EPS)
        return m, inv, m * inv

    def gain_column():
        return wo_ref[:, qd : qd + 1].astype(F32)

    def of(s):
        return slice(s * rows, (s + 1) * rows)

    def blocks():
        for s in range(seqs):
            for g in range(GROUPS):
                for b in range(2):
                    for j in range(SHARE):
                        n = g * SHARE + j
                        yield (s, g, b, slice(None), slice(j * blk, (j + 1) * blk)), (
                            slice(n * HEAD, (n + 1) * HEAD), slice(s * rows + b * blk, s * rows + (b + 1) * blk))

    @pl.when(f == 0)
    def _():
        for there, here in blocks():
            att_ref[here] = xs[2 * there[0] + 1][there[1:]]
        branch = dot(wo_ref[:, :qd], att_ref[...], TN)
        for s in range(seqs):
            mid_ref[:, of(s)] = xs[2 * s][...].astype(F32) + branch[:, of(s)]
            cots_ref[:, s * rows : s * rows + blk] = cot_ref[s, :, :blk]
            cots_ref[:, s * rows + blk : (s + 1) * rows] = got_ref[s]
        _, _, n2 = norm()
        h_ref[...] = (n2 * gain_column()).astype(BF)

    h = h_ref[...]
    cot = cots_ref[...]
    gate = dot(wg_ref[...], h, TN)
    up = dot(wu_ref[...], h, TN)
    sig = jax.nn.sigmoid(gate)
    act = gate * sig
    inner = (act * up).astype(BF)
    part = dot(wd_ref[...], inner, NN)
    d_inner = dot(wd_ref[...], cot, TN)
    d_gate = (d_inner * up * (sig + act * (1.0 - sig))).astype(BF)
    d_up = (d_inner * act).astype(BF)
    d_part = dot(wg_ref[...], d_gate, NN) + dot(wu_ref[...], d_up, NN)

    @pl.when(f == 0)
    def _():
        acc_ref[...] = part
        dh_ref[...] = d_part

    @pl.when(f > 0)
    def _():
        acc_ref[...] += part
        dh_ref[...] += d_part

    grad_gate = dot(h, d_gate, NT)
    grad_up = dot(h, d_up, NT)
    grad_down = dot(cot, inner, NT)
    if box:
        cols = width // nc
        per = fn * steps // nd

        def pack(b1s, b2s):
            for k in range(nc // steps):
                c = f * (nc // steps) + k
                lanes = slice(k * part_fn, (k + 1) * part_fn)
                for d in range(nd):
                    part_rows = slice(d * shard, (d + 1) * shard)
                    at = places[d * nc + c]
                    b1s[k % 2][at, :, :part_fn] = grad_gate[part_rows, lanes].astype(BF)
                    b1s[k % 2][at, :, part_fn:] = grad_up[part_rows, lanes].astype(BF)
            for i in range(fn // per):
                for c in range(nc):
                    p = fold_down(grad_down[c * cols : (c + 1) * cols, i * per : (i + 1) * per]).astype(BF)
                    b2s[c % 2][places[32 + (f * (fn // per) + i) * nc + c], :, 256:640] = p

        by_core(places[96], grads, pack)
    else:
        grads[0][...] = grad_gate.astype(BF)
        grads[1][...] = grad_up.astype(BF)
        grads[2][...] = grad_down.astype(BF)

    @pl.when(f == pl.num_programs(0) - 1)
    def _():
        m, inv, n2 = norm()
        out = (m + acc_ref[...]).astype(BF)
        d_h2 = dh_ref[...]
        e2 = d_h2 * gain_column()
        d_middle = cots_ref[...].astype(F32) + inv * (e2 - n2 * jnp.mean(e2 * n2, axis=0, keepdims=True))
        for s in range(seqs):
            near_ref[s] = out[:, s * rows : s * rows + blk]
            far_ref[s] = out[:, s * rows + blk : (s + 1) * rows]
            dm_ref[s] = d_middle[:, of(s)]
        branch = d_middle.astype(BF)
        d_att = dot(wo_ref[:, :qd], branch, NN).astype(BF)
        for there, here in blocks():
            do_ref[there] = d_att[here]
        grad_out = dot(att_ref[...], branch, NT)
        gain = jnp.broadcast_to(jnp.sum(d_h2 * n2, axis=1, keepdims=True), (width, 128))
        if box:
            def pack_out(b1s, b2s):
                for d in range(nd):
                    part_rows = slice(d * shard, (d + 1) * shard)
                    for c in range(nc):
                        p = jnp.concatenate([grad_out[part_rows, c * cols : (c + 1) * cols], gain[part_rows, :112]], axis=1)
                        b2s[c % 2][places[32 + d * nc + c], :, :256] = p.astype(BF)

            by_core(places[96], grads, pack_out)
        else:
            grads[3][...] = jnp.concatenate([grad_out, gain[:, :64]], axis=1).astype(BF)


def post_kernel(box, nd, nc, counts, places, *refs):
    seqs = []
    for n in counts:
        seqs.append(refs[:n])
        refs = refs[n:]
    w_ref, outs, acc_ref = refs[0], refs[1:-1], refs[-1]
    kvd, qd = GROUPS * HEAD, HEADS * HEAD
    r = pl.program_id(0)

    @pl.when(r == 0)
    def _():
        acc_ref[...] = jnp.zeros_like(acc_ref)
        acc_ref[:, :qd] = sum(dot(h_ref[0], dq_ref[...], NT) for dq_ref, h_ref, *_ in seqs)

    for k in range(nc):
        @pl.when(r == k)
        def _():
            terms = []
            for _, h_ref, *kvs in seqs:
                n = nc // len(kvs)
                terms.append(dot(h_ref[0], kvs[k // n][k % n], NT))
            acc_ref[:, qd : qd + 2 * kvd] += sum(terms)

    @pl.when(r == nc - 1)
    def _():
        g = acc_ref[...]
        w = w_ref[...].astype(F32)
        used = qd + 2 * kvd
        gain = jnp.sum(g[:, :used] * w[:, :used], axis=1, keepdims=True) / w[:, used : used + 1]
        if not box:
            outs[0][...] = jnp.concatenate([g[:, :used], jnp.broadcast_to(gain, (g.shape[0], 64))], axis=1).astype(BF)
            return
        shard = g.shape[0] // nd
        gain = jnp.broadcast_to(gain, (g.shape[0], 16))
        qn, kn = qd // nc, kvd // nc

        def pack(both):
            for d in range(nd):
                r = slice(d * shard, (d + 1) * shard)
                for c in range(nc):
                    p = jnp.concatenate(
                        [g[r, c * qn : (c + 1) * qn], g[r, qd + c * kn : qd + (c + 1) * kn],
                         g[r, qd + kvd + c * kn : qd + kvd + (c + 1) * kn], gain[r]], axis=1)
                    both[c % 2][places[d * nc + c]] = p.astype(BF)

        by_core(places[96], outs, pack)


def token_kernel(*refs):
    *kvs, dq_ref, w_ref, x_ref, dm_ref, near_ref, far_ref = refs
    qd, kvd = HEADS * HEAD, GROUPS * HEAD
    x = x_ref[...].astype(F32)
    inv = lax.rsqrt(jnp.mean(x * x, axis=0, keepdims=True) + EPS)
    n1 = x * inv
    dkv = sum(v[0].astype(F32) for v in kvs).astype(BF)
    d_h1 = dot(w_ref[:, :qd], dq_ref[...], NN) + dot(w_ref[:, qd : qd + 2 * kvd], dkv, NN)
    e1 = d_h1 * w_ref[:, qd + 2 * kvd : qd + 2 * kvd + 1].astype(F32)
    out = (dm_ref[0] + inv * (e1 - n1 * jnp.mean(e1 * n1, axis=0, keepdims=True))).astype(BF)
    blk = near_ref.shape[1]
    near_ref[...] = out[:, :blk]
    far_ref[...] = out[:, blk:]


def key_block(ref, loc, blk, rows=None):
    r, half = loc // 2, loc % 2
    lanes = pl.ds(pl.multiple_of(half * blk, blk), blk)
    if rows is None:
        return ref[0, r, :, lanes]
    return ref[0, r, :rows, lanes]


def attend_kernel(pairs, table, q_ref, k_ref, v_ref, p_ref, o_ref, l_ref, s_ref, m_ref, acc_ref):
    wide = q_ref.shape[-1]
    blk = wide // SHARE

    def score(t, diagonal):
        qb, loc = table[2 * t], table[2 * t + 1]
        s = dot(key_block(k_ref, loc, blk), q_ref[0, qb], TN)
        if diagonal:
            k_at = lax.broadcasted_iota(jnp.int32, (blk, wide), 0)
            q_at = lax.broadcasted_iota(jnp.int32, (blk, wide), 1) % blk
            s = jnp.where(k_at <= q_at, s, -1e30)
        s_ref[t] = s
        top = jnp.max(s.reshape(blk // 8, 8, wide), axis=0)
        if diagonal:
            m_ref[qb] = top
        else:
            m_ref[qb] = jnp.maximum(m_ref[qb], top)

    for t in range(2):
        score(t, True)
    lax.fori_loop(2, pairs, lambda t, c: (score(t, False), c)[1], 0, unroll=pairs - 2)
    for b in range(2):
        m_ref[b] = jnp.broadcast_to(jnp.max(m_ref[b], axis=0, keepdims=True), m_ref.shape[1:])
    acc_ref[...] = jnp.zeros_like(acc_ref)

    def weigh(t, c):
        qb, loc = table[2 * t], table[2 * t + 1]
        p = jnp.exp(s_ref[t] - m_ref[qb, 0:1]).astype(BF)
        p_ref[0, t] = p
        acc_ref[qb] += dot(key_block(v_ref, loc, blk), p, NN)
        return c

    lax.fori_loop(0, pairs, weigh, 0, unroll=pairs)
    for b in range(2):
        inv = 1.0 / acc_ref[b, HEAD : HEAD + 1]
        l_ref[0, b] = inv
        o_ref[0, b] = (acc_ref[b, :HEAD] * inv).astype(BF)


def attend_back_kernel(pairs, order, table, p_ref, q_ref, k_ref, v_ref, o_ref, do_ref, l_ref, cos_ref, sin_ref,
                       dq_ref, *rest):
    *outs, da_ref, dka_ref, dva_ref, dqa_ref = rest
    wide = q_ref.shape[-1]
    blk = wide // SHARE
    row = lax.broadcasted_iota(jnp.int32, (AUG - HEAD, wide), 0)
    for b in range(2):
        d = (do_ref[0, 0, b].astype(F32) * l_ref[0, b]).astype(BF)
        delta = -jnp.sum(d.astype(F32) * o_ref[0, b].astype(F32), axis=0, keepdims=True)
        hi = delta.astype(BF).astype(F32)
        mid = (delta - hi).astype(BF).astype(F32)
        low = delta - hi - mid
        da_ref[b, :HEAD] = d
        da_ref[b, HEAD:] = jnp.where(row == 0, hi, jnp.where(row == 1, mid, jnp.where(row == 2, low, 0.0))).astype(BF)
    dka_ref[...] = jnp.zeros_like(dka_ref)
    dva_ref[...] = jnp.zeros_like(dva_ref)
    dqa_ref[...] = jnp.zeros_like(dqa_ref)

    def step(t, c):
        qb, loc = table[2 * t], table[2 * t + 1]
        p = p_ref[0, t]
        dp = dot(key_block(v_ref, loc, blk), da_ref[qb], TN)
        ds = (p.astype(F32) * dp).astype(BF)
        dqa_ref[qb] += dot(key_block(k_ref, loc, blk, HEAD), ds, NN)
        dka_ref[loc] += dot(q_ref[0, qb, :HEAD], ds, NT)
        dva_ref[loc] += dot(da_ref[qb, :HEAD], p, NT)
        return c

    lax.fori_loop(0, pairs, step, 0, unroll=pairs)
    scale = 1.0 / math.sqrt(HEAD)
    for b in range(2):
        lanes = slice(b * blk, (b + 1) * blk)
        cos, sin = cos_ref[0, :, lanes] * scale, sin_ref[0, :, lanes] * scale
        for j in range(SHARE):
            dq_ref[0, j, :, lanes] = turn(dqa_ref[b, :, j * blk : (j + 1) * blk], cos, sin, 1, -1.0).astype(BF)
    n = len(order) // len(outs)
    for r, at in enumerate(order):
        out_ref = outs[at // n]
        for b in range(2):
            lanes = slice(b * blk, (b + 1) * blk)
            cos, sin = cos_ref[r, :, lanes], sin_ref[r, :, lanes]
            out_ref[at % n, 0, 0, :, lanes] = turn(dka_ref[2 * r + b], cos, sin, 1, -1.0).astype(BF)
            out_ref[at % n, 1, 0, :, lanes] = dva_ref[2 * r + b].astype(BF)


def solution(mesh):
    sizes = {name: mesh.shape[name] for name in ("dp", "ctx")}
    rows = P("dp", "ctx", None)
    grid = P("dp", "ctx")
    line = P("dp")
    return jax.shard_map(
        functools.partial(per_device, sizes),
        mesh=mesh,
        in_specs=(rows, grid, line, grid, grid, grid, grid, line, grid, grid, grid, rows),
        out_specs=(rows, rows, line, grid, grid, grid, grid, line, grid, grid, grid),
        check_vma=False,
    )
```

```python
import functools
import math

import jax
import jax.numpy as jnp
import numpy as np
from jax import lax
from jax.experimental import pallas as pl
from jax.experimental.pallas import tpu as pltpu
from jax.sharding import PartitionSpec as P

HEADS = 9
GROUPS = 3
SHARE = HEADS // GROUPS
HEAD = 64
HALF = HEAD // 2
AUG = HEAD + 16
EPS = 1e-05
ROPE_BASE = 100000.0
VMEM = 56 << 20
BF = jnp.bfloat16
F32 = jnp.float32


def params(semantics=None):
    return pltpu.CompilerParams(vmem_limit_bytes=VMEM, dimension_semantics=semantics)


def dot(a, b, dims):
    return lax.dot_general(a, b, (dims, ((), ())), preferred_element_type=F32)


NN = ((1,), (0,))
NT = ((1,), (1,))
TN = ((0,), (0,))


def swap(x, axis, size, mask):
    return lax.ppermute(x, axis, [(i, i ^ mask) for i in range(size)])


def bits_of(size):
    return [1 << k for k in range(size.bit_length() - 1)]


def spread(x, steps, sizes):
    x = x[None]
    for axis, bit in steps:
        x = jnp.concatenate([x, swap(x, axis, sizes[axis], bit)], axis=0)
    return x


def gather_up(x, steps, sizes):
    for axis, bit in reversed(steps):
        half = x.shape[0] // 2
        other = swap(x[half:], axis, sizes[axis], bit)
        x = (x[:half].astype(F32) + other.astype(F32)).astype(x.dtype)
    return x[0]


def slot_table(steps, axis, size, me):
    order = [bit for a, bit in steps if a == axis]
    rel = jnp.arange(size, dtype=jnp.int32) ^ me
    place = jnp.zeros_like(rel)
    for k, bit in enumerate(order):
        place = place | jnp.where((rel & bit) != 0, 1 << k, 0)
    return place


Z_MASKS = (2, 4, 6)


def stack_z(x, sizes):
    return jnp.stack([x] + [swap(x, "dp", sizes["dp"], m) for m in Z_MASKS])


def grow(x, axis, mask, sizes):
    return jnp.concatenate([x, swap(x, axis, sizes[axis], mask)], axis=0)


def add(keep, other):
    half = keep.shape[0] // 2
    plus = lambda a, b: (a.astype(F32) + b.astype(F32)).astype(BF)
    return plus(keep[:half], other[:half]), plus(keep[half:], other[half:])


def fold(keep, send, axis, mask, sizes):
    return add(keep, swap(send, axis, sizes[axis], mask))


def fold_z(lo, hi, sizes):
    parts = [lo[0], swap(lo[1], "dp", sizes["dp"], 2), swap(hi[0], "dp", sizes["dp"], 4), swap(hi[1], "dp", sizes["dp"], 6)]
    return sum(p.astype(F32) for p in parts)


def place_table(me_d, me_c):
    d = (jnp.arange(8, dtype=jnp.int32) ^ me_d)[:, None]
    c = (jnp.arange(4, dtype=jnp.int32) ^ me_c)[None, :]
    x, z, y = d & 1, d >> 1, c >> 1
    return (x * 8 + y * 4 + z).reshape(-1), (z * 4 + x * 2 + y).reshape(-1), jnp.broadcast_to(c & 1, (8, 4)).reshape(-1)


def fold_down(d):
    n = d.shape[0] // 2
    return jnp.concatenate([d[:n], d[n:]], axis=1)


def unfold_down(p):
    m = p.shape[1] // 2
    return jnp.concatenate([p[:, :m], p[:, m:]], axis=0)


def after_all(xs, *others):
    return lax.optimization_barrier(tuple(xs) + others)[: len(xs)]


def after(x, *others):
    return lax.optimization_barrier((x,) + others)[0]


def per_device(sizes, tokens, segments, attn_gain, query_weight, key_matrix, value_matrix,
               out_weight, mlp_gain, gate_weight, up_weight, down_weight, cotangent):
    nd, nc = sizes["dp"], sizes["ctx"]
    tokens, cotangent = jnp.swapaxes(tokens, 1, 2), jnp.swapaxes(cotangent, 1, 2)
    seqs, width, rows = tokens.shape
    blk = rows // 2
    me_d = lax.axis_index("dp")
    me_c = lax.axis_index("ctx")
    last = nc - 1
    kvd = GROUPS * HEAD
    qd = HEADS * HEAD
    qn, kn, fn = query_weight.shape[1], key_matrix.shape[1], gate_weight.shape[1]
    ff = fn * nc
    shard = width // nd
    box = nd == 8 and nc == 4
    csteps = [("ctx", b) for b in reversed(bits_of(nc))]
    wsteps = [("dp", b) for b in reversed(bits_of(nd))] + csteps

    ctx_bits = [b for _, b in csteps]

    def piece_rel(i):
        return sum(b for k, b in enumerate(ctx_bits) if i >> k & 1)

    place = {piece_rel(i): i for i in range(nc)}

    def balanced(all_pieces):
        rel = [all_pieces[place[r]] for r in range(nc)]
        return jnp.stack([jnp.concatenate([rel[r][..., :blk], rel[r ^ last][..., blk:]], axis=-1) for r in range(nc)])

    owner = me_c ^ jnp.arange(nc, dtype=jnp.int32)
    lane = jnp.arange(blk, dtype=jnp.int32)
    index = jnp.concatenate(
        [owner[:, None] * rows + lane[None], (last - owner[:, None]) * rows + blk + lane[None]], axis=1)
    inverse = ROPE_BASE ** (-2.0 * jnp.arange(HALF).astype(F32) / HEAD)

    def angles(seg_all, s):
        zseg = balanced(seg_all[:, s])
        before = jnp.where(zseg == 0, 0, jnp.where(zseg == 1, jnp.sum(zseg < 1), jnp.sum(zseg < 2)))
        phase = (index - before).astype(F32)[:, None, :] * inverse[None, :, None]
        return zseg[:, None, :], jnp.cos(phase), jnp.sin(phase)

    pad = lambda n: jnp.zeros((shard, n), BF)
    a_own = jnp.concatenate([query_weight, key_matrix, value_matrix, attn_gain[:, None], pad(15)], axis=1)
    b1_own = jnp.concatenate([gate_weight, up_weight], axis=1)
    b2_own = jnp.concatenate([out_weight, mlp_gain[:, None], pad(111)], axis=1)
    if box:
        b2_own = jnp.concatenate([b2_own, fold_down(down_weight.T)], axis=1)
        a_z = stack_z(a_own, sizes)
        b2_y = grow(b2_own[None], "ctx", 2, sizes)
        seg_y = grow(segments[None], "ctx", 2, sizes)
        a_z, b2_y, seg_y, tok = lax.optimization_barrier((a_z, b2_y, seg_y, tokens))
        a_y = grow(a_z, "ctx", 2, sizes)
        b2_x = grow(b2_y, "dp", 1, sizes)
        seg_all = grow(seg_y, "ctx", 1, sizes)
        tok0_y = grow(tok[0][None], "ctx", 2, sizes)
        a_y, b2_x, b1_own = lax.optimization_barrier((a_y, b2_x, b1_own))
        a_x = grow(a_y, "dp", 1, sizes)
        b1_z = stack_z(b1_own, sizes)
        tables = [angles(seg_all, s) for s in range(seqs)]
        a_x, tok0_y, tok, b1_z, tables = lax.optimization_barrier((a_x, tok0_y, tok, b1_z, tables))
        tokens_all = [(tok0_y, swap(tok0_y, "ctx", nc, 1))]
        a_parts = a_x, swap(a_x, "ctx", nc, 1)
        b1_got = swap(b1_z, "dp", nd, 1)
        tok1 = tok[1][None]
        tok1_got = swap(tok1, "ctx", nc, 2)
        at1, at2, other1 = place_table(me_d, me_c)
        places = jnp.concatenate([at1, at2, other1, me_c[None] & 1, me_c[None], me_d[None]])
        w_all = pl.pallas_call(
            unpack_a_kernel,
            in_specs=[pl.BlockSpec(memory_space=pltpu.SMEM)] + [pl.BlockSpec(memory_space=pltpu.VMEM)] * 2,
            out_specs=pl.BlockSpec(memory_space=pltpu.VMEM),
            out_shape=jax.ShapeDtypeStruct((nd, shard, 1024), BF),
            compiler_params=params(),
            name="unpack_a",
        )(places, *a_parts).reshape(width, 1024)
        b2_got = [swap(p, "dp", nd, m) for p, m in zip(after_all([b2_x] * 3, w_all), Z_MASKS)]

    def unpack_b(b1, b1x, b2, b2x):
        b1, b1x = (v.reshape(2, 2, 4, shard, 2 * fn) for v in (b1, b1x))
        b2, b2x = (v.reshape(4, 2, 2, shard, 640) for v in (b2, b2x))
        piece1 = pl.BlockSpec((2, 2, 1, shard, 2 * fn), lambda z, t: (0, 0, jnp.bitwise_xor(z, t[98] // 2), 0, 0))
        piece2 = pl.BlockSpec((1, 2, 2, shard, 640), lambda z, t: (jnp.bitwise_xor(z, t[98] // 2), 0, 0, 0, 0))
        duo = lambda n: pl.BlockSpec((2, shard, n), lambda z, t: (z, 0, 0))
        wg, wu, wo, wd = pl.pallas_call(
            unpack_b_kernel,
            grid_spec=pltpu.PrefetchScalarGridSpec(
                num_scalar_prefetch=1,
                grid=(4,),
                in_specs=[piece1, piece1, piece2, piece2],
                out_specs=[duo(ff), duo(ff), duo(640), pl.BlockSpec((nd, shard, ff // 4), lambda z, t: (0, 0, z))],
            ),
            out_shape=[jax.ShapeDtypeStruct((nd, shard, ff), BF), jax.ShapeDtypeStruct((nd, shard, ff), BF),
                       jax.ShapeDtypeStruct((nd, shard, 640), BF), jax.ShapeDtypeStruct((nd, shard, ff), BF)],
            compiler_params=params(),
            name="unpack_b",
        )(places, b1, b1x, b2, b2x)
        return wg.reshape(width, ff), wu.reshape(width, ff), wo.reshape(width, 640), wd.reshape(width, ff)

    if not box:
        dslot = slot_table(wsteps, "dp", nd, me_d)
        cslot = slot_table(wsteps, "ctx", nc, me_c)

        def whole(own):
            x = spread(own, wsteps, sizes)
            x = x.reshape((nc, nd) + own.shape)
            return jnp.take(jnp.take(x, cslot, axis=0), dslot, axis=1)

        def join(x):
            return x.transpose(1, 2, 0, 3).reshape(nd * x.shape[2], nc * x.shape[3])

        a = whole(a_own)
        w_all = jnp.concatenate(
            [join(a[..., :qn]), join(a[..., qn : qn + kn]), join(a[..., qn + kn : qn + 2 * kn]),
             a[0, :, :, 240:241].reshape(width, 1), jnp.zeros((width, 63), BF)], axis=1)
        b1 = whole(b1_own)
        b2 = whole(b2_own)
        wg, wu = join(b1[..., :fn]), join(b1[..., fn:])
        wo = jnp.concatenate([join(b2[..., :qn]), b2[0, :, :, qn : qn + 1].reshape(width, 1), jnp.zeros((width, 63), BF)], axis=1)
        wd = join(whole(down_weight)).T
        places = jnp.zeros((99,), jnp.int32)
        tokens_all = [spread(tokens[s], csteps, sizes) for s in range(seqs)]
        seg_all = spread(segments, csteps, sizes)
        tables = [angles(seg_all, s) for s in range(seqs)]
        tokens_all = [(v[: nc // 2], v[nc // 2 :]) for v in tokens_all]
        cot_got = swap(cotangent[..., blk:], "ctx", nc, last)

    table = jnp.asarray(pair_table(nc))[me_c].reshape(-1)
    pairs = 2 * nc + 1
    wide_q = SHARE * blk

    saved = []
    for s in range(seqs):
        tok_own, tok_got = tokens_all[s]
        zseg, cos_t, sin_t = tables[s]

        piece = lambda *tail: pl.BlockSpec((1,) + tail, lambda r: (r,) + (0,) * len(tail))
        fixed = lambda *shape: pl.BlockSpec(shape, lambda r: (0,) * len(shape))
        if s:
            tok_own = after(tok_own, prob)
        half = lambda at: pl.BlockSpec((1, width, blk), at)
        near = half(lambda r: (r // 2, 0, 0))
        opposite = half(lambda r: ((nc - 1 - r) // 2, 0, 1))
        h1, k_t, v_t, q_t, x_own = pl.pallas_call(
            pre_kernel,
            grid=(nc,),
            in_specs=[near, near, opposite, opposite, fixed(width, 1024), piece(HALF, rows), piece(HALF, rows), piece(1, rows)],
            out_specs=[piece(width, rows),
                       pl.BlockSpec((GROUPS, 1, AUG, rows), lambda r: (0, r, 0, 0)),
                       pl.BlockSpec((GROUPS, 1, AUG, rows), lambda r: (0, r, 0, 0)),
                       fixed(GROUPS, 2, AUG, wide_q), fixed(width, rows)],
            out_shape=[jax.ShapeDtypeStruct((nc, width, rows), BF),
                       jax.ShapeDtypeStruct((GROUPS, nc, AUG, rows), BF),
                       jax.ShapeDtypeStruct((GROUPS, nc, AUG, rows), BF),
                       jax.ShapeDtypeStruct((GROUPS, 2, AUG, wide_q), BF),
                       jax.ShapeDtypeStruct((width, rows), BF)],
            compiler_params=params(),
            cost_estimate=pl.CostEstimate(flops=4_500_000_000, bytes_accessed=10_000_000, transcendentals=0),
            name="pre",
        )(tok_own, tok_got, tok_own, tok_got, w_all, cos_t, sin_t, zseg)

        if box and s == 0:
            q_t, k_t, v_t, h1, x_own, b1_got, tok1_got = lax.optimization_barrier((q_t, k_t, v_t, h1, x_own, b1_got, tok1_got))
            b1_x = jnp.concatenate([b1_z, b1_got], axis=0)
            b1_got = swap(b1_x, "ctx", nc, 2)
            tok1_y = jnp.concatenate([tok1, tok1_got], axis=0)
            tokens_all.append((tok1_y, swap(tok1_y, "ctx", nc, 1)))
            q_t = after(q_t, b1_x, tok1_y)
        if box and s == 1:
            q_t, k_t, v_t, h1, x_own, b1_got, b2_got = lax.optimization_barrier((q_t, k_t, v_t, h1, x_own, b1_got, b2_got))
            b1_y = jnp.concatenate([b1_x, b1_got], axis=0)
            b2_z = jnp.concatenate([b2_x] + list(b2_got), axis=0)
            b1_far, b2_far = swap(b1_y, "ctx", nc, 1), swap(b2_z, "ctx", nc, 1)
            cot_got = swap(after(cotangent, q_t)[..., blk:], "ctx", nc, last)
            q_t = after(q_t, b1_y, b2_z)
        att = lambda *tail: pl.BlockSpec((1,) + tail, lambda g, t: (g,) + (0,) * len(tail))
        prob, o_t, inv_l = pl.pallas_call(
            functools.partial(attend_kernel, pairs),
            grid_spec=pltpu.PrefetchScalarGridSpec(
                num_scalar_prefetch=1,
                grid=(GROUPS,),
                in_specs=[att(2, AUG, wide_q), att(nc, AUG, rows), att(nc, AUG, rows)],
                out_specs=[att(pairs, blk, wide_q), att(2, HEAD, wide_q), att(2, 1, wide_q)],
                scratch_shapes=[pltpu.VMEM((pairs, blk, wide_q), F32), pltpu.VMEM((2, 8, wide_q), F32),
                                pltpu.VMEM((2, AUG, wide_q), F32)],
            ),
            out_shape=[jax.ShapeDtypeStruct((GROUPS, pairs, blk, wide_q), BF),
                       jax.ShapeDtypeStruct((GROUPS, 2, HEAD, wide_q), BF),
                       jax.ShapeDtypeStruct((GROUPS, 2, 1, wide_q), F32)],
            compiler_params=params(),
            cost_estimate=pl.CostEstimate(flops=12_000_000_000, bytes_accessed=12_000_000, transcendentals=0),
            name="attend",
        )(table, q_t, k_t, v_t)
        if box and s == 1:
            prob, o_t, inv_l, b1_far, b2_far, cot_got = lax.optimization_barrier((prob, o_t, inv_l, b1_far, b2_far, cot_got))
            wg, wu, wo, wd = unpack_b(b1_y, b1_far, b2_z, b2_far)
        saved.append((x_own, cos_t, sin_t, h1, k_t, v_t, q_t, prob, o_t, inv_l))

    total = seqs * rows
    steps = 2
    fstep = ff // steps
    fixed = lambda *shape: pl.BlockSpec(shape, lambda f, t: (0,) * len(shape))
    if box:
        grad_specs = [fixed(16, shard, 2 * fn)] * 2 + [fixed(16, shard, 640)] * 2
        grad_shapes = [jax.ShapeDtypeStruct((16, shard, 2 * fn), BF)] * 2 + [jax.ShapeDtypeStruct((16, shard, 640), BF)] * 2
    else:
        grad_specs = [pl.BlockSpec((width, fstep), lambda f, t: (0, f))] * 2
        grad_specs += [pl.BlockSpec((width, fstep), lambda f, t: (0, f)), fixed(width, 640)]
        grad_shapes = [jax.ShapeDtypeStruct((width, ff), BF)] * 3 + [jax.ShapeDtypeStruct((width, 640), BF)]
    out_near, out_far, d_middle, do_t, *grads = pl.pallas_call(
        functools.partial(middle_kernel, box, nd, nc, seqs),
        grid_spec=pltpu.PrefetchScalarGridSpec(
            num_scalar_prefetch=1,
            grid=(steps,),
            in_specs=[fixed(width, rows), fixed(GROUPS, 2, HEAD, wide_q)] * seqs
            + [fixed(seqs, width, rows), fixed(seqs, width, blk)] + [pl.BlockSpec((width, fstep), lambda f, t: (0, f))] * 3 + [fixed(width, 640)],
            out_specs=[fixed(seqs, width, blk), fixed(seqs, width, blk), fixed(seqs, width, rows), fixed(seqs, GROUPS, 2, HEAD, wide_q)] + grad_specs,
            scratch_shapes=[pltpu.VMEM((qd, total), BF), pltpu.VMEM((width, total), F32), pltpu.VMEM((width, total), BF),
                            pltpu.VMEM((width, total), BF), pltpu.VMEM((width, total), F32), pltpu.VMEM((width, total), F32)],
        ),
        out_shape=[jax.ShapeDtypeStruct((seqs, width, blk), BF), jax.ShapeDtypeStruct((seqs, width, blk), BF),
                   jax.ShapeDtypeStruct((seqs, width, rows), F32),
                   jax.ShapeDtypeStruct((seqs, GROUPS, 2, HEAD, wide_q), BF)] + grad_shapes,
        compiler_params=params(),
        cost_estimate=pl.CostEstimate(flops=36_000_000_000, bytes_accessed=20_000_000, transcendentals=0),
        name="middle",
    )(places, *[v[k] for v in saved for k in (0, 8)], cotangent, cot_got, wg, wu, wd, wo)

    def settle(pieces):
        x = jnp.take(jnp.take(pieces, jnp.argsort(dslot), axis=0), jnp.argsort(cslot), axis=1)
        x = jnp.swapaxes(x, 0, 1).reshape((nc * nd,) + pieces.shape[2:])
        return gather_up(x, wsteps, sizes).astype(F32)

    def cut(g):
        r, c = g.shape
        return g.reshape(nd, r // nd, nc, c // nc).transpose(0, 2, 1, 3)

    def repeat(column):
        return jnp.broadcast_to(column.reshape(nd, 1, shard, 1), (nd, nc, shard, 1))

    if box:
        b1_got = swap(grads[1], "ctx", nc, 1)
        b2_got = swap(grads[3], "ctx", nc, 1)
    else:
        gate_sum, up_sum, down_sum = settle(cut(grads[0])), settle(cut(grads[1])), settle(cut(grads[2].T))
        b2_sum = settle(jnp.concatenate([cut(grads[3][:, :qd]), repeat(grads[3][:, qd])], axis=-1))
        out_sum, gain2_sum = b2_sum[:, :qn], b2_sum[:, qn]

    out_away = swap(out_far, "ctx", nc, last)
    half = nc // 2
    backs, dkv_owns = [], []
    for s in range(seqs):
        _, cos_t, sin_t, h1, k_t, v_t, q_t, prob, o_t, inv_l = saved[s]
        if s:
            q_t = after(q_t, backs[0][0], *((b1 + b2) if box else ()))
        att = lambda *tail: pl.BlockSpec((1,) + tail, lambda g, t: (g,) + (0,) * len(tail))
        fixed = lambda *shape: pl.BlockSpec(shape, lambda g, t: (0,) * len(shape))
        pair_of = pl.BlockSpec((1, 1, 2, HEAD, wide_q), lambda g, t: (s, g, 0, 0, 0))
        count = 1 if box and s == 0 else half
        kv_out = pl.BlockSpec((count, 2, 1, HEAD, rows), lambda g, t: (0, 0, g, 0, 0))
        dq_t, *kvs = pl.pallas_call(
            functools.partial(attend_back_kernel, pairs, tuple(place[r] for r in range(nc))),
            grid_spec=pltpu.PrefetchScalarGridSpec(
                num_scalar_prefetch=1,
                grid=(GROUPS,),
                in_specs=[att(pairs, blk, wide_q), att(2, AUG, wide_q), att(nc, AUG, rows), att(nc, AUG, rows),
                          att(2, HEAD, wide_q), pair_of, att(2, 1, wide_q), fixed(nc, HALF, rows), fixed(nc, HALF, rows)],
                out_specs=[att(SHARE, HEAD, rows)] + [kv_out] * (nc // count),
                scratch_shapes=[pltpu.VMEM((2, AUG, wide_q), BF), pltpu.VMEM((2 * nc, HEAD, blk), F32),
                                pltpu.VMEM((2 * nc, HEAD, blk), F32), pltpu.VMEM((2, HEAD, wide_q), F32)],
            ),
            out_shape=[jax.ShapeDtypeStruct((GROUPS, SHARE, HEAD, rows), BF)]
            + [jax.ShapeDtypeStruct((count, 2, GROUPS, HEAD, rows), BF)] * (nc // count),
            compiler_params=params(),
            cost_estimate=pl.CostEstimate(flops=20_000_000_000, bytes_accessed=12_000_000, transcendentals=0),
            name="attend_back",
        )(table, prob, q_t, k_t, v_t, o_t, do_t, inv_l, cos_t, sin_t)
        if box and s == 0:
            dq_t, b1_got, b2_got, out_away, *kvs = lax.optimization_barrier((dq_t, b1_got, b2_got, out_away, *kvs))
        if box and s == 1:
            dq_t, b1_got, z_got, dkv0, *kvs = lax.optimization_barrier((dq_t, b1_got, z_got, dkv0, *kvs))
            dkv_owns[0] = [dkv_owns[0][0]] + list(dkv0)
        kvs = [v.reshape(count, 2 * kvd, rows) for v in kvs]
        backs.append([dq_t.reshape(qd, rows), h1] + kvs)
        if box and s == 0:
            dkv0 = [swap(v, "ctx", nc, piece_rel(k)) for k, v in enumerate(kvs) if k]
            dkv_owns.append(kvs[:1])
            b1, b2 = add(grads[0], b1_got), add(grads[2], b2_got)
            b1_got = swap(b1[1], "dp", nd, 1)
            z_got = swap(b2[1][:4], "dp", nd, 4)
        else:
            dkv_got = swap(kvs[1], "ctx", nc, csteps[-1][1])
            if box:
                b1 = add(b1[0], b1_got)
                b1_got = swap(b1[1], "ctx", nc, 2)
                b2_parts = [b2[0][:4], z_got] + [swap(p, "dp", nd, m) for p, m in ((b2[0][4:], 2), (b2[1][4:], 6))]
            low, high = add(kvs[0], dkv_got)
            dkv_owns.append([low, swap(high, "ctx", nc, csteps[0][1])])

    def token(s, dqr_t):
        return pl.pallas_call(
            token_kernel,
            grid=(1,),
            in_specs=[pl.BlockSpec((1, 2 * kvd, rows), lambda i: (0, 0, 0))] * len(dkv_owns[s])
            + [pl.BlockSpec((qd, rows), lambda i: (0, 0)), pl.BlockSpec((width, 1024), lambda i: (0, 0)),
               pl.BlockSpec((width, rows), lambda i: (0, 0)), pl.BlockSpec((1, width, rows), lambda i: (s, 0, 0))],
            out_specs=[pl.BlockSpec((width, blk), lambda i: (0, 0))] * 2,
            out_shape=[jax.ShapeDtypeStruct((width, blk), BF)] * 2,
            compiler_params=params(),
            cost_estimate=pl.CostEstimate(flops=4_000_000_000, bytes_accessed=5_000_000, transcendentals=0),
            name="token",
        )(*dkv_owns[s], dqr_t, w_all, saved[s][0], d_middle)

    near0, far0 = token(0, after(backs[0][0], backs[1][0], dkv_owns[1][0], *((b1[0],) if box else ())))
    away0 = swap(far0, "ctx", nc, last)
    spot = [place[r] for r in range(nc)]
    hid_of = pl.BlockSpec((1, width, rows), lambda r, t: (t[99 + r], 0, 0))
    fixed = lambda *shape: pl.BlockSpec(shape, lambda r, t: (0,) * len(shape))
    if box:
        a_specs = [fixed(16, shard, 256)] * 2
        a_shapes = [jax.ShapeDtypeStruct((16, shard, 256), BF)] * 2
    else:
        a_specs, a_shapes = [fixed(width, 1024)], [jax.ShapeDtypeStruct((width, 1024), BF)]
    ops = [v for back in backs for v in back]
    ops[0] = after(ops[0], near0)
    places = jnp.concatenate([places, jnp.asarray([spot.index(i) for i in range(nc)], jnp.int32)])
    a_out = pl.pallas_call(
        functools.partial(post_kernel, box, nd, nc, tuple(len(v) for v in backs)),
        grid_spec=pltpu.PrefetchScalarGridSpec(
            num_scalar_prefetch=1,
            grid=(nc,),
            in_specs=[sp for back in backs for sp in [fixed(qd, rows), hid_of] + [fixed(*v.shape) for v in back[2:]]] + [fixed(width, 1024)],
            out_specs=a_specs,
            scratch_shapes=[pltpu.VMEM((width, 1024), F32)],
        ),
        out_shape=a_shapes,
        compiler_params=params(),
        cost_estimate=pl.CostEstimate(flops=15_000_000_000, bytes_accessed=10_000_000, transcendentals=0),
        name="post",
    )(places, *ops, w_all)

    if box:
        *a_out, b1_got, b2_parts, away0 = lax.optimization_barrier((*a_out, b1_got, b2_parts, away0))
        a_got = swap(a_out[1], "ctx", nc, 1)
        a_got, dkv_owns[1] = lax.optimization_barrier((a_got, dkv_owns[1]))
        total_of = lambda parts: sum(p.astype(F32) for p in parts)
        b2 = total_of(b2_parts).astype(BF)
        b2_got = swap(b2[2:], "dp", nd, 1)
        b1 = add(b1[0], b1_got)
        a = add(a_out[0], a_got)
        a_got = swap(a[1], "dp", nd, 1)
        b1_parts = [b1[0][0]] + [swap(p, "dp", nd, m) for p, m in zip((b1[0][1], b1[1][0], b1[1][1]), Z_MASKS)]
    mine, away = token(1, after(backs[1][0], *((a[0], b2[0]) if box else ())))
    if box:
        mine, away, a_got, b1_parts, b2_got = lax.optimization_barrier((mine, away, a_got, b1_parts, b2_got))
    token_near, token_away = [near0, mine], [away0, swap(away, "ctx", nc, last)]
    if box:
        a = add(a[0], a_got)
        b2 = (b2[:2].astype(F32) + b2_got.astype(F32)).astype(BF)
        b2_got = swap(b2[1], "ctx", nc, 2)
        a = fold(*a, "ctx", 2, sizes)
        a, token_away, b2_got = lax.optimization_barrier((a, token_away, b2_got))
        b1_sum = total_of(b1_parts)
        b2_sum = b2[0].astype(F32) + b2_got.astype(F32)
        gate_sum, up_sum = b1_sum[:, :fn], b1_sum[:, fn:]
        out_sum, gain2_sum, down_sum = b2_sum[:, :qn], b2_sum[:, qn], unfold_down(b2_sum[:, 256:]).T

    if box:
        a_sum = fold_z(*a, sizes)
    else:
        a = a_out[0]
        a_sum = settle(jnp.concatenate(
            [cut(a[:, :qd]), cut(a[:, qd : qd + kvd]), cut(a[:, qd + kvd : qd + 2 * kvd]), repeat(a[:, 960])], axis=-1))

    def home(mine, away):
        return jnp.swapaxes(jnp.concatenate([mine, away], axis=-1), 1, 2)

    return (
        home(out_near, out_away),
        home(jnp.stack(token_near), jnp.stack(token_away)),
        a_sum[:, 2 * kn + qn],
        a_sum[:, :qn],
        a_sum[:, qn : qn + kn],
        a_sum[:, qn + kn : qn + 2 * kn],
        out_sum,
        gain2_sum,
        gate_sum,
        up_sum,
        down_sum,
    )


def pair_table(nc):
    out = []
    for me in range(nc):
        spots = {}
        for r in range(nc):
            d = me ^ r
            spots[2 * d] = 2 * r
            spots[2 * (nc - 1 - d) + 1] = 2 * r + 1
        mine = [2 * me, 2 * (nc - 1 - me) + 1]
        rows = [(i, spots[mine[i]]) for i in range(2)]
        rows += [(i, spots[k]) for i in range(2) for k in range(mine[i])]
        out.append(rows)
    return np.array(out, np.int32)


def turn(x, cos, sin, heads, sign):
    parts = []
    for h in range(heads):
        lo, hi = x[h * HEAD : h * HEAD + HALF], x[h * HEAD + HALF : (h + 1) * HEAD]
        parts += [lo * cos - sign * hi * sin, hi * cos + sign * lo * sin]
    return jnp.concatenate(parts, axis=0)


def unpack_a_kernel(places, own_ref, other_ref, w_ref):
    nd = w_ref.shape[0]
    nc = 4
    qn, kn = 144, 48
    qd, kvd = qn * nc, kn * nc

    def write(cores):
        for d in range(nd):
            for c in range(nc):
                p = cores[c % 2][places[d * nc + c]].astype(F32)
                if c == 0:
                    cols = [[], [], []]
                    gain = p[:, 240:256]
                cols[0].append(p[:, :qn])
                cols[1].append(p[:, qn : qn + kn])
                cols[2].append(p[:, qn + kn : qn + 2 * kn])
            row = cols[0] + cols[1] + cols[2] + [gain, jnp.zeros((p.shape[0], 48), F32)]
            w_ref[d] = jnp.concatenate(row, axis=1).astype(BF)

    core = places[96]
    pl.when(core == 0)(lambda: write((own_ref, other_ref)))
    pl.when(core == 1)(lambda: write((other_ref, own_ref)))


def unpack_b_kernel(places, b1_ref, b1x_ref, b2_ref, b2x_ref, g_ref, u_ref, o_ref, w_ref):
    nc = 4
    fn = b1_ref.shape[-1] // 2
    shard = b1_ref.shape[-2]
    me_y, me_x = places[97] // 2, places[98] % 2

    def write(one, two):
        for x in range(2):
            at_x = jnp.bitwise_xor(me_x, x)
            outs = []
            for c in range(nc):
                y = jnp.bitwise_xor(me_y, c // 2)
                p = one[c % 2][y, at_x, 0]
                g_ref[x, :, c * fn : (c + 1) * fn] = p[:, :fn]
                u_ref[x, :, c * fn : (c + 1) * fn] = p[:, fn:]
                p = two[c % 2][0, at_x, y].astype(F32)
                outs.append(p[:, :144])
                for i in range(2):
                    w_ref[2 * c + i, :, x * 192 : (x + 1) * 192] = p[:, 256 + 192 * i : 448 + 192 * i].astype(BF)
                if c == 0:
                    gain = p[:, 144:160]
            o_ref[x] = jnp.concatenate(outs + [gain, jnp.zeros((shard, 48), F32)], axis=1).astype(BF)

    core = places[96]
    pl.when(core == 0)(lambda: write((b1_ref, b1x_ref), (b2_ref, b2x_ref)))
    pl.when(core == 1)(lambda: write((b1x_ref, b1_ref), (b2x_ref, b2_ref)))


def pre_kernel(own_ref, got_ref, own2_ref, got2_ref, w_ref, cos_ref, sin_ref, seg_ref, h_ref, k_ref, v_ref, q_ref, x_ref):
    mine = lax.rem(pl.program_id(0), 2) == 0
    x = jnp.concatenate([jnp.where(mine, own_ref[0].astype(F32), got_ref[0].astype(F32)),
                         jnp.where(mine, got2_ref[0].astype(F32), own2_ref[0].astype(F32))], axis=1)
    inv = lax.rsqrt(jnp.mean(x * x, axis=0, keepdims=True) + EPS)
    qd, kvd = HEADS * HEAD, GROUPS * HEAD
    gain = w_ref[:, qd + 2 * kvd : qd + 2 * kvd + 1].astype(F32)
    h = ((x * inv) * gain).astype(BF)
    h_ref[0] = h
    cos, sin, seg = cos_ref[0], sin_ref[0], seg_ref[0]
    rows = x.shape[1]
    blk = rows // 2
    kv = dot(w_ref[:, qd : qd + 2 * kvd], h, TN)
    keys = turn(kv[:kvd], cos, sin, GROUPS, 1.0).astype(BF)
    values = kv[kvd:].astype(BF)
    row = lax.broadcasted_iota(jnp.int32, (AUG - HEAD, rows), 0)
    other = jnp.where((row < 3) & (row != seg), -1e30, 0.0).astype(BF)
    ones = (row < 3).astype(BF)
    for g in range(GROUPS):
        k_ref[g, 0, :HEAD] = keys[g * HEAD : (g + 1) * HEAD]
        k_ref[g, 0, HEAD:] = other
        v_ref[g, 0, :HEAD] = values[g * HEAD : (g + 1) * HEAD]
        v_ref[g, 0, HEAD:] = ones

    @pl.when(pl.program_id(0) == 0)
    def _():
        q = turn(dot(w_ref[:, :qd], h, TN), cos, sin, HEADS, 1.0).astype(BF) * (1.0 / math.sqrt(HEAD))
        x_ref[...] = x.astype(BF)
        same = (row == seg).astype(BF)
        for g in range(GROUPS):
            for b in range(2):
                for j in range(SHARE):
                    n = g * SHARE + j
                    q_ref[g, b, :HEAD, j * blk : (j + 1) * blk] = q[n * HEAD : (n + 1) * HEAD, b * blk : (b + 1) * blk]
                    q_ref[g, b, HEAD:, j * blk : (j + 1) * blk] = same[:, b * blk : (b + 1) * blk]


def by_core(core, refs, write):
    pairs = [refs[i : i + 2] for i in range(0, len(refs), 2)]
    pl.when(core == 0)(lambda: write(*pairs))
    pl.when(core == 1)(lambda: write(*[p[::-1] for p in pairs]))


def middle_kernel(box, nd, nc, seqs, places, *refs):
    xs, refs = refs[: 2 * seqs], refs[2 * seqs :]
    cot_ref, got_ref, wg_ref, wu_ref, wd_ref, wo_ref, near_ref, far_ref, dm_ref, do_ref, *rest = refs
    grads, (att_ref, mid_ref, h_ref, cots_ref, acc_ref, dh_ref) = rest[:4], rest[4:]
    f = pl.program_id(0)
    blk = got_ref.shape[2]
    rows = 2 * blk
    qd, width = HEADS * HEAD, cot_ref.shape[1]
    shard = width // nd
    fn = wg_ref.shape[1]
    steps = 2
    part_fn = fn * steps // nc

    def norm():
        m = mid_ref[...]
        inv = lax.rsqrt(jnp.mean(m * m, axis=0, keepdims=True) + EPS)
        return m, inv, m * inv

    def gain_column():
        return wo_ref[:, qd : qd + 1].astype(F32)

    def of(s):
        return slice(s * rows, (s + 1) * rows)

    def blocks():
        for s in range(seqs):
            for g in range(GROUPS):
                for b in range(2):
                    for j in range(SHARE):
                        n = g * SHARE + j
                        yield (s, g, b, slice(None), slice(j * blk, (j + 1) * blk)), (
                            slice(n * HEAD, (n + 1) * HEAD), slice(s * rows + b * blk, s * rows + (b + 1) * blk))

    @pl.when(f == 0)
    def _():
        for there, here in blocks():
            att_ref[here] = xs[2 * there[0] + 1][there[1:]]
        branch = dot(wo_ref[:, :qd], att_ref[...], TN)
        for s in range(seqs):
            mid_ref[:, of(s)] = xs[2 * s][...].astype(F32) + branch[:, of(s)]
            cots_ref[:, s * rows : s * rows + blk] = cot_ref[s, :, :blk]
            cots_ref[:, s * rows + blk : (s + 1) * rows] = got_ref[s]
        _, _, n2 = norm()
        h_ref[...] = (n2 * gain_column()).astype(BF)

    h = h_ref[...]
    cot = cots_ref[...]
    gate = dot(wg_ref[...], h, TN)
    up = dot(wu_ref[...], h, TN)
    sig = jax.nn.sigmoid(gate)
    act = gate * sig
    inner = (act * up).astype(BF)
    part = dot(wd_ref[...], inner, NN)
    d_inner = dot(wd_ref[...], cot, TN)
    d_gate = (d_inner * up * (sig + act * (1.0 - sig))).astype(BF)
    d_up = (d_inner * act).astype(BF)
    d_part = dot(wg_ref[...], d_gate, NN) + dot(wu_ref[...], d_up, NN)

    @pl.when(f == 0)
    def _():
        acc_ref[...] = part
        dh_ref[...] = d_part

    @pl.when(f > 0)
    def _():
        acc_ref[...] += part
        dh_ref[...] += d_part

    grad_gate = dot(h, d_gate, NT)
    grad_up = dot(h, d_up, NT)
    grad_down = dot(cot, inner, NT)
    if box:
        cols = width // nc
        per = fn * steps // nd

        def pack(b1s, b2s):
            for k in range(nc // steps):
                c = f * (nc // steps) + k
                lanes = slice(k * part_fn, (k + 1) * part_fn)
                for d in range(nd):
                    part_rows = slice(d * shard, (d + 1) * shard)
                    at = places[d * nc + c]
                    b1s[k % 2][at, :, :part_fn] = grad_gate[part_rows, lanes].astype(BF)
                    b1s[k % 2][at, :, part_fn:] = grad_up[part_rows, lanes].astype(BF)
            for i in range(fn // per):
                for c in range(nc):
                    p = fold_down(grad_down[c * cols : (c + 1) * cols, i * per : (i + 1) * per]).astype(BF)
                    b2s[c % 2][places[32 + (f * (fn // per) + i) * nc + c], :, 256:640] = p

        by_core(places[96], grads, pack)
    else:
        grads[0][...] = grad_gate.astype(BF)
        grads[1][...] = grad_up.astype(BF)
        grads[2][...] = grad_down.astype(BF)

    @pl.when(f == pl.num_programs(0) - 1)
    def _():
        m, inv, n2 = norm()
        out = (m + acc_ref[...]).astype(BF)
        d_h2 = dh_ref[...]
        e2 = d_h2 * gain_column()
        d_middle = cots_ref[...].astype(F32) + inv * (e2 - n2 * jnp.mean(e2 * n2, axis=0, keepdims=True))
        for s in range(seqs):
            near_ref[s] = out[:, s * rows : s * rows + blk]
            far_ref[s] = out[:, s * rows + blk : (s + 1) * rows]
            dm_ref[s] = d_middle[:, of(s)]
        branch = d_middle.astype(BF)
        d_att = dot(wo_ref[:, :qd], branch, NN).astype(BF)
        for there, here in blocks():
            do_ref[there] = d_att[here]
        grad_out = dot(att_ref[...], branch, NT)
        gain = jnp.broadcast_to(jnp.sum(d_h2 * n2, axis=1, keepdims=True), (width, 128))
        if box:
            def pack_out(b1s, b2s):
                for d in range(nd):
                    part_rows = slice(d * shard, (d + 1) * shard)
                    for c in range(nc):
                        p = jnp.concatenate([grad_out[part_rows, c * cols : (c + 1) * cols], gain[part_rows, :112]], axis=1)
                        b2s[c % 2][places[32 + d * nc + c], :, :256] = p.astype(BF)

            by_core(places[96], grads, pack_out)
        else:
            grads[3][...] = jnp.concatenate([grad_out, gain[:, :64]], axis=1).astype(BF)


def post_kernel(box, nd, nc, counts, places, *refs):
    seqs = []
    for n in counts:
        seqs.append(refs[:n])
        refs = refs[n:]
    w_ref, outs, acc_ref = refs[0], refs[1:-1], refs[-1]
    kvd, qd = GROUPS * HEAD, HEADS * HEAD
    r = pl.program_id(0)

    @pl.when(r == 0)
    def _():
        acc_ref[...] = jnp.zeros_like(acc_ref)
        acc_ref[:, :qd] = sum(dot(h_ref[0], dq_ref[...], NT) for dq_ref, h_ref, *_ in seqs)

    for k in range(nc):
        @pl.when(r == k)
        def _():
            terms = []
            for _, h_ref, *kvs in seqs:
                n = nc // len(kvs)
                terms.append(dot(h_ref[0], kvs[k // n][k % n], NT))
            acc_ref[:, qd : qd + 2 * kvd] += sum(terms)

    @pl.when(r == nc - 1)
    def _():
        g = acc_ref[...]
        w = w_ref[...].astype(F32)
        used = qd + 2 * kvd
        gain = jnp.sum(g[:, :used] * w[:, :used], axis=1, keepdims=True) / w[:, used : used + 1]
        if not box:
            outs[0][...] = jnp.concatenate([g[:, :used], jnp.broadcast_to(gain, (g.shape[0], 64))], axis=1).astype(BF)
            return
        shard = g.shape[0] // nd
        gain = jnp.broadcast_to(gain, (g.shape[0], 16))
        qn, kn = qd // nc, kvd // nc

        def pack(both):
            for d in range(nd):
                r = slice(d * shard, (d + 1) * shard)
                for c in range(nc):
                    p = jnp.concatenate(
                        [g[r, c * qn : (c + 1) * qn], g[r, qd + c * kn : qd + (c + 1) * kn],
                         g[r, qd + kvd + c * kn : qd + kvd + (c + 1) * kn], gain[r]], axis=1)
                    both[c % 2][places[d * nc + c]] = p.astype(BF)

        by_core(places[96], outs, pack)


def token_kernel(*refs):
    *kvs, dq_ref, w_ref, x_ref, dm_ref, near_ref, far_ref = refs
    qd, kvd = HEADS * HEAD, GROUPS * HEAD
    x = x_ref[...].astype(F32)
    inv = lax.rsqrt(jnp.mean(x * x, axis=0, keepdims=True) + EPS)
    n1 = x * inv
    dkv = sum(v[0].astype(F32) for v in kvs).astype(BF)
    d_h1 = dot(w_ref[:, :qd], dq_ref[...], NN) + dot(w_ref[:, qd : qd + 2 * kvd], dkv, NN)
    e1 = d_h1 * w_ref[:, qd + 2 * kvd : qd + 2 * kvd + 1].astype(F32)
    out = (dm_ref[0] + inv * (e1 - n1 * jnp.mean(e1 * n1, axis=0, keepdims=True))).astype(BF)
    blk = near_ref.shape[1]
    near_ref[...] = out[:, :blk]
    far_ref[...] = out[:, blk:]


def key_block(ref, loc, blk, rows=None):
    r, half = loc // 2, loc % 2
    lanes = pl.ds(pl.multiple_of(half * blk, blk), blk)
    if rows is None:
        return ref[0, r, :, lanes]
    return ref[0, r, :rows, lanes]


def attend_kernel(pairs, table, q_ref, k_ref, v_ref, p_ref, o_ref, l_ref, s_ref, m_ref, acc_ref):
    wide = q_ref.shape[-1]
    blk = wide // SHARE

    def score(t, diagonal):
        qb, loc = table[2 * t], table[2 * t + 1]
        s = dot(key_block(k_ref, loc, blk), q_ref[0, qb], TN)
        if diagonal:
            k_at = lax.broadcasted_iota(jnp.int32, (blk, wide), 0)
            q_at = lax.broadcasted_iota(jnp.int32, (blk, wide), 1) % blk
            s = jnp.where(k_at <= q_at, s, -1e30)
        s_ref[t] = s
        top = jnp.max(s.reshape(blk // 8, 8, wide), axis=0)
        if diagonal:
            m_ref[qb] = top
        else:
            m_ref[qb] = jnp.maximum(m_ref[qb], top)

    for t in range(2):
        score(t, True)
    lax.fori_loop(2, pairs, lambda t, c: (score(t, False), c)[1], 0, unroll=pairs - 2)
    for b in range(2):
        m_ref[b] = jnp.broadcast_to(jnp.max(m_ref[b], axis=0, keepdims=True), m_ref.shape[1:])
    acc_ref[...] = jnp.zeros_like(acc_ref)

    def weigh(t, c):
        qb, loc = table[2 * t], table[2 * t + 1]
        p = jnp.exp(s_ref[t] - m_ref[qb, 0:1]).astype(BF)
        p_ref[0, t] = p
        acc_ref[qb] += dot(key_block(v_ref, loc, blk), p, NN)
        return c

    lax.fori_loop(0, pairs, weigh, 0, unroll=pairs)
    for b in range(2):
        inv = 1.0 / acc_ref[b, HEAD : HEAD + 1]
        l_ref[0, b] = inv
        o_ref[0, b] = (acc_ref[b, :HEAD] * inv).astype(BF)


def attend_back_kernel(pairs, order, table, p_ref, q_ref, k_ref, v_ref, o_ref, do_ref, l_ref, cos_ref, sin_ref,
                       dq_ref, *rest):
    *outs, da_ref, dka_ref, dva_ref, dqa_ref = rest
    wide = q_ref.shape[-1]
    blk = wide // SHARE
    row = lax.broadcasted_iota(jnp.int32, (AUG - HEAD, wide), 0)
    for b in range(2):
        d = (do_ref[0, 0, b].astype(F32) * l_ref[0, b]).astype(BF)
        delta = -jnp.sum(d.astype(F32) * o_ref[0, b].astype(F32), axis=0, keepdims=True)
        hi = delta.astype(BF).astype(F32)
        mid = (delta - hi).astype(BF).astype(F32)
        low = delta - hi - mid
        da_ref[b, :HEAD] = d
        da_ref[b, HEAD:] = jnp.where(row == 0, hi, jnp.where(row == 1, mid, jnp.where(row == 2, low, 0.0))).astype(BF)
    dka_ref[...] = jnp.zeros_like(dka_ref)
    dva_ref[...] = jnp.zeros_like(dva_ref)
    dqa_ref[...] = jnp.zeros_like(dqa_ref)

    def step(t, c):
        qb, loc = table[2 * t], table[2 * t + 1]
        p = p_ref[0, t]
        dp = dot(key_block(v_ref, loc, blk), da_ref[qb], TN)
        ds = (p.astype(F32) * dp).astype(BF)
        dqa_ref[qb] += dot(key_block(k_ref, loc, blk, HEAD), ds, NN)
        dka_ref[loc] += dot(q_ref[0, qb, :HEAD], ds, NT)
        dva_ref[loc] += dot(da_ref[qb, :HEAD], p, NT)
        return c

    lax.fori_loop(0, pairs, step, 0, unroll=pairs)
    scale = 1.0 / math.sqrt(HEAD)
    for b in range(2):
        lanes = slice(b * blk, (b + 1) * blk)
        cos, sin = cos_ref[0, :, lanes] * scale, sin_ref[0, :, lanes] * scale
        for j in range(SHARE):
            dq_ref[0, j, :, lanes] = turn(dqa_ref[b, :, j * blk : (j + 1) * blk], cos, sin, 1, -1.0).astype(BF)
    n = len(order) // len(outs)
    for r, at in enumerate(order):
        out_ref = outs[at // n]
        for b in range(2):
            lanes = slice(b * blk, (b + 1) * blk)
            cos, sin = cos_ref[r, :, lanes], sin_ref[r, :, lanes]
            out_ref[at % n, 0, 0, :, lanes] = turn(dka_ref[2 * r + b], cos, sin, 1, -1.0).astype(BF)
            out_ref[at % n, 1, 0, :, lanes] = dva_ref[2 * r + b].astype(BF)


def solution(mesh):
    sizes = {name: mesh.shape[name] for name in ("dp", "ctx")}
    rows = P("dp", "ctx", None)
    grid = P("dp", "ctx")
    line = P("dp")
    return jax.shard_map(
        functools.partial(per_device, sizes),
        mesh=mesh,
        in_specs=(rows, grid, line, grid, grid, grid, grid, line, grid, grid, grid, rows),
        out_specs=(rows, rows, line, grid, grid, grid, grid, line, grid, grid, grid),
        check_vma=False,
    )
```

```python
import functools
import math

import jax
import jax.numpy as jnp
import numpy as np
from jax import lax
from jax.experimental import pallas as pl
from jax.experimental.pallas import tpu as pltpu
from jax.sharding import PartitionSpec as P

HEADS = 9
GROUPS = 3
SHARE = HEADS // GROUPS
HEAD = 64
HALF = HEAD // 2
AUG = HEAD + 16
EPS = 1e-05
ROPE_BASE = 100000.0
VMEM = 56 << 20
BF = jnp.bfloat16
F32 = jnp.float32


def params(semantics=None):
    return pltpu.CompilerParams(vmem_limit_bytes=VMEM, dimension_semantics=semantics)


def dot(a, b, dims):
    return lax.dot_general(a, b, (dims, ((), ())), preferred_element_type=F32)


NN = ((1,), (0,))
NT = ((1,), (1,))
TN = ((0,), (0,))


def swap(x, axis, size, mask):
    return lax.ppermute(x, axis, [(i, i ^ mask) for i in range(size)])


def bits_of(size):
    return [1 << k for k in range(size.bit_length() - 1)]


def spread(x, steps, sizes):
    x = x[None]
    for axis, bit in steps:
        x = jnp.concatenate([x, swap(x, axis, sizes[axis], bit)], axis=0)
    return x


def gather_up(x, steps, sizes):
    for axis, bit in reversed(steps):
        half = x.shape[0] // 2
        other = swap(x[half:], axis, sizes[axis], bit)
        x = (x[:half].astype(F32) + other.astype(F32)).astype(x.dtype)
    return x[0]


def slot_table(steps, axis, size, me):
    order = [bit for a, bit in steps if a == axis]
    rel = jnp.arange(size, dtype=jnp.int32) ^ me
    place = jnp.zeros_like(rel)
    for k, bit in enumerate(order):
        place = place | jnp.where((rel & bit) != 0, 1 << k, 0)
    return place


Z_MASKS = (2, 4, 6)


def stack_z(x, sizes):
    return jnp.stack([x] + [swap(x, "dp", sizes["dp"], m) for m in Z_MASKS])


def grow(x, axis, mask, sizes):
    return jnp.concatenate([x, swap(x, axis, sizes[axis], mask)], axis=0)


def add(keep, other):
    half = keep.shape[0] // 2
    plus = lambda a, b: (a.astype(F32) + b.astype(F32)).astype(BF)
    return plus(keep[:half], other[:half]), plus(keep[half:], other[half:])


def fold(keep, send, axis, mask, sizes):
    return add(keep, swap(send, axis, sizes[axis], mask))


def fold_z(lo, hi, sizes):
    parts = [lo[0], swap(lo[1], "dp", sizes["dp"], 2), swap(hi[0], "dp", sizes["dp"], 4), swap(hi[1], "dp", sizes["dp"], 6)]
    return sum(p.astype(F32) for p in parts)


def place_table(me_d, me_c):
    d = (jnp.arange(8, dtype=jnp.int32) ^ me_d)[:, None]
    c = (jnp.arange(4, dtype=jnp.int32) ^ me_c)[None, :]
    x, z, y = d & 1, d >> 1, c >> 1
    return (x * 8 + y * 4 + z).reshape(-1), (z * 4 + x * 2 + y).reshape(-1), jnp.broadcast_to(c & 1, (8, 4)).reshape(-1)


def fold_down(d):
    n = d.shape[0] // 2
    return jnp.concatenate([d[:n], d[n:]], axis=1)


def unfold_down(p):
    m = p.shape[1] // 2
    return jnp.concatenate([p[:, :m], p[:, m:]], axis=0)


def after_all(xs, *others):
    return lax.optimization_barrier(tuple(xs) + others)[: len(xs)]


def after(x, *others):
    return lax.optimization_barrier((x,) + others)[0]


def per_device(sizes, tokens, segments, attn_gain, query_weight, key_matrix, value_matrix,
               out_weight, mlp_gain, gate_weight, up_weight, down_weight, cotangent):
    nd, nc = sizes["dp"], sizes["ctx"]
    tokens, cotangent = jnp.swapaxes(tokens, 1, 2), jnp.swapaxes(cotangent, 1, 2)
    seqs, width, rows = tokens.shape
    blk = rows // 2
    me_d = lax.axis_index("dp")
    me_c = lax.axis_index("ctx")
    last = nc - 1
    kvd = GROUPS * HEAD
    qd = HEADS * HEAD
    qn, kn, fn = query_weight.shape[1], key_matrix.shape[1], gate_weight.shape[1]
    ff = fn * nc
    shard = width // nd
    box = nd == 8 and nc == 4
    csteps = [("ctx", b) for b in reversed(bits_of(nc))]
    wsteps = [("dp", b) for b in reversed(bits_of(nd))] + csteps

    ctx_bits = [b for _, b in csteps]

    def piece_rel(i):
        return sum(b for k, b in enumerate(ctx_bits) if i >> k & 1)

    place = {piece_rel(i): i for i in range(nc)}

    def balanced(all_pieces):
        rel = [all_pieces[place[r]] for r in range(nc)]
        return jnp.stack([jnp.concatenate([rel[r][..., :blk], rel[r ^ last][..., blk:]], axis=-1) for r in range(nc)])

    owner = me_c ^ jnp.arange(nc, dtype=jnp.int32)
    lane = jnp.arange(blk, dtype=jnp.int32)
    index = jnp.concatenate(
        [owner[:, None] * rows + lane[None], (last - owner[:, None]) * rows + blk + lane[None]], axis=1)
    inverse = ROPE_BASE ** (-2.0 * jnp.arange(HALF).astype(F32) / HEAD)

    def angles(seg_all, s):
        zseg = balanced(seg_all[:, s])
        before = jnp.where(zseg == 0, 0, jnp.where(zseg == 1, jnp.sum(zseg < 1), jnp.sum(zseg < 2)))
        phase = (index - before).astype(F32)[:, None, :] * inverse[None, :, None]
        return zseg[:, None, :], jnp.cos(phase), jnp.sin(phase)

    pad = lambda n: jnp.zeros((shard, n), BF)
    a_own = jnp.concatenate([query_weight, key_matrix, value_matrix, attn_gain[:, None], pad(15)], axis=1)
    b1_own = jnp.concatenate([gate_weight, up_weight], axis=1)
    b2_own = jnp.concatenate([out_weight, mlp_gain[:, None], pad(111)], axis=1)
    if box:
        b2_own = jnp.concatenate([b2_own, fold_down(down_weight.T)], axis=1)
        a_z = stack_z(a_own, sizes)
        b2_y = grow(b2_own[None], "ctx", 2, sizes)
        seg_y = grow(segments[None], "ctx", 2, sizes)
        a_z, b2_y, seg_y, tok = lax.optimization_barrier((a_z, b2_y, seg_y, tokens))
        a_y = grow(a_z, "ctx", 2, sizes)
        b2_x = grow(b2_y, "dp", 1, sizes)
        seg_all = grow(seg_y, "ctx", 1, sizes)
        tok0_y = grow(tok[0][None], "ctx", 2, sizes)
        a_y, b2_x, b1_own = lax.optimization_barrier((a_y, b2_x, b1_own))
        a_x = grow(a_y, "dp", 1, sizes)
        b1_z = stack_z(b1_own, sizes)
        tables = [angles(seg_all, s) for s in range(seqs)]
        a_x, tok0_y, tok, b1_z, tables = lax.optimization_barrier((a_x, tok0_y, tok, b1_z, tables))
        tokens_all = [(tok0_y, swap(tok0_y, "ctx", nc, 1))]
        a_parts = a_x, swap(a_x, "ctx", nc, 1)
        b1_got = swap(b1_z, "dp", nd, 1)
        tok1 = tok[1][None]
        tok1_got = swap(tok1, "ctx", nc, 2)
        at1, at2, other1 = place_table(me_d, me_c)
        places = jnp.concatenate([at1, at2, other1, me_c[None] & 1, me_c[None], me_d[None]])
        w_all = pl.pallas_call(
            unpack_a_kernel,
            in_specs=[pl.BlockSpec(memory_space=pltpu.SMEM)] + [pl.BlockSpec(memory_space=pltpu.VMEM)] * 2,
            out_specs=pl.BlockSpec(memory_space=pltpu.VMEM),
            out_shape=jax.ShapeDtypeStruct((nd, shard, 1024), BF),
            compiler_params=params(),
            name="unpack_a",
        )(places, *a_parts).reshape(width, 1024)
        b2_got = [swap(p, "dp", nd, m) for p, m in zip(after_all([b2_x] * 3, w_all), Z_MASKS)]

    if not box:
        dslot = slot_table(wsteps, "dp", nd, me_d)
        cslot = slot_table(wsteps, "ctx", nc, me_c)

        def whole(own):
            x = spread(own, wsteps, sizes)
            x = x.reshape((nc, nd) + own.shape)
            return jnp.take(jnp.take(x, cslot, axis=0), dslot, axis=1)

        def join(x):
            return x.transpose(1, 2, 0, 3).reshape(nd * x.shape[2], nc * x.shape[3])

        a = whole(a_own)
        w_all = jnp.concatenate(
            [join(a[..., :qn]), join(a[..., qn : qn + kn]), join(a[..., qn + kn : qn + 2 * kn]),
             a[0, :, :, 240:241].reshape(width, 1), jnp.zeros((width, 63), BF)], axis=1)
        b1 = whole(b1_own)
        b2 = whole(b2_own)
        wg, wu = join(b1[..., :fn]), join(b1[..., fn:])
        wo = jnp.concatenate([join(b2[..., :qn]), b2[0, :, :, qn : qn + 1].reshape(width, 1), jnp.zeros((width, 63), BF)], axis=1)
        wd = join(whole(down_weight)).T
        places = jnp.zeros((99,), jnp.int32)
        tokens_all = [spread(tokens[s], csteps, sizes) for s in range(seqs)]
        seg_all = spread(segments, csteps, sizes)
        tables = [angles(seg_all, s) for s in range(seqs)]
        tokens_all = [(v[: nc // 2], v[nc // 2 :]) for v in tokens_all]
        cot_got = swap(cotangent[..., blk:], "ctx", nc, last)

    table = jnp.asarray(pair_table(nc))[me_c].reshape(-1)
    pairs = 2 * nc + 1
    wide_q = SHARE * blk

    saved = []
    for s in range(seqs):
        tok_own, tok_got = tokens_all[s]
        zseg, cos_t, sin_t = tables[s]

        piece = lambda *tail: pl.BlockSpec((1,) + tail, lambda r: (r,) + (0,) * len(tail))
        fixed = lambda *shape: pl.BlockSpec(shape, lambda r: (0,) * len(shape))
        if s:
            tok_own = after(tok_own, prob)
        half = lambda at: pl.BlockSpec((1, width, blk), at)
        near = half(lambda r: (r // 2, 0, 0))
        opposite = half(lambda r: ((nc - 1 - r) // 2, 0, 1))
        h1, k_t, v_t, q_t, x_own = pl.pallas_call(
            pre_kernel,
            grid=(nc,),
            in_specs=[near, near, opposite, opposite, fixed(width, 1024), piece(HALF, rows), piece(HALF, rows), piece(1, rows)],
            out_specs=[piece(width, rows),
                       pl.BlockSpec((GROUPS, 1, AUG, rows), lambda r: (0, r, 0, 0)),
                       pl.BlockSpec((GROUPS, 1, AUG, rows), lambda r: (0, r, 0, 0)),
                       fixed(GROUPS, 2, AUG, wide_q), fixed(width, rows)],
            out_shape=[jax.ShapeDtypeStruct((nc, width, rows), BF),
                       jax.ShapeDtypeStruct((GROUPS, nc, AUG, rows), BF),
                       jax.ShapeDtypeStruct((GROUPS, nc, AUG, rows), BF),
                       jax.ShapeDtypeStruct((GROUPS, 2, AUG, wide_q), BF),
                       jax.ShapeDtypeStruct((width, rows), BF)],
            compiler_params=params(),
            cost_estimate=pl.CostEstimate(flops=4_500_000_000, bytes_accessed=10_000_000, transcendentals=0),
            name="pre",
        )(tok_own, tok_got, tok_own, tok_got, w_all, cos_t, sin_t, zseg)

        if box and s == 0:
            q_t, k_t, v_t, h1, x_own, b1_got, tok1_got = lax.optimization_barrier((q_t, k_t, v_t, h1, x_own, b1_got, tok1_got))
            b1_x = jnp.concatenate([b1_z, b1_got], axis=0)
            b1_got = swap(b1_x, "ctx", nc, 2)
            tok1_y = jnp.concatenate([tok1, tok1_got], axis=0)
            tokens_all.append((tok1_y, swap(tok1_y, "ctx", nc, 1)))
            q_t = after(q_t, b1_x, tok1_y)
        if box and s == 1:
            q_t, k_t, v_t, h1, x_own, b1_got, b2_got = lax.optimization_barrier((q_t, k_t, v_t, h1, x_own, b1_got, b2_got))
            b1_y = jnp.concatenate([b1_x, b1_got], axis=0)
            b2_z = jnp.concatenate([b2_x] + list(b2_got), axis=0)
            b1_far, b2_far = swap(b1_y, "ctx", nc, 1), swap(b2_z, "ctx", nc, 1)
            cot_got = swap(after(cotangent, q_t)[..., blk:], "ctx", nc, last)
            q_t = after(q_t, b1_y, b2_z)
        att = lambda *tail: pl.BlockSpec((1,) + tail, lambda g, t: (g,) + (0,) * len(tail))
        prob, o_t, inv_l = pl.pallas_call(
            functools.partial(attend_kernel, pairs),
            grid_spec=pltpu.PrefetchScalarGridSpec(
                num_scalar_prefetch=1,
                grid=(GROUPS,),
                in_specs=[att(2, AUG, wide_q), att(nc, AUG, rows), att(nc, AUG, rows)],
                out_specs=[att(pairs, blk, wide_q), att(2, HEAD, wide_q), att(2, 1, wide_q)],
                scratch_shapes=[pltpu.VMEM((pairs, blk, wide_q), F32), pltpu.VMEM((2, 8, wide_q), F32),
                                pltpu.VMEM((2, AUG, wide_q), F32)],
            ),
            out_shape=[jax.ShapeDtypeStruct((GROUPS, pairs, blk, wide_q), BF),
                       jax.ShapeDtypeStruct((GROUPS, 2, HEAD, wide_q), BF),
                       jax.ShapeDtypeStruct((GROUPS, 2, 1, wide_q), F32)],
            compiler_params=params(),
            cost_estimate=pl.CostEstimate(flops=12_000_000_000, bytes_accessed=12_000_000, transcendentals=0),
            name="attend",
        )(table, q_t, k_t, v_t)
        if box and s == 1:
            prob, o_t, inv_l, b1_far, b2_far, cot_got = lax.optimization_barrier((prob, o_t, inv_l, b1_far, b2_far, cot_got))
            weights = [v.reshape(2, 2, 4, shard, 2 * fn) for v in (b1_y, b1_far)]
            weights += [v.reshape(4, 2, 2, shard, 640) for v in (b2_z, b2_far)]
        saved.append((x_own, cos_t, sin_t, h1, k_t, v_t, q_t, prob, o_t, inv_l))

    total = seqs * rows
    steps = 2
    fstep = ff // steps
    once = lambda *shape: pl.BlockSpec(shape, lambda f, t: (0,) * len(shape), pipeline_mode=pl.Buffered(1))
    if box:
        weight_specs = [pl.BlockSpec((1, 2, 4, shard, 2 * fn), lambda f, t: (jnp.bitwise_xor(f, t[97] // 2), 0, 0, 0, 0))] * 2
        weight_specs += [once(4, 2, 2, shard, 640)] * 2
        weight_scratch = [pltpu.VMEM((width, fstep), BF)] * 3 + [pltpu.VMEM((width, 640), BF)]
    else:
        weights = [wg, wu, wd, wo]
        weight_specs = [pl.BlockSpec((width, fstep), lambda f, t: (0, f))] * 3 + [once(width, 640)]
        weight_scratch = []
    fixed = lambda *shape: pl.BlockSpec(shape, lambda f, t: (0,) * len(shape))
    if box:
        grad_specs = [fixed(16, shard, 2 * fn)] * 2 + [fixed(16, shard, 640)] * 2
        grad_shapes = [jax.ShapeDtypeStruct((16, shard, 2 * fn), BF)] * 2 + [jax.ShapeDtypeStruct((16, shard, 640), BF)] * 2
    else:
        grad_specs = [pl.BlockSpec((width, fstep), lambda f, t: (0, f))] * 2
        grad_specs += [pl.BlockSpec((width, fstep), lambda f, t: (0, f)), fixed(width, 640)]
        grad_shapes = [jax.ShapeDtypeStruct((width, ff), BF)] * 3 + [jax.ShapeDtypeStruct((width, 640), BF)]
    out_near, out_far, d_middle, do_t, *grads = pl.pallas_call(
        functools.partial(middle_kernel, box, nd, nc, seqs),
        grid_spec=pltpu.PrefetchScalarGridSpec(
            num_scalar_prefetch=1,
            grid=(steps,),
            in_specs=[once(width, rows), once(GROUPS, 2, HEAD, wide_q)] * seqs
            + [once(seqs, width, rows), once(seqs, width, blk)] + weight_specs,
            out_specs=[fixed(seqs, width, blk), fixed(seqs, width, blk), fixed(seqs, width, rows), fixed(seqs, GROUPS, 2, HEAD, wide_q)] + grad_specs,
            scratch_shapes=[pltpu.VMEM((qd, total), BF), pltpu.VMEM((width, total), F32), pltpu.VMEM((width, total), BF),
                            pltpu.VMEM((width, total), BF), pltpu.VMEM((width, total), F32), pltpu.VMEM((width, total), F32)]
            + weight_scratch,
        ),
        out_shape=[jax.ShapeDtypeStruct((seqs, width, blk), BF), jax.ShapeDtypeStruct((seqs, width, blk), BF),
                   jax.ShapeDtypeStruct((seqs, width, rows), F32),
                   jax.ShapeDtypeStruct((seqs, GROUPS, 2, HEAD, wide_q), BF)] + grad_shapes,
        compiler_params=params(),
        cost_estimate=pl.CostEstimate(flops=36_000_000_000, bytes_accessed=20_000_000, transcendentals=0),
        name="middle",
    )(places, *[v[k] for v in saved for k in (0, 8)], cotangent, cot_got, *weights)

    def settle(pieces):
        x = jnp.take(jnp.take(pieces, jnp.argsort(dslot), axis=0), jnp.argsort(cslot), axis=1)
        x = jnp.swapaxes(x, 0, 1).reshape((nc * nd,) + pieces.shape[2:])
        return gather_up(x, wsteps, sizes).astype(F32)

    def cut(g):
        r, c = g.shape
        return g.reshape(nd, r // nd, nc, c // nc).transpose(0, 2, 1, 3)

    def repeat(column):
        return jnp.broadcast_to(column.reshape(nd, 1, shard, 1), (nd, nc, shard, 1))

    if box:
        b1_got = swap(grads[1], "ctx", nc, 1)
        b2_got = swap(grads[3], "ctx", nc, 1)
    else:
        gate_sum, up_sum, down_sum = settle(cut(grads[0])), settle(cut(grads[1])), settle(cut(grads[2].T))
        b2_sum = settle(jnp.concatenate([cut(grads[3][:, :qd]), repeat(grads[3][:, qd])], axis=-1))
        out_sum, gain2_sum = b2_sum[:, :qn], b2_sum[:, qn]

    out_away = swap(out_far, "ctx", nc, last)
    half = nc // 2
    backs, dkv_owns = [], []
    for s in range(seqs):
        _, cos_t, sin_t, h1, k_t, v_t, q_t, prob, o_t, inv_l = saved[s]
        if s:
            q_t = after(q_t, backs[0][0], *((b1 + b2) if box else ()))
        att = lambda *tail: pl.BlockSpec((1,) + tail, lambda g, t: (g,) + (0,) * len(tail))
        fixed = lambda *shape: pl.BlockSpec(shape, lambda g, t: (0,) * len(shape))
        pair_of = pl.BlockSpec((1, 1, 2, HEAD, wide_q), lambda g, t: (s, g, 0, 0, 0))
        count = 1 if box and s == 0 else half
        kv_out = pl.BlockSpec((count, 2, 1, HEAD, rows), lambda g, t: (0, 0, g, 0, 0))
        dq_t, *kvs = pl.pallas_call(
            functools.partial(attend_back_kernel, pairs, tuple(place[r] for r in range(nc))),
            grid_spec=pltpu.PrefetchScalarGridSpec(
                num_scalar_prefetch=1,
                grid=(GROUPS,),
                in_specs=[att(pairs, blk, wide_q), att(2, AUG, wide_q), att(nc, AUG, rows), att(nc, AUG, rows),
                          att(2, HEAD, wide_q), pair_of, att(2, 1, wide_q), fixed(nc, HALF, rows), fixed(nc, HALF, rows)],
                out_specs=[att(SHARE, HEAD, rows)] + [kv_out] * (nc // count),
                scratch_shapes=[pltpu.VMEM((2, AUG, wide_q), BF), pltpu.VMEM((2 * nc, HEAD, blk), F32),
                                pltpu.VMEM((2 * nc, HEAD, blk), F32), pltpu.VMEM((2, HEAD, wide_q), F32)],
            ),
            out_shape=[jax.ShapeDtypeStruct((GROUPS, SHARE, HEAD, rows), BF)]
            + [jax.ShapeDtypeStruct((count, 2, GROUPS, HEAD, rows), BF)] * (nc // count),
            compiler_params=params(),
            cost_estimate=pl.CostEstimate(flops=20_000_000_000, bytes_accessed=12_000_000, transcendentals=0),
            name="attend_back",
        )(table, prob, q_t, k_t, v_t, o_t, do_t, inv_l, cos_t, sin_t)
        if box and s == 0:
            dq_t, b1_got, b2_got, out_away, *kvs = lax.optimization_barrier((dq_t, b1_got, b2_got, out_away, *kvs))
        if box and s == 1:
            dq_t, b1_got, z_got, dkv0, *kvs = lax.optimization_barrier((dq_t, b1_got, z_got, dkv0, *kvs))
            dkv_owns[0] = [dkv_owns[0][0]] + list(dkv0)
        kvs = [v.reshape(count, 2 * kvd, rows) for v in kvs]
        backs.append([dq_t.reshape(qd, rows), h1] + kvs)
        if box and s == 0:
            dkv0 = [swap(v, "ctx", nc, piece_rel(k)) for k, v in enumerate(kvs) if k]
            dkv_owns.append(kvs[:1])
            b1, b2 = add(grads[0], b1_got), add(grads[2], b2_got)
            b1_got = swap(b1[1], "dp", nd, 1)
            z_got = swap(b2[1][:4], "dp", nd, 4)
        else:
            dkv_got = swap(kvs[1], "ctx", nc, csteps[-1][1])
            if box:
                b1 = add(b1[0], b1_got)
                b1_got = swap(b1[1], "ctx", nc, 2)
                b2_parts = [b2[0][:4], z_got] + [swap(p, "dp", nd, m) for p, m in ((b2[0][4:], 2), (b2[1][4:], 6))]
            low, high = add(kvs[0], dkv_got)
            dkv_owns.append([low, swap(high, "ctx", nc, csteps[0][1])])

    def token(s, dqr_t):
        return pl.pallas_call(
            token_kernel,
            grid=(1,),
            in_specs=[pl.BlockSpec((1, 2 * kvd, rows), lambda i: (0, 0, 0))] * len(dkv_owns[s])
            + [pl.BlockSpec((qd, rows), lambda i: (0, 0)), pl.BlockSpec((width, 1024), lambda i: (0, 0)),
               pl.BlockSpec((width, rows), lambda i: (0, 0)), pl.BlockSpec((1, width, rows), lambda i: (s, 0, 0))],
            out_specs=[pl.BlockSpec((width, blk), lambda i: (0, 0))] * 2,
            out_shape=[jax.ShapeDtypeStruct((width, blk), BF)] * 2,
            compiler_params=params(),
            cost_estimate=pl.CostEstimate(flops=4_000_000_000, bytes_accessed=5_000_000, transcendentals=0),
            name="token",
        )(*dkv_owns[s], dqr_t, w_all, saved[s][0], d_middle)

    near0, far0 = token(0, after(backs[0][0], backs[1][0], dkv_owns[1][0], *((b1[0],) if box else ())))
    away0 = swap(far0, "ctx", nc, last)
    spot = [place[r] for r in range(nc)]
    hid_of = pl.BlockSpec((1, width, rows), lambda r, t: (t[99 + r], 0, 0))
    fixed = lambda *shape: pl.BlockSpec(shape, lambda r, t: (0,) * len(shape))
    if box:
        a_specs = [fixed(16, shard, 256)] * 2
        a_shapes = [jax.ShapeDtypeStruct((16, shard, 256), BF)] * 2
    else:
        a_specs, a_shapes = [fixed(width, 1024)], [jax.ShapeDtypeStruct((width, 1024), BF)]
    ops = [v for back in backs for v in back]
    ops[0] = after(ops[0], near0)
    places = jnp.concatenate([places, jnp.asarray([spot.index(i) for i in range(nc)], jnp.int32)])
    a_out = pl.pallas_call(
        functools.partial(post_kernel, box, nd, nc, tuple(len(v) for v in backs)),
        grid_spec=pltpu.PrefetchScalarGridSpec(
            num_scalar_prefetch=1,
            grid=(nc,),
            in_specs=[sp for back in backs for sp in [fixed(qd, rows), hid_of] + [fixed(*v.shape) for v in back[2:]]] + [fixed(width, 1024)],
            out_specs=a_specs,
            scratch_shapes=[pltpu.VMEM((width, 1024), F32)],
        ),
        out_shape=a_shapes,
        compiler_params=params(),
        cost_estimate=pl.CostEstimate(flops=15_000_000_000, bytes_accessed=10_000_000, transcendentals=0),
        name="post",
    )(places, *ops, w_all)

    if box:
        *a_out, b1_got, b2_parts, away0 = lax.optimization_barrier((*a_out, b1_got, b2_parts, away0))
        a_got = swap(a_out[1], "ctx", nc, 1)
        a_got, dkv_owns[1] = lax.optimization_barrier((a_got, dkv_owns[1]))
        total_of = lambda parts: sum(p.astype(F32) for p in parts)
        b2 = total_of(b2_parts).astype(BF)
        b2_got = swap(b2[2:], "dp", nd, 1)
        b1 = add(b1[0], b1_got)
        a = add(a_out[0], a_got)
        a_got = swap(a[1], "dp", nd, 1)
        b1_parts = [b1[0][0]] + [swap(p, "dp", nd, m) for p, m in zip((b1[0][1], b1[1][0], b1[1][1]), Z_MASKS)]
    mine, away = token(1, after(backs[1][0], *((a[0], b2[0]) if box else ())))
    if box:
        mine, away, a_got, b1_parts, b2_got = lax.optimization_barrier((mine, away, a_got, b1_parts, b2_got))
    token_near, token_away = [near0, mine], [away0, swap(away, "ctx", nc, last)]
    if box:
        a = add(a[0], a_got)
        b2 = (b2[:2].astype(F32) + b2_got.astype(F32)).astype(BF)
        b2_got = swap(b2[1], "ctx", nc, 2)
        a = fold(*a, "ctx", 2, sizes)
        a, token_away, b2_got = lax.optimization_barrier((a, token_away, b2_got))
        b1_sum = total_of(b1_parts)
        b2_sum = b2[0].astype(F32) + b2_got.astype(F32)
        gate_sum, up_sum = b1_sum[:, :fn], b1_sum[:, fn:]
        out_sum, gain2_sum, down_sum = b2_sum[:, :qn], b2_sum[:, qn], unfold_down(b2_sum[:, 256:]).T

    if box:
        a_sum = fold_z(*a, sizes)
    else:
        a = a_out[0]
        a_sum = settle(jnp.concatenate(
            [cut(a[:, :qd]), cut(a[:, qd : qd + kvd]), cut(a[:, qd + kvd : qd + 2 * kvd]), repeat(a[:, 960])], axis=-1))

    def home(mine, away):
        return jnp.swapaxes(jnp.concatenate([mine, away], axis=-1), 1, 2)

    return (
        home(out_near, out_away),
        home(jnp.stack(token_near), jnp.stack(token_away)),
        a_sum[:, 2 * kn + qn],
        a_sum[:, :qn],
        a_sum[:, qn : qn + kn],
        a_sum[:, qn + kn : qn + 2 * kn],
        out_sum,
        gain2_sum,
        gate_sum,
        up_sum,
        down_sum,
    )


def pair_table(nc):
    out = []
    for me in range(nc):
        spots = {}
        for r in range(nc):
            d = me ^ r
            spots[2 * d] = 2 * r
            spots[2 * (nc - 1 - d) + 1] = 2 * r + 1
        mine = [2 * me, 2 * (nc - 1 - me) + 1]
        rows = [(i, spots[mine[i]]) for i in range(2)]
        rows += [(i, spots[k]) for i in range(2) for k in range(mine[i])]
        out.append(rows)
    return np.array(out, np.int32)


def turn(x, cos, sin, heads, sign):
    parts = []
    for h in range(heads):
        lo, hi = x[h * HEAD : h * HEAD + HALF], x[h * HEAD + HALF : (h + 1) * HEAD]
        parts += [lo * cos - sign * hi * sin, hi * cos + sign * lo * sin]
    return jnp.concatenate(parts, axis=0)


def unpack_a_kernel(places, own_ref, other_ref, w_ref):
    nd = w_ref.shape[0]
    nc = 4
    qn, kn = 144, 48
    qd, kvd = qn * nc, kn * nc

    def write(cores):
        for d in range(nd):
            for c in range(nc):
                p = cores[c % 2][places[d * nc + c]].astype(F32)
                if c == 0:
                    cols = [[], [], []]
                    gain = p[:, 240:256]
                cols[0].append(p[:, :qn])
                cols[1].append(p[:, qn : qn + kn])
                cols[2].append(p[:, qn + kn : qn + 2 * kn])
            row = cols[0] + cols[1] + cols[2] + [gain, jnp.zeros((p.shape[0], 48), F32)]
            w_ref[d] = jnp.concatenate(row, axis=1).astype(BF)

    core = places[96]
    pl.when(core == 0)(lambda: write((own_ref, other_ref)))
    pl.when(core == 1)(lambda: write((other_ref, own_ref)))


def pre_kernel(own_ref, got_ref, own2_ref, got2_ref, w_ref, cos_ref, sin_ref, seg_ref, h_ref, k_ref, v_ref, q_ref, x_ref):
    mine = lax.rem(pl.program_id(0), 2) == 0
    x = jnp.concatenate([jnp.where(mine, own_ref[0].astype(F32), got_ref[0].astype(F32)),
                         jnp.where(mine, got2_ref[0].astype(F32), own2_ref[0].astype(F32))], axis=1)
    inv = lax.rsqrt(jnp.mean(x * x, axis=0, keepdims=True) + EPS)
    qd, kvd = HEADS * HEAD, GROUPS * HEAD
    gain = w_ref[:, qd + 2 * kvd : qd + 2 * kvd + 1].astype(F32)
    h = ((x * inv) * gain).astype(BF)
    h_ref[0] = h
    cos, sin, seg = cos_ref[0], sin_ref[0], seg_ref[0]
    rows = x.shape[1]
    blk = rows // 2
    kv = dot(w_ref[:, qd : qd + 2 * kvd], h, TN)
    keys = turn(kv[:kvd], cos, sin, GROUPS, 1.0).astype(BF)
    values = kv[kvd:].astype(BF)
    row = lax.broadcasted_iota(jnp.int32, (AUG - HEAD, rows), 0)
    other = jnp.where((row < 3) & (row != seg), -1e30, 0.0).astype(BF)
    ones = (row < 3).astype(BF)
    for g in range(GROUPS):
        k_ref[g, 0, :HEAD] = keys[g * HEAD : (g + 1) * HEAD]
        k_ref[g, 0, HEAD:] = other
        v_ref[g, 0, :HEAD] = values[g * HEAD : (g + 1) * HEAD]
        v_ref[g, 0, HEAD:] = ones

    @pl.when(pl.program_id(0) == 0)
    def _():
        q = turn(dot(w_ref[:, :qd], h, TN), cos, sin, HEADS, 1.0).astype(BF) * (1.0 / math.sqrt(HEAD))
        x_ref[...] = x.astype(BF)
        same = (row == seg).astype(BF)
        for g in range(GROUPS):
            for b in range(2):
                for j in range(SHARE):
                    n = g * SHARE + j
                    q_ref[g, b, :HEAD, j * blk : (j + 1) * blk] = q[n * HEAD : (n + 1) * HEAD, b * blk : (b + 1) * blk]
                    q_ref[g, b, HEAD:, j * blk : (j + 1) * blk] = same[:, b * blk : (b + 1) * blk]


def by_core(core, refs, write):
    pairs = [refs[i : i + 2] for i in range(0, len(refs), 2)]
    pl.when(core == 0)(lambda: write(*pairs))
    pl.when(core == 1)(lambda: write(*[p[::-1] for p in pairs]))


def join_weights(places, f, g_ref, u_ref, w_ref, o_ref, one, two):
    fn = one[0].shape[-1] // 2
    me_y, me_x, me_z = places[97] // 2, places[98] % 2, places[98] // 2
    flip = jnp.bitwise_xor
    high = one[0].shape[-2]

    def stack(ref, i, rows):
        ref[2 * high * i : 2 * high * (i + 1)] = jnp.concatenate(rows, axis=0).astype(BF)

    for z in range(4):
        at_z = flip(z, me_z)
        rows = [[one[k][0, flip(x, me_x), at_z].astype(F32) for k in range(2)] for x in range(2)]
        stack(g_ref, z, [jnp.concatenate([p[:, :fn] for p in row], axis=1) for row in rows])
        stack(u_ref, z, [jnp.concatenate([p[:, fn:] for p in row], axis=1) for row in rows])
    for c in range(4):
        y = flip(c // 2, me_y)
        pieces = [two[c % 2][flip(2 * f + i // 2, me_z), flip(i % 2, me_x), y, :, 256:640].astype(F32) for i in range(4)]
        stack(w_ref, c, [jnp.concatenate([p[:, j * 192 : (j + 1) * 192] for p in pieces], axis=1) for j in range(2)])

    @pl.when(f == 0)
    def _():
        for z in range(4):
            rows = []
            for x in range(2):
                pieces = [two[c % 2][flip(z, me_z), flip(x, me_x), flip(c // 2, me_y), :, :256].astype(F32) for c in range(4)]
                rows.append(jnp.concatenate([p[:, :144] for p in pieces] + [pieces[0][:, 144:208]], axis=1))
            stack(o_ref, z, rows)


def middle_kernel(box, nd, nc, seqs, places, *refs):
    xs, refs = refs[: 2 * seqs], refs[2 * seqs :]
    cot_ref, got_ref, wg_ref, wu_ref, wd_ref, wo_ref, near_ref, far_ref, dm_ref, do_ref, *rest = refs
    grads, (att_ref, mid_ref, h_ref, cots_ref, acc_ref, dh_ref), made = rest[:4], rest[4:10], rest[10:]
    f = pl.program_id(0)
    if box:
        parts = (wg_ref, wu_ref, wd_ref, wo_ref)
        wg_ref, wu_ref, wd_ref, wo_ref = made
        by_core(places[96], parts, functools.partial(join_weights, places, f, *made))
    blk = got_ref.shape[2]
    rows = 2 * blk
    qd, width = HEADS * HEAD, cot_ref.shape[1]
    shard = width // nd
    fn = wg_ref.shape[1]
    steps = 2
    part_fn = fn * steps // nc

    def norm():
        m = mid_ref[...]
        inv = lax.rsqrt(jnp.mean(m * m, axis=0, keepdims=True) + EPS)
        return m, inv, m * inv

    def gain_column():
        return wo_ref[:, qd : qd + 1].astype(F32)

    def of(s):
        return slice(s * rows, (s + 1) * rows)

    def blocks():
        for s in range(seqs):
            for g in range(GROUPS):
                for b in range(2):
                    for j in range(SHARE):
                        n = g * SHARE + j
                        yield (s, g, b, slice(None), slice(j * blk, (j + 1) * blk)), (
                            slice(n * HEAD, (n + 1) * HEAD), slice(s * rows + b * blk, s * rows + (b + 1) * blk))

    @pl.when(f == 0)
    def _():
        for there, here in blocks():
            att_ref[here] = xs[2 * there[0] + 1][there[1:]]
        branch = dot(wo_ref[:, :qd], att_ref[...], TN)
        for s in range(seqs):
            mid_ref[:, of(s)] = xs[2 * s][...].astype(F32) + branch[:, of(s)]
            cots_ref[:, s * rows : s * rows + blk] = cot_ref[s, :, :blk]
            cots_ref[:, s * rows + blk : (s + 1) * rows] = got_ref[s]
        _, _, n2 = norm()
        h_ref[...] = (n2 * gain_column()).astype(BF)

    h = h_ref[...]
    cot = cots_ref[...]
    gate = dot(wg_ref[...], h, TN)
    up = dot(wu_ref[...], h, TN)
    sig = jax.nn.sigmoid(gate)
    act = gate * sig
    inner = (act * up).astype(BF)
    part = dot(wd_ref[...], inner, NN)
    d_inner = dot(wd_ref[...], cot, TN)
    d_gate = (d_inner * up * (sig + act * (1.0 - sig))).astype(BF)
    d_up = (d_inner * act).astype(BF)
    d_part = dot(wg_ref[...], d_gate, NN) + dot(wu_ref[...], d_up, NN)

    @pl.when(f == 0)
    def _():
        acc_ref[...] = part
        dh_ref[...] = d_part

    @pl.when(f > 0)
    def _():
        acc_ref[...] += part
        dh_ref[...] += d_part

    grad_gate = dot(h, d_gate, NT)
    grad_up = dot(h, d_up, NT)
    grad_down = dot(cot, inner, NT)
    if box:
        cols = width // nc
        per = fn * steps // nd

        def pack(b1s, b2s):
            for k in range(nc // steps):
                c = f * (nc // steps) + k
                lanes = slice(k * part_fn, (k + 1) * part_fn)
                for d in range(nd):
                    part_rows = slice(d * shard, (d + 1) * shard)
                    at = places[d * nc + c]
                    b1s[k % 2][at, :, :part_fn] = grad_gate[part_rows, lanes].astype(BF)
                    b1s[k % 2][at, :, part_fn:] = grad_up[part_rows, lanes].astype(BF)
            for i in range(fn // per):
                for c in range(nc):
                    p = fold_down(grad_down[c * cols : (c + 1) * cols, i * per : (i + 1) * per]).astype(BF)
                    b2s[c % 2][places[32 + (f * (fn // per) + i) * nc + c], :, 256:640] = p

        by_core(places[96], grads, pack)
    else:
        grads[0][...] = grad_gate.astype(BF)
        grads[1][...] = grad_up.astype(BF)
        grads[2][...] = grad_down.astype(BF)

    @pl.when(f == pl.num_programs(0) - 1)
    def _():
        m, inv, n2 = norm()
        out = (m + acc_ref[...]).astype(BF)
        d_h2 = dh_ref[...]
        e2 = d_h2 * gain_column()
        d_middle = cots_ref[...].astype(F32) + inv * (e2 - n2 * jnp.mean(e2 * n2, axis=0, keepdims=True))
        for s in range(seqs):
            near_ref[s] = out[:, s * rows : s * rows + blk]
            far_ref[s] = out[:, s * rows + blk : (s + 1) * rows]
            dm_ref[s] = d_middle[:, of(s)]
        branch = d_middle.astype(BF)
        d_att = dot(wo_ref[:, :qd], branch, NN).astype(BF)
        for there, here in blocks():
            do_ref[there] = d_att[here]
        grad_out = dot(att_ref[...], branch, NT)
        gain = jnp.broadcast_to(jnp.sum(d_h2 * n2, axis=1, keepdims=True), (width, 128))
        if box:
            def pack_out(b1s, b2s):
                for d in range(nd):
                    part_rows = slice(d * shard, (d + 1) * shard)
                    for c in range(nc):
                        p = jnp.concatenate([grad_out[part_rows, c * cols : (c + 1) * cols], gain[part_rows, :112]], axis=1)
                        b2s[c % 2][places[32 + d * nc + c], :, :256] = p.astype(BF)

            by_core(places[96], grads, pack_out)
        else:
            grads[3][...] = jnp.concatenate([grad_out, gain[:, :64]], axis=1).astype(BF)


def post_kernel(box, nd, nc, counts, places, *refs):
    seqs = []
    for n in counts:
        seqs.append(refs[:n])
        refs = refs[n:]
    w_ref, outs, acc_ref = refs[0], refs[1:-1], refs[-1]
    kvd, qd = GROUPS * HEAD, HEADS * HEAD
    r = pl.program_id(0)

    @pl.when(r == 0)
    def _():
        acc_ref[...] = jnp.zeros_like(acc_ref)
        acc_ref[:, :qd] = sum(dot(h_ref[0], dq_ref[...], NT) for dq_ref, h_ref, *_ in seqs)

    for k in range(nc):
        @pl.when(r == k)
        def _():
            terms = []
            for _, h_ref, *kvs in seqs:
                n = nc // len(kvs)
                terms.append(dot(h_ref[0], kvs[k // n][k % n], NT))
            acc_ref[:, qd : qd + 2 * kvd] += sum(terms)

    @pl.when(r == nc - 1)
    def _():
        g = acc_ref[...]
        w = w_ref[...].astype(F32)
        used = qd + 2 * kvd
        gain = jnp.sum(g[:, :used] * w[:, :used], axis=1, keepdims=True) / w[:, used : used + 1]
        if not box:
            outs[0][...] = jnp.concatenate([g[:, :used], jnp.broadcast_to(gain, (g.shape[0], 64))], axis=1).astype(BF)
            return
        shard = g.shape[0] // nd
        gain = jnp.broadcast_to(gain, (g.shape[0], 16))
        qn, kn = qd // nc, kvd // nc

        def pack(both):
            for d in range(nd):
                r = slice(d * shard, (d + 1) * shard)
                for c in range(nc):
                    p = jnp.concatenate(
                        [g[r, c * qn : (c + 1) * qn], g[r, qd + c * kn : qd + (c + 1) * kn],
                         g[r, qd + kvd + c * kn : qd + kvd + (c + 1) * kn], gain[r]], axis=1)
                    both[c % 2][places[d * nc + c]] = p.astype(BF)

        by_core(places[96], outs, pack)


def token_kernel(*refs):
    *kvs, dq_ref, w_ref, x_ref, dm_ref, near_ref, far_ref = refs
    qd, kvd = HEADS * HEAD, GROUPS * HEAD
    x = x_ref[...].astype(F32)
    inv = lax.rsqrt(jnp.mean(x * x, axis=0, keepdims=True) + EPS)
    n1 = x * inv
    dkv = sum(v[0].astype(F32) for v in kvs).astype(BF)
    d_h1 = dot(w_ref[:, :qd], dq_ref[...], NN) + dot(w_ref[:, qd : qd + 2 * kvd], dkv, NN)
    e1 = d_h1 * w_ref[:, qd + 2 * kvd : qd + 2 * kvd + 1].astype(F32)
    out = (dm_ref[0] + inv * (e1 - n1 * jnp.mean(e1 * n1, axis=0, keepdims=True))).astype(BF)
    blk = near_ref.shape[1]
    near_ref[...] = out[:, :blk]
    far_ref[...] = out[:, blk:]


def key_block(ref, loc, blk, rows=None):
    r, half = loc // 2, loc % 2
    lanes = pl.ds(pl.multiple_of(half * blk, blk), blk)
    if rows is None:
        return ref[0, r, :, lanes]
    return ref[0, r, :rows, lanes]


def attend_kernel(pairs, table, q_ref, k_ref, v_ref, p_ref, o_ref, l_ref, s_ref, m_ref, acc_ref):
    wide = q_ref.shape[-1]
    blk = wide // SHARE

    def score(t, diagonal):
        qb, loc = table[2 * t], table[2 * t + 1]
        s = dot(key_block(k_ref, loc, blk), q_ref[0, qb], TN)
        if diagonal:
            k_at = lax.broadcasted_iota(jnp.int32, (blk, wide), 0)
            q_at = lax.broadcasted_iota(jnp.int32, (blk, wide), 1) % blk
            s = jnp.where(k_at <= q_at, s, -1e30)
        s_ref[t] = s
        top = jnp.max(s.reshape(blk // 8, 8, wide), axis=0)
        if diagonal:
            m_ref[qb] = top
        else:
            m_ref[qb] = jnp.maximum(m_ref[qb], top)

    for t in range(2):
        score(t, True)
    lax.fori_loop(2, pairs, lambda t, c: (score(t, False), c)[1], 0, unroll=pairs - 2)
    for b in range(2):
        m_ref[b] = jnp.broadcast_to(jnp.max(m_ref[b], axis=0, keepdims=True), m_ref.shape[1:])
    acc_ref[...] = jnp.zeros_like(acc_ref)

    def weigh(t, c):
        qb, loc = table[2 * t], table[2 * t + 1]
        p = jnp.exp(s_ref[t] - m_ref[qb, 0:1]).astype(BF)
        p_ref[0, t] = p
        acc_ref[qb] += dot(key_block(v_ref, loc, blk), p, NN)
        return c

    lax.fori_loop(0, pairs, weigh, 0, unroll=pairs)
    for b in range(2):
        inv = 1.0 / acc_ref[b, HEAD : HEAD + 1]
        l_ref[0, b] = inv
        o_ref[0, b] = (acc_ref[b, :HEAD] * inv).astype(BF)


def attend_back_kernel(pairs, order, table, p_ref, q_ref, k_ref, v_ref, o_ref, do_ref, l_ref, cos_ref, sin_ref,
                       dq_ref, *rest):
    *outs, da_ref, dka_ref, dva_ref, dqa_ref = rest
    wide = q_ref.shape[-1]
    blk = wide // SHARE
    row = lax.broadcasted_iota(jnp.int32, (AUG - HEAD, wide), 0)
    for b in range(2):
        d = (do_ref[0, 0, b].astype(F32) * l_ref[0, b]).astype(BF)
        delta = -jnp.sum(d.astype(F32) * o_ref[0, b].astype(F32), axis=0, keepdims=True)
        hi = delta.astype(BF).astype(F32)
        mid = (delta - hi).astype(BF).astype(F32)
        low = delta - hi - mid
        da_ref[b, :HEAD] = d
        da_ref[b, HEAD:] = jnp.where(row == 0, hi, jnp.where(row == 1, mid, jnp.where(row == 2, low, 0.0))).astype(BF)
    dka_ref[...] = jnp.zeros_like(dka_ref)
    dva_ref[...] = jnp.zeros_like(dva_ref)
    dqa_ref[...] = jnp.zeros_like(dqa_ref)

    def step(t, c):
        qb, loc = table[2 * t], table[2 * t + 1]
        p = p_ref[0, t]
        dp = dot(key_block(v_ref, loc, blk), da_ref[qb], TN)
        ds = (p.astype(F32) * dp).astype(BF)
        dqa_ref[qb] += dot(key_block(k_ref, loc, blk, HEAD), ds, NN)
        dka_ref[loc] += dot(q_ref[0, qb, :HEAD], ds, NT)
        dva_ref[loc] += dot(da_ref[qb, :HEAD], p, NT)
        return c

    lax.fori_loop(0, pairs, step, 0, unroll=pairs)
    scale = 1.0 / math.sqrt(HEAD)
    for b in range(2):
        lanes = slice(b * blk, (b + 1) * blk)
        cos, sin = cos_ref[0, :, lanes] * scale, sin_ref[0, :, lanes] * scale
        for j in range(SHARE):
            dq_ref[0, j, :, lanes] = turn(dqa_ref[b, :, j * blk : (j + 1) * blk], cos, sin, 1, -1.0).astype(BF)
    n = len(order) // len(outs)
    for r, at in enumerate(order):
        out_ref = outs[at // n]
        for b in range(2):
            lanes = slice(b * blk, (b + 1) * blk)
            cos, sin = cos_ref[r, :, lanes], sin_ref[r, :, lanes]
            out_ref[at % n, 0, 0, :, lanes] = turn(dka_ref[2 * r + b], cos, sin, 1, -1.0).astype(BF)
            out_ref[at % n, 1, 0, :, lanes] = dva_ref[2 * r + b].astype(BF)


def solution(mesh):
    sizes = {name: mesh.shape[name] for name in ("dp", "ctx")}
    rows = P("dp", "ctx", None)
    grid = P("dp", "ctx")
    line = P("dp")
    return jax.shard_map(
        functools.partial(per_device, sizes),
        mesh=mesh,
        in_specs=(rows, grid, line, grid, grid, grid, grid, line, grid, grid, grid, rows),
        out_specs=(rows, rows, line, grid, grid, grid, grid, line, grid, grid, grid),
        check_vma=False,
    )
```

```python
import functools
import math

import jax
import jax.numpy as jnp
import numpy as np
from jax import lax
from jax.experimental import pallas as pl
from jax.experimental.pallas import tpu as pltpu
from jax.sharding import PartitionSpec as P

HEADS = 9
GROUPS = 3
SHARE = HEADS // GROUPS
HEAD = 64
HALF = HEAD // 2
AUG = HEAD + 16
EPS = 1e-05
ROPE_BASE = 100000.0
VMEM = 56 << 20
BF = jnp.bfloat16
F32 = jnp.float32


def params(semantics=None):
    return pltpu.CompilerParams(vmem_limit_bytes=VMEM, dimension_semantics=semantics)


def dot(a, b, dims):
    return lax.dot_general(a, b, (dims, ((), ())), preferred_element_type=F32)


NN = ((1,), (0,))
NT = ((1,), (1,))
TN = ((0,), (0,))


def swap(x, axis, size, mask):
    return lax.ppermute(x, axis, [(i, i ^ mask) for i in range(size)])


def bits_of(size):
    return [1 << k for k in range(size.bit_length() - 1)]


def spread(x, steps, sizes):
    x = x[None]
    for axis, bit in steps:
        x = jnp.concatenate([x, swap(x, axis, sizes[axis], bit)], axis=0)
    return x


def gather_up(x, steps, sizes):
    for axis, bit in reversed(steps):
        half = x.shape[0] // 2
        other = swap(x[half:], axis, sizes[axis], bit)
        x = (x[:half].astype(F32) + other.astype(F32)).astype(x.dtype)
    return x[0]


def slot_table(steps, axis, size, me):
    order = [bit for a, bit in steps if a == axis]
    rel = jnp.arange(size, dtype=jnp.int32) ^ me
    place = jnp.zeros_like(rel)
    for k, bit in enumerate(order):
        place = place | jnp.where((rel & bit) != 0, 1 << k, 0)
    return place


Z_MASKS = (2, 4, 6)


def stack_z(x, sizes):
    return jnp.stack([x] + [swap(x, "dp", sizes["dp"], m) for m in Z_MASKS])


def grow(x, axis, mask, sizes):
    return jnp.concatenate([x, swap(x, axis, sizes[axis], mask)], axis=0)


def add(keep, other):
    half = keep.shape[0] // 2
    plus = lambda a, b: (a.astype(F32) + b.astype(F32)).astype(BF)
    return plus(keep[:half], other[:half]), plus(keep[half:], other[half:])


def fold(keep, send, axis, mask, sizes):
    return add(keep, swap(send, axis, sizes[axis], mask))


def fold_z(lo, hi, sizes):
    parts = [lo[0], swap(lo[1], "dp", sizes["dp"], 2), swap(hi[0], "dp", sizes["dp"], 4), swap(hi[1], "dp", sizes["dp"], 6)]
    return sum(p.astype(F32) for p in parts)


def place_table(me_d, me_c):
    d = (jnp.arange(8, dtype=jnp.int32) ^ me_d)[:, None]
    c = (jnp.arange(4, dtype=jnp.int32) ^ me_c)[None, :]
    x, z, y = d & 1, d >> 1, c >> 1
    return (x * 8 + y * 4 + z).reshape(-1), (z * 4 + x * 2 + y).reshape(-1), jnp.broadcast_to(c & 1, (8, 4)).reshape(-1)


def fold_down(d):
    n = d.shape[0] // 2
    return jnp.concatenate([d[:n], d[n:]], axis=1)


def unfold_down(p):
    m = p.shape[1] // 2
    return jnp.concatenate([p[:, :m], p[:, m:]], axis=0)


def after_all(xs, *others):
    return lax.optimization_barrier(tuple(xs) + others)[: len(xs)]


def after(x, *others):
    return lax.optimization_barrier((x,) + others)[0]


def per_device(sizes, tokens, segments, attn_gain, query_weight, key_matrix, value_matrix,
               out_weight, mlp_gain, gate_weight, up_weight, down_weight, cotangent):
    nd, nc = sizes["dp"], sizes["ctx"]
    tokens, cotangent = jnp.swapaxes(tokens, 1, 2), jnp.swapaxes(cotangent, 1, 2)
    seqs, width, rows = tokens.shape
    blk = rows // 2
    me_d = lax.axis_index("dp")
    me_c = lax.axis_index("ctx")
    last = nc - 1
    kvd = GROUPS * HEAD
    qd = HEADS * HEAD
    qn, kn, fn = query_weight.shape[1], key_matrix.shape[1], gate_weight.shape[1]
    ff = fn * nc
    shard = width // nd
    box = nd == 8 and nc == 4
    csteps = [("ctx", b) for b in reversed(bits_of(nc))]
    wsteps = [("dp", b) for b in reversed(bits_of(nd))] + csteps

    ctx_bits = [b for _, b in csteps]

    def piece_rel(i):
        return sum(b for k, b in enumerate(ctx_bits) if i >> k & 1)

    place = {piece_rel(i): i for i in range(nc)}

    def balanced(all_pieces):
        rel = [all_pieces[place[r]] for r in range(nc)]
        return jnp.stack([jnp.concatenate([rel[r][..., :blk], rel[r ^ last][..., blk:]], axis=-1) for r in range(nc)])

    owner = me_c ^ jnp.arange(nc, dtype=jnp.int32)
    lane = jnp.arange(blk, dtype=jnp.int32)
    index = jnp.concatenate(
        [owner[:, None] * rows + lane[None], (last - owner[:, None]) * rows + blk + lane[None]], axis=1)
    inverse = ROPE_BASE ** (-2.0 * jnp.arange(HALF).astype(F32) / HEAD)

    def angles(seg_all, s):
        zseg = balanced(seg_all[:, s])
        before = jnp.where(zseg == 0, 0, jnp.where(zseg == 1, jnp.sum(zseg < 1), jnp.sum(zseg < 2)))
        phase = (index - before).astype(F32)[:, None, :] * inverse[None, :, None]
        return zseg[:, None, :], jnp.cos(phase), jnp.sin(phase)

    pad = lambda n: jnp.zeros((shard, n), BF)
    a_own = jnp.concatenate([query_weight, key_matrix, value_matrix, attn_gain[:, None], pad(15)], axis=1)
    b1_own = jnp.concatenate([gate_weight, up_weight], axis=1)
    b2_own = jnp.concatenate([out_weight, mlp_gain[:, None], pad(111)], axis=1)
    if box:
        b2_own = jnp.concatenate([b2_own, fold_down(down_weight.T)], axis=1)
        a_z = stack_z(a_own, sizes)
        b2_y = grow(b2_own[None], "ctx", 2, sizes)
        seg_y = grow(segments[None], "ctx", 2, sizes)
        a_z, b2_y, seg_y, tok = lax.optimization_barrier((a_z, b2_y, seg_y, tokens))
        a_y = grow(a_z, "ctx", 2, sizes)
        b2_x = grow(b2_y, "dp", 1, sizes)
        seg_all = grow(seg_y, "ctx", 1, sizes)
        tok0_y = grow(tok[0][None], "ctx", 2, sizes)
        a_y, b2_x, b1_own = lax.optimization_barrier((a_y, b2_x, b1_own))
        a_x = grow(a_y, "dp", 1, sizes)
        b1_z = stack_z(b1_own, sizes)
        tables = [angles(seg_all, s) for s in range(seqs)]
        a_x, tok0_y, tok, b1_z, tables = lax.optimization_barrier((a_x, tok0_y, tok, b1_z, tables))
        tokens_all = [(tok0_y, swap(tok0_y, "ctx", nc, 1))]
        a_parts = a_x, swap(a_x, "ctx", nc, 1)
        b1_got = swap(b1_z, "dp", nd, 1)
        tok1 = tok[1][None]
        tok1_got = swap(tok1, "ctx", nc, 2)
        at1, at2, other1 = place_table(me_d, me_c)
        places = jnp.concatenate([at1, at2, other1, me_c[None] & 1, me_c[None], me_d[None]])
        w_all = pl.pallas_call(
            unpack_a_kernel,
            in_specs=[pl.BlockSpec(memory_space=pltpu.SMEM)] + [pl.BlockSpec(memory_space=pltpu.VMEM)] * 2,
            out_specs=pl.BlockSpec(memory_space=pltpu.VMEM),
            out_shape=jax.ShapeDtypeStruct((nd, shard, 1024), BF),
            compiler_params=params(),
            name="unpack_a",
        )(places, *a_parts).reshape(width, 1024)
        b2_got = [swap(p, "dp", nd, m) for p, m in zip(after_all([b2_x] * 3, w_all), Z_MASKS)]

    if not box:
        dslot = slot_table(wsteps, "dp", nd, me_d)
        cslot = slot_table(wsteps, "ctx", nc, me_c)

        def whole(own):
            x = spread(own, wsteps, sizes)
            x = x.reshape((nc, nd) + own.shape)
            return jnp.take(jnp.take(x, cslot, axis=0), dslot, axis=1)

        def join(x):
            return x.transpose(1, 2, 0, 3).reshape(nd * x.shape[2], nc * x.shape[3])

        a = whole(a_own)
        w_all = jnp.concatenate(
            [join(a[..., :qn]), join(a[..., qn : qn + kn]), join(a[..., qn + kn : qn + 2 * kn]),
             a[0, :, :, 240:241].reshape(width, 1), jnp.zeros((width, 63), BF)], axis=1)
        b1 = whole(b1_own)
        b2 = whole(b2_own)
        wg, wu = join(b1[..., :fn]), join(b1[..., fn:])
        wo = jnp.concatenate([join(b2[..., :qn]), b2[0, :, :, qn : qn + 1].reshape(width, 1), jnp.zeros((width, 63), BF)], axis=1)
        wd = join(whole(down_weight)).T
        places = jnp.zeros((99,), jnp.int32)
        tokens_all = [spread(tokens[s], csteps, sizes) for s in range(seqs)]
        seg_all = spread(segments, csteps, sizes)
        tables = [angles(seg_all, s) for s in range(seqs)]
        tokens_all = [(v[: nc // 2], v[nc // 2 :]) for v in tokens_all]
        cot_got = swap(cotangent[..., blk:], "ctx", nc, last)

    table = jnp.asarray(pair_table(nc))[me_c].reshape(-1)
    pairs = 2 * nc + 1
    wide_q = SHARE * blk

    saved = []
    for s in range(seqs):
        tok_own, tok_got = tokens_all[s]
        zseg, cos_t, sin_t = tables[s]

        piece = lambda *tail: pl.BlockSpec((1,) + tail, lambda r: (r,) + (0,) * len(tail))
        fixed = lambda *shape: pl.BlockSpec(shape, lambda r: (0,) * len(shape))
        if s:
            tok_own = after(tok_own, prob)
        half = lambda at: pl.BlockSpec((1, width, blk), at)
        near = half(lambda r: (r // 2, 0, 0))
        opposite = half(lambda r: ((nc - 1 - r) // 2, 0, 1))
        h1, k_t, v_t, q_t, x_own = pl.pallas_call(
            pre_kernel,
            grid=(nc,),
            in_specs=[near, near, opposite, opposite, fixed(width, 1024), piece(HALF, rows), piece(HALF, rows), piece(1, rows)],
            out_specs=[piece(width, rows),
                       pl.BlockSpec((GROUPS, 1, AUG, rows), lambda r: (0, r, 0, 0)),
                       pl.BlockSpec((GROUPS, 1, AUG, rows), lambda r: (0, r, 0, 0)),
                       fixed(GROUPS, 2, AUG, wide_q), fixed(width, rows)],
            out_shape=[jax.ShapeDtypeStruct((nc, width, rows), BF),
                       jax.ShapeDtypeStruct((GROUPS, nc, AUG, rows), BF),
                       jax.ShapeDtypeStruct((GROUPS, nc, AUG, rows), BF),
                       jax.ShapeDtypeStruct((GROUPS, 2, AUG, wide_q), BF),
                       jax.ShapeDtypeStruct((width, rows), BF)],
            compiler_params=params(),
            cost_estimate=pl.CostEstimate(flops=4_500_000_000, bytes_accessed=10_000_000, transcendentals=0),
            name="pre",
        )(tok_own, tok_got, tok_own, tok_got, w_all, cos_t, sin_t, zseg)

        if box and s == 0:
            q_t, k_t, v_t, h1, x_own, b1_got, tok1_got = lax.optimization_barrier((q_t, k_t, v_t, h1, x_own, b1_got, tok1_got))
            b1_x = jnp.concatenate([b1_z, b1_got], axis=0)
            b1_got = swap(b1_x, "ctx", nc, 2)
            tok1_y = jnp.concatenate([tok1, tok1_got], axis=0)
            tokens_all.append((tok1_y, swap(tok1_y, "ctx", nc, 1)))
            q_t = after(q_t, b1_x, tok1_y)
        if box and s == 1:
            q_t, k_t, v_t, h1, x_own, b1_got, b2_got = lax.optimization_barrier((q_t, k_t, v_t, h1, x_own, b1_got, b2_got))
            b1_y = jnp.concatenate([b1_x, b1_got], axis=0)
            b2_z = jnp.concatenate([b2_x] + list(b2_got), axis=0)
            b1_far, b2_far = swap(b1_y, "ctx", nc, 1), swap(b2_z, "ctx", nc, 1)
            cot_got = swap(after(cotangent, q_t)[..., blk:], "ctx", nc, last)
            q_t = after(q_t, b1_y, b2_z)
        att = lambda *tail: pl.BlockSpec((1,) + tail, lambda g, t: (g,) + (0,) * len(tail))
        prob, o_t, inv_l = pl.pallas_call(
            functools.partial(attend_kernel, pairs),
            grid_spec=pltpu.PrefetchScalarGridSpec(
                num_scalar_prefetch=1,
                grid=(GROUPS,),
                in_specs=[att(2, AUG, wide_q), att(nc, AUG, rows), att(nc, AUG, rows)],
                out_specs=[att(pairs, blk, wide_q), att(2, HEAD, wide_q), att(2, 1, wide_q)],
                scratch_shapes=[pltpu.VMEM((pairs, blk, wide_q), F32), pltpu.VMEM((2, 8, wide_q), F32),
                                pltpu.VMEM((2, AUG, wide_q), F32)],
            ),
            out_shape=[jax.ShapeDtypeStruct((GROUPS, pairs, blk, wide_q), BF),
                       jax.ShapeDtypeStruct((GROUPS, 2, HEAD, wide_q), BF),
                       jax.ShapeDtypeStruct((GROUPS, 2, 1, wide_q), F32)],
            compiler_params=params(),
            cost_estimate=pl.CostEstimate(flops=12_000_000_000, bytes_accessed=12_000_000, transcendentals=0),
            name="attend",
        )(table, q_t, k_t, v_t)
        if box and s == 1:
            prob, o_t, inv_l, b1_far, b2_far, cot_got = lax.optimization_barrier((prob, o_t, inv_l, b1_far, b2_far, cot_got))
            weights = [v.reshape(2, 2, 4, shard, 2 * fn) for v in (b1_y, b1_far)]
            weights += [v.reshape(4, 2, 2, shard, 640) for v in (b2_z, b2_far)]
        saved.append((x_own, cos_t, sin_t, h1, k_t, v_t, q_t, prob, o_t, inv_l))

    total = seqs * rows
    steps = 2
    fstep = ff // steps
    once = lambda *shape: pl.BlockSpec(shape, lambda f, t: (0,) * len(shape), pipeline_mode=pl.Buffered(1))
    if box:
        weight_specs = [pl.BlockSpec((1, 2, 4, shard, 2 * fn), lambda f, t: (jnp.bitwise_xor(f, t[97] // 2), 0, 0, 0, 0))] * 2
        weight_specs += [once(4, 2, 2, shard, 640)] * 2
        weight_scratch = [pltpu.VMEM((width, fstep), BF)] * 3 + [pltpu.VMEM((width, 640), BF)]
    else:
        weights = [wg, wu, wd, wo]
        weight_specs = [pl.BlockSpec((width, fstep), lambda f, t: (0, f))] * 3 + [once(width, 640)]
        weight_scratch = []
    fixed = lambda *shape: pl.BlockSpec(shape, lambda f, t: (0,) * len(shape))
    if box:
        grad_specs = [fixed(16, shard, 2 * fn)] * 2 + [fixed(16, shard, 640)] * 2
        grad_shapes = [jax.ShapeDtypeStruct((16, shard, 2 * fn), BF)] * 2 + [jax.ShapeDtypeStruct((16, shard, 640), BF)] * 2
    else:
        grad_specs = [pl.BlockSpec((width, fstep), lambda f, t: (0, f))] * 2
        grad_specs += [pl.BlockSpec((width, fstep), lambda f, t: (0, f)), fixed(width, 640)]
        grad_shapes = [jax.ShapeDtypeStruct((width, ff), BF)] * 3 + [jax.ShapeDtypeStruct((width, 640), BF)]
    out_near, out_far, d_middle, do_t, *grads = pl.pallas_call(
        functools.partial(middle_kernel, box, nd, nc, seqs),
        grid_spec=pltpu.PrefetchScalarGridSpec(
            num_scalar_prefetch=1,
            grid=(steps,),
            in_specs=[once(width, rows), once(GROUPS, 2, HEAD, wide_q)] * seqs
            + [once(seqs, width, rows), once(seqs, width, blk)] + weight_specs,
            out_specs=[fixed(seqs, width, blk), fixed(seqs, width, blk), fixed(seqs, width, rows), fixed(seqs, GROUPS, 2, HEAD, wide_q)] + grad_specs,
            scratch_shapes=[pltpu.VMEM((qd, total), BF), pltpu.VMEM((width, total), F32), pltpu.VMEM((width, total), BF),
                            pltpu.VMEM((width, total), BF), pltpu.VMEM((width, total), F32), pltpu.VMEM((width, total), F32)]
            + weight_scratch,
        ),
        out_shape=[jax.ShapeDtypeStruct((seqs, width, blk), BF), jax.ShapeDtypeStruct((seqs, width, blk), BF),
                   jax.ShapeDtypeStruct((seqs, width, rows), F32),
                   jax.ShapeDtypeStruct((seqs, GROUPS, 2, HEAD, wide_q), BF)] + grad_shapes,
        compiler_params=params(),
        cost_estimate=pl.CostEstimate(flops=36_000_000_000, bytes_accessed=20_000_000, transcendentals=0),
        name="middle",
    )(places, *[v[k] for v in saved for k in (0, 8)], cotangent, cot_got, *weights)

    def settle(pieces):
        x = jnp.take(jnp.take(pieces, jnp.argsort(dslot), axis=0), jnp.argsort(cslot), axis=1)
        x = jnp.swapaxes(x, 0, 1).reshape((nc * nd,) + pieces.shape[2:])
        return gather_up(x, wsteps, sizes).astype(F32)

    def cut(g):
        r, c = g.shape
        return g.reshape(nd, r // nd, nc, c // nc).transpose(0, 2, 1, 3)

    def repeat(column):
        return jnp.broadcast_to(column.reshape(nd, 1, shard, 1), (nd, nc, shard, 1))

    if box:
        b1_got = swap(grads[1], "ctx", nc, 1)
        b2_got = swap(grads[3], "ctx", nc, 1)
    else:
        gate_sum, up_sum, down_sum = settle(cut(grads[0])), settle(cut(grads[1])), settle(cut(grads[2].T))
        b2_sum = settle(jnp.concatenate([cut(grads[3][:, :qd]), repeat(grads[3][:, qd])], axis=-1))
        out_sum, gain2_sum = b2_sum[:, :qn], b2_sum[:, qn]

    out_away = swap(out_far, "ctx", nc, last)
    half = nc // 2
    backs, dkv_owns = [], []
    for s in range(seqs):
        _, cos_t, sin_t, h1, k_t, v_t, q_t, prob, o_t, inv_l = saved[s]
        if s:
            q_t = after(q_t, backs[0][0], *((b1 + b2) if box else ()))
        att = lambda *tail: pl.BlockSpec((1,) + tail, lambda g, t: (g,) + (0,) * len(tail))
        fixed = lambda *shape: pl.BlockSpec(shape, lambda g, t: (0,) * len(shape))
        pair_of = pl.BlockSpec((1, 1, 2, HEAD, wide_q), lambda g, t: (s, g, 0, 0, 0))
        count = 1 if box and s == 0 else half
        kv_out = pl.BlockSpec((count, 2, 1, HEAD, rows), lambda g, t: (0, 0, g, 0, 0))
        dq_t, *kvs = pl.pallas_call(
            functools.partial(attend_back_kernel, pairs, tuple(place[r] for r in range(nc))),
            grid_spec=pltpu.PrefetchScalarGridSpec(
                num_scalar_prefetch=1,
                grid=(GROUPS,),
                in_specs=[att(pairs, blk, wide_q), att(2, AUG, wide_q), att(nc, AUG, rows), att(nc, AUG, rows),
                          att(2, HEAD, wide_q), pair_of, att(2, 1, wide_q), fixed(nc, HALF, rows), fixed(nc, HALF, rows)],
                out_specs=[att(SHARE, HEAD, rows)] + [kv_out] * (nc // count),
                scratch_shapes=[pltpu.VMEM((2, AUG, wide_q), BF), pltpu.VMEM((2 * nc, HEAD, blk), F32),
                                pltpu.VMEM((2 * nc, HEAD, blk), F32), pltpu.VMEM((2, HEAD, wide_q), F32)],
            ),
            out_shape=[jax.ShapeDtypeStruct((GROUPS, SHARE, HEAD, rows), BF)]
            + [jax.ShapeDtypeStruct((count, 2, GROUPS, HEAD, rows), BF)] * (nc // count),
            compiler_params=params(),
            cost_estimate=pl.CostEstimate(flops=20_000_000_000, bytes_accessed=12_000_000, transcendentals=0),
            name="attend_back",
        )(table, prob, q_t, k_t, v_t, o_t, do_t, inv_l, cos_t, sin_t)
        if box and s == 0:
            dq_t, b1_got, b2_got, out_away, *kvs = lax.optimization_barrier((dq_t, b1_got, b2_got, out_away, *kvs))
        if box and s == 1:
            dq_t, b1_got, z_got, dkv0, *kvs = lax.optimization_barrier((dq_t, b1_got, z_got, dkv0, *kvs))
            dkv_owns[0] = [dkv_owns[0][0]] + list(dkv0)
        kvs = [v.reshape(count, 2 * kvd, rows) for v in kvs]
        backs.append([dq_t.reshape(qd, rows), h1] + kvs)
        if box and s == 0:
            dkv0 = [swap(v, "ctx", nc, piece_rel(k)) for k, v in enumerate(kvs) if k]
            dkv_owns.append(kvs[:1])
            b1, b2 = add(grads[0], b1_got), add(grads[2], b2_got)
            b1_got = swap(b1[1], "dp", nd, 1)
            z_got = swap(b2[1][:4], "dp", nd, 4)
        else:
            dkv_got = swap(kvs[1], "ctx", nc, csteps[-1][1])
            if box:
                b1 = add(b1[0], b1_got)
                b1_got = swap(b1[1], "ctx", nc, 2)
                b2_parts = [b2[0][:4], z_got] + [swap(p, "dp", nd, m) for p, m in ((b2[0][4:], 2), (b2[1][4:], 6))]
            low, high = add(kvs[0], dkv_got)
            dkv_owns.append([low, swap(high, "ctx", nc, csteps[0][1])])

    def token(s, dqr_t):
        return pl.pallas_call(
            token_kernel,
            grid=(1,),
            in_specs=[pl.BlockSpec((1, 2 * kvd, rows), lambda i: (0, 0, 0))] * len(dkv_owns[s])
            + [pl.BlockSpec((qd, rows), lambda i: (0, 0)), pl.BlockSpec((width, 1024), lambda i: (0, 0)),
               pl.BlockSpec((width, rows), lambda i: (0, 0)), pl.BlockSpec((1, width, rows), lambda i: (s, 0, 0))],
            out_specs=[pl.BlockSpec((width, blk), lambda i: (0, 0))] * 2,
            out_shape=[jax.ShapeDtypeStruct((width, blk), BF)] * 2,
            compiler_params=params(),
            cost_estimate=pl.CostEstimate(flops=4_000_000_000, bytes_accessed=5_000_000, transcendentals=0),
            name="token",
        )(*dkv_owns[s], dqr_t, w_all, saved[s][0], d_middle)

    near0, far0 = token(0, after(backs[0][0], backs[1][0], dkv_owns[1][0], *((b1[0],) if box else ())))
    away0 = swap(far0, "ctx", nc, last)
    spot = [place[r] for r in range(nc)]
    hid_of = pl.BlockSpec((1, width, rows), lambda r, t: (t[99 + r], 0, 0))
    fixed = lambda *shape: pl.BlockSpec(shape, lambda r, t: (0,) * len(shape))
    if box:
        a_specs = [fixed(16, shard, 256)] * 2
        a_shapes = [jax.ShapeDtypeStruct((16, shard, 256), BF)] * 2
    else:
        a_specs, a_shapes = [fixed(width, 1024)], [jax.ShapeDtypeStruct((width, 1024), BF)]
    ops = [v for back in backs for v in back]
    ops[0] = after(ops[0], near0)
    places = jnp.concatenate([places, jnp.asarray([spot.index(i) for i in range(nc)], jnp.int32)])
    a_out = pl.pallas_call(
        functools.partial(post_kernel, box, nd, nc, tuple(len(v) for v in backs)),
        grid_spec=pltpu.PrefetchScalarGridSpec(
            num_scalar_prefetch=1,
            grid=(nc,),
            in_specs=[sp for back in backs for sp in [fixed(qd, rows), hid_of] + [fixed(*v.shape) for v in back[2:]]] + [fixed(width, 1024)],
            out_specs=a_specs,
            scratch_shapes=[pltpu.VMEM((width, 1024), F32)],
        ),
        out_shape=a_shapes,
        compiler_params=params(),
        cost_estimate=pl.CostEstimate(flops=15_000_000_000, bytes_accessed=10_000_000, transcendentals=0),
        name="post",
    )(places, *ops, w_all)

    if box:
        *a_out, b1_got, b2_parts, away0 = lax.optimization_barrier((*a_out, b1_got, b2_parts, away0))
        a_got = swap(a_out[1], "ctx", nc, 1)
        a_got, dkv_owns[1] = lax.optimization_barrier((a_got, dkv_owns[1]))
        total_of = lambda parts: sum(p.astype(F32) for p in parts)
        b2 = total_of(b2_parts).astype(BF)
        b2_got = swap(b2[2:], "dp", nd, 1)
        b1 = add(b1[0], b1_got)
        a = add(a_out[0], a_got)
        a_got = swap(a[1], "dp", nd, 1)
        b1_parts = [b1[0][0]] + [swap(p, "dp", nd, m) for p, m in zip((b1[0][1], b1[1][0], b1[1][1]), Z_MASKS)]
    mine, away = token(1, after(backs[1][0], *((a[0], b2[0]) if box else ())))
    if box:
        mine, away, a_got, b1_parts, b2_got = lax.optimization_barrier((mine, away, a_got, b1_parts, b2_got))
    token_near, token_away = [near0, mine], [away0, swap(away, "ctx", nc, last)]
    if box:
        a = add(a[0], a_got)
        b2 = (b2[:2].astype(F32) + b2_got.astype(F32)).astype(BF)
        b2_got = swap(b2[1], "ctx", nc, 2)
        a = fold(*a, "ctx", 2, sizes)
        a, b2_got = lax.optimization_barrier((a, b2_got))
        b1_sum = total_of(b1_parts)
        b2_sum = b2[0].astype(F32) + b2_got.astype(F32)
        gate_sum, up_sum = b1_sum[:, :fn], b1_sum[:, fn:]
        out_sum, gain2_sum, down_sum = b2_sum[:, :qn], b2_sum[:, qn], unfold_down(b2_sum[:, 256:]).T

    if box:
        low, high = a
        a_parts = [low[0]] + [swap(p, "dp", nd, m) for p, m in zip((low[1], high[0], high[1]), Z_MASKS)]
        a_parts, token_away = lax.optimization_barrier((a_parts, token_away))
        a_sum = total_of(a_parts)
    else:
        a = a_out[0]
        a_sum = settle(jnp.concatenate(
            [cut(a[:, :qd]), cut(a[:, qd : qd + kvd]), cut(a[:, qd + kvd : qd + 2 * kvd]), repeat(a[:, 960])], axis=-1))

    def home(mine, away):
        return jnp.swapaxes(jnp.concatenate([mine, away], axis=-1), 1, 2)

    return (
        home(out_near, out_away),
        home(jnp.stack(token_near), jnp.stack(token_away)),
        a_sum[:, 2 * kn + qn],
        a_sum[:, :qn],
        a_sum[:, qn : qn + kn],
        a_sum[:, qn + kn : qn + 2 * kn],
        out_sum,
        gain2_sum,
        gate_sum,
        up_sum,
        down_sum,
    )


def pair_table(nc):
    out = []
    for me in range(nc):
        spots = {}
        for r in range(nc):
            d = me ^ r
            spots[2 * d] = 2 * r
            spots[2 * (nc - 1 - d) + 1] = 2 * r + 1
        mine = [2 * me, 2 * (nc - 1 - me) + 1]
        rows = [(i, spots[mine[i]]) for i in range(2)]
        rows += [(i, spots[k]) for i in range(2) for k in range(mine[i])]
        out.append(rows)
    return np.array(out, np.int32)


def turn(x, cos, sin, heads, sign):
    parts = []
    for h in range(heads):
        lo, hi = x[h * HEAD : h * HEAD + HALF], x[h * HEAD + HALF : (h + 1) * HEAD]
        parts += [lo * cos - sign * hi * sin, hi * cos + sign * lo * sin]
    return jnp.concatenate(parts, axis=0)


def unpack_a_kernel(places, own_ref, other_ref, w_ref):
    nd = w_ref.shape[0]
    nc = 4
    qn, kn = 144, 48
    qd, kvd = qn * nc, kn * nc

    def write(cores):
        for d in range(nd):
            for c in range(nc):
                p = cores[c % 2][places[d * nc + c]].astype(F32)
                if c == 0:
                    cols = [[], [], []]
                    gain = p[:, 240:256]
                cols[0].append(p[:, :qn])
                cols[1].append(p[:, qn : qn + kn])
                cols[2].append(p[:, qn + kn : qn + 2 * kn])
            row = cols[0] + cols[1] + cols[2] + [gain, jnp.zeros((p.shape[0], 48), F32)]
            w_ref[d] = jnp.concatenate(row, axis=1).astype(BF)

    core = places[96]
    pl.when(core == 0)(lambda: write((own_ref, other_ref)))
    pl.when(core == 1)(lambda: write((other_ref, own_ref)))


def pre_kernel(own_ref, got_ref, own2_ref, got2_ref, w_ref, cos_ref, sin_ref, seg_ref, h_ref, k_ref, v_ref, q_ref, x_ref):
    mine = lax.rem(pl.program_id(0), 2) == 0
    x = jnp.concatenate([jnp.where(mine, own_ref[0].astype(F32), got_ref[0].astype(F32)),
                         jnp.where(mine, got2_ref[0].astype(F32), own2_ref[0].astype(F32))], axis=1)
    inv = lax.rsqrt(jnp.mean(x * x, axis=0, keepdims=True) + EPS)
    qd, kvd = HEADS * HEAD, GROUPS * HEAD
    gain = w_ref[:, qd + 2 * kvd : qd + 2 * kvd + 1].astype(F32)
    h = ((x * inv) * gain).astype(BF)
    h_ref[0] = h
    cos, sin, seg = cos_ref[0], sin_ref[0], seg_ref[0]
    rows = x.shape[1]
    blk = rows // 2
    kv = dot(w_ref[:, qd : qd + 2 * kvd], h, TN)
    keys = turn(kv[:kvd], cos, sin, GROUPS, 1.0).astype(BF)
    values = kv[kvd:].astype(BF)
    row = lax.broadcasted_iota(jnp.int32, (AUG - HEAD, rows), 0)
    other = jnp.where((row < 3) & (row != seg), -1e30, 0.0).astype(BF)
    ones = (row < 3).astype(BF)
    for g in range(GROUPS):
        k_ref[g, 0, :HEAD] = keys[g * HEAD : (g + 1) * HEAD]
        k_ref[g, 0, HEAD:] = other
        v_ref[g, 0, :HEAD] = values[g * HEAD : (g + 1) * HEAD]
        v_ref[g, 0, HEAD:] = ones

    @pl.when(pl.program_id(0) == 0)
    def _():
        q = turn(dot(w_ref[:, :qd], h, TN), cos, sin, HEADS, 1.0).astype(BF) * (1.0 / math.sqrt(HEAD))
        x_ref[...] = x.astype(BF)
        same = (row == seg).astype(BF)
        for g in range(GROUPS):
            for b in range(2):
                for j in range(SHARE):
                    n = g * SHARE + j
                    q_ref[g, b, :HEAD, j * blk : (j + 1) * blk] = q[n * HEAD : (n + 1) * HEAD, b * blk : (b + 1) * blk]
                    q_ref[g, b, HEAD:, j * blk : (j + 1) * blk] = same[:, b * blk : (b + 1) * blk]


def by_core(core, refs, write):
    pairs = [refs[i : i + 2] for i in range(0, len(refs), 2)]
    pl.when(core == 0)(lambda: write(*pairs))
    pl.when(core == 1)(lambda: write(*[p[::-1] for p in pairs]))


def join_weights(places, f, g_ref, u_ref, w_ref, o_ref, one, two):
    fn = one[0].shape[-1] // 2
    me_y, me_x, me_z = places[97] // 2, places[98] % 2, places[98] // 2
    flip = jnp.bitwise_xor
    high = one[0].shape[-2]

    def stack(ref, i, rows):
        ref[2 * high * i : 2 * high * (i + 1)] = jnp.concatenate(rows, axis=0).astype(BF)

    for z in range(4):
        at_z = flip(z, me_z)
        rows = [[one[k][0, flip(x, me_x), at_z].astype(F32) for k in range(2)] for x in range(2)]
        stack(g_ref, z, [jnp.concatenate([p[:, :fn] for p in row], axis=1) for row in rows])
        stack(u_ref, z, [jnp.concatenate([p[:, fn:] for p in row], axis=1) for row in rows])
    for c in range(4):
        y = flip(c // 2, me_y)
        pieces = [two[c % 2][flip(2 * f + i // 2, me_z), flip(i % 2, me_x), y, :, 256:640].astype(F32) for i in range(4)]
        stack(w_ref, c, [jnp.concatenate([p[:, j * 192 : (j + 1) * 192] for p in pieces], axis=1) for j in range(2)])

    @pl.when(f == 0)
    def _():
        for z in range(4):
            rows = []
            for x in range(2):
                pieces = [two[c % 2][flip(z, me_z), flip(x, me_x), flip(c // 2, me_y), :, :256].astype(F32) for c in range(4)]
                rows.append(jnp.concatenate([p[:, :144] for p in pieces] + [pieces[0][:, 144:208]], axis=1))
            stack(o_ref, z, rows)


def middle_kernel(box, nd, nc, seqs, places, *refs):
    xs, refs = refs[: 2 * seqs], refs[2 * seqs :]
    cot_ref, got_ref, wg_ref, wu_ref, wd_ref, wo_ref, near_ref, far_ref, dm_ref, do_ref, *rest = refs
    grads, (att_ref, mid_ref, h_ref, cots_ref, acc_ref, dh_ref), made = rest[:4], rest[4:10], rest[10:]
    f = pl.program_id(0)
    if box:
        parts = (wg_ref, wu_ref, wd_ref, wo_ref)
        wg_ref, wu_ref, wd_ref, wo_ref = made
        by_core(places[96], parts, functools.partial(join_weights, places, f, *made))
    blk = got_ref.shape[2]
    rows = 2 * blk
    qd, width = HEADS * HEAD, cot_ref.shape[1]
    shard = width // nd
    fn = wg_ref.shape[1]
    steps = 2
    part_fn = fn * steps // nc

    def norm():
        m = mid_ref[...]
        inv = lax.rsqrt(jnp.mean(m * m, axis=0, keepdims=True) + EPS)
        return m, inv, m * inv

    def gain_column():
        return wo_ref[:, qd : qd + 1].astype(F32)

    def of(s):
        return slice(s * rows, (s + 1) * rows)

    def blocks():
        for s in range(seqs):
            for g in range(GROUPS):
                for b in range(2):
                    for j in range(SHARE):
                        n = g * SHARE + j
                        yield (s, g, b, slice(None), slice(j * blk, (j + 1) * blk)), (
                            slice(n * HEAD, (n + 1) * HEAD), slice(s * rows + b * blk, s * rows + (b + 1) * blk))

    @pl.when(f == 0)
    def _():
        for there, here in blocks():
            att_ref[here] = xs[2 * there[0] + 1][there[1:]]
        branch = dot(wo_ref[:, :qd], att_ref[...], TN)
        for s in range(seqs):
            mid_ref[:, of(s)] = xs[2 * s][...].astype(F32) + branch[:, of(s)]
            cots_ref[:, s * rows : s * rows + blk] = cot_ref[s, :, :blk]
            cots_ref[:, s * rows + blk : (s + 1) * rows] = got_ref[s]
        _, _, n2 = norm()
        h_ref[...] = (n2 * gain_column()).astype(BF)

    h = h_ref[...]
    cot = cots_ref[...]
    gate = dot(wg_ref[...], h, TN)
    up = dot(wu_ref[...], h, TN)
    sig = jax.nn.sigmoid(gate)
    act = gate * sig
    inner = (act * up).astype(BF)
    part = dot(wd_ref[...], inner, NN)
    d_inner = dot(wd_ref[...], cot, TN)
    d_gate = (d_inner * up * (sig + act * (1.0 - sig))).astype(BF)
    d_up = (d_inner * act).astype(BF)
    d_part = dot(wg_ref[...], d_gate, NN) + dot(wu_ref[...], d_up, NN)

    @pl.when(f == 0)
    def _():
        acc_ref[...] = part
        dh_ref[...] = d_part

    @pl.when(f > 0)
    def _():
        acc_ref[...] += part
        dh_ref[...] += d_part

    grad_gate = dot(h, d_gate, NT)
    grad_up = dot(h, d_up, NT)
    grad_down = dot(cot, inner, NT)
    if box:
        cols = width // nc
        per = fn * steps // nd

        def pack(b1s, b2s):
            for k in range(nc // steps):
                c = f * (nc // steps) + k
                lanes = slice(k * part_fn, (k + 1) * part_fn)
                for d in range(nd):
                    part_rows = slice(d * shard, (d + 1) * shard)
                    at = places[d * nc + c]
                    b1s[k % 2][at, :, :part_fn] = grad_gate[part_rows, lanes].astype(BF)
                    b1s[k % 2][at, :, part_fn:] = grad_up[part_rows, lanes].astype(BF)
            for i in range(fn // per):
                for c in range(nc):
                    p = fold_down(grad_down[c * cols : (c + 1) * cols, i * per : (i + 1) * per]).astype(BF)
                    b2s[c % 2][places[32 + (f * (fn // per) + i) * nc + c], :, 256:640] = p

        by_core(places[96], grads, pack)
    else:
        grads[0][...] = grad_gate.astype(BF)
        grads[1][...] = grad_up.astype(BF)
        grads[2][...] = grad_down.astype(BF)

    @pl.when(f == pl.num_programs(0) - 1)
    def _():
        m, inv, n2 = norm()
        out = (m + acc_ref[...]).astype(BF)
        d_h2 = dh_ref[...]
        e2 = d_h2 * gain_column()
        d_middle = cots_ref[...].astype(F32) + inv * (e2 - n2 * jnp.mean(e2 * n2, axis=0, keepdims=True))
        for s in range(seqs):
            near_ref[s] = out[:, s * rows : s * rows + blk]
            far_ref[s] = out[:, s * rows + blk : (s + 1) * rows]
            dm_ref[s] = d_middle[:, of(s)]
        branch = d_middle.astype(BF)
        d_att = dot(wo_ref[:, :qd], branch, NN).astype(BF)
        for there, here in blocks():
            do_ref[there] = d_att[here]
        grad_out = dot(att_ref[...], branch, NT)
        gain = jnp.broadcast_to(jnp.sum(d_h2 * n2, axis=1, keepdims=True), (width, 128))
        if box:
            def pack_out(b1s, b2s):
                for d in range(nd):
                    part_rows = slice(d * shard, (d + 1) * shard)
                    for c in range(nc):
                        p = jnp.concatenate([grad_out[part_rows, c * cols : (c + 1) * cols], gain[part_rows, :112]], axis=1)
                        b2s[c % 2][places[32 + d * nc + c], :, :256] = p.astype(BF)

            by_core(places[96], grads, pack_out)
        else:
            grads[3][...] = jnp.concatenate([grad_out, gain[:, :64]], axis=1).astype(BF)


def post_kernel(box, nd, nc, counts, places, *refs):
    seqs = []
    for n in counts:
        seqs.append(refs[:n])
        refs = refs[n:]
    w_ref, outs, acc_ref = refs[0], refs[1:-1], refs[-1]
    kvd, qd = GROUPS * HEAD, HEADS * HEAD
    r = pl.program_id(0)

    @pl.when(r == 0)
    def _():
        acc_ref[...] = jnp.zeros_like(acc_ref)
        acc_ref[:, :qd] = sum(dot(h_ref[0], dq_ref[...], NT) for dq_ref, h_ref, *_ in seqs)

    for k in range(nc):
        @pl.when(r == k)
        def _():
            terms = []
            for _, h_ref, *kvs in seqs:
                n = nc // len(kvs)
                terms.append(dot(h_ref[0], kvs[k // n][k % n], NT))
            acc_ref[:, qd : qd + 2 * kvd] += sum(terms)

    @pl.when(r == nc - 1)
    def _():
        g = acc_ref[...]
        w = w_ref[...].astype(F32)
        used = qd + 2 * kvd
        gain = jnp.sum(g[:, :used] * w[:, :used], axis=1, keepdims=True) / w[:, used : used + 1]
        if not box:
            outs[0][...] = jnp.concatenate([g[:, :used], jnp.broadcast_to(gain, (g.shape[0], 64))], axis=1).astype(BF)
            return
        shard = g.shape[0] // nd
        gain = jnp.broadcast_to(gain, (g.shape[0], 16))
        qn, kn = qd // nc, kvd // nc

        def pack(both):
            for d in range(nd):
                r = slice(d * shard, (d + 1) * shard)
                for c in range(nc):
                    p = jnp.concatenate(
                        [g[r, c * qn : (c + 1) * qn], g[r, qd + c * kn : qd + (c + 1) * kn],
                         g[r, qd + kvd + c * kn : qd + kvd + (c + 1) * kn], gain[r]], axis=1)
                    both[c % 2][places[d * nc + c]] = p.astype(BF)

        by_core(places[96], outs, pack)


def token_kernel(*refs):
    *kvs, dq_ref, w_ref, x_ref, dm_ref, near_ref, far_ref = refs
    qd, kvd = HEADS * HEAD, GROUPS * HEAD
    x = x_ref[...].astype(F32)
    inv = lax.rsqrt(jnp.mean(x * x, axis=0, keepdims=True) + EPS)
    n1 = x * inv
    dkv = sum(v[0].astype(F32) for v in kvs).astype(BF)
    d_h1 = dot(w_ref[:, :qd], dq_ref[...], NN) + dot(w_ref[:, qd : qd + 2 * kvd], dkv, NN)
    e1 = d_h1 * w_ref[:, qd + 2 * kvd : qd + 2 * kvd + 1].astype(F32)
    out = (dm_ref[0] + inv * (e1 - n1 * jnp.mean(e1 * n1, axis=0, keepdims=True))).astype(BF)
    blk = near_ref.shape[1]
    near_ref[...] = out[:, :blk]
    far_ref[...] = out[:, blk:]


def key_block(ref, loc, blk, rows=None):
    r, half = loc // 2, loc % 2
    lanes = pl.ds(pl.multiple_of(half * blk, blk), blk)
    if rows is None:
        return ref[0, r, :, lanes]
    return ref[0, r, :rows, lanes]


def attend_kernel(pairs, table, q_ref, k_ref, v_ref, p_ref, o_ref, l_ref, s_ref, m_ref, acc_ref):
    wide = q_ref.shape[-1]
    blk = wide // SHARE

    def score(t, diagonal):
        qb, loc = table[2 * t], table[2 * t + 1]
        s = dot(key_block(k_ref, loc, blk), q_ref[0, qb], TN)
        if diagonal:
            k_at = lax.broadcasted_iota(jnp.int32, (blk, wide), 0)
            q_at = lax.broadcasted_iota(jnp.int32, (blk, wide), 1) % blk
            s = jnp.where(k_at <= q_at, s, -1e30)
        s_ref[t] = s
        top = jnp.max(s.reshape(blk // 8, 8, wide), axis=0)
        if diagonal:
            m_ref[qb] = top
        else:
            m_ref[qb] = jnp.maximum(m_ref[qb], top)

    for t in range(2):
        score(t, True)
    lax.fori_loop(2, pairs, lambda t, c: (score(t, False), c)[1], 0, unroll=pairs - 2)
    for b in range(2):
        m_ref[b] = jnp.broadcast_to(jnp.max(m_ref[b], axis=0, keepdims=True), m_ref.shape[1:])
    acc_ref[...] = jnp.zeros_like(acc_ref)

    def weigh(t, c):
        qb, loc = table[2 * t], table[2 * t + 1]
        p = jnp.exp(s_ref[t] - m_ref[qb, 0:1]).astype(BF)
        p_ref[0, t] = p
        acc_ref[qb] += dot(key_block(v_ref, loc, blk), p, NN)
        return c

    lax.fori_loop(0, pairs, weigh, 0, unroll=pairs)
    for b in range(2):
        inv = 1.0 / acc_ref[b, HEAD : HEAD + 1]
        l_ref[0, b] = inv
        o_ref[0, b] = (acc_ref[b, :HEAD] * inv).astype(BF)


def attend_back_kernel(pairs, order, table, p_ref, q_ref, k_ref, v_ref, o_ref, do_ref, l_ref, cos_ref, sin_ref,
                       dq_ref, *rest):
    *outs, da_ref, dka_ref, dva_ref, dqa_ref = rest
    wide = q_ref.shape[-1]
    blk = wide // SHARE
    row = lax.broadcasted_iota(jnp.int32, (AUG - HEAD, wide), 0)
    for b in range(2):
        d = (do_ref[0, 0, b].astype(F32) * l_ref[0, b]).astype(BF)
        delta = -jnp.sum(d.astype(F32) * o_ref[0, b].astype(F32), axis=0, keepdims=True)
        hi = delta.astype(BF).astype(F32)
        mid = (delta - hi).astype(BF).astype(F32)
        low = delta - hi - mid
        da_ref[b, :HEAD] = d
        da_ref[b, HEAD:] = jnp.where(row == 0, hi, jnp.where(row == 1, mid, jnp.where(row == 2, low, 0.0))).astype(BF)
    dka_ref[...] = jnp.zeros_like(dka_ref)
    dva_ref[...] = jnp.zeros_like(dva_ref)
    dqa_ref[...] = jnp.zeros_like(dqa_ref)

    def step(t, c):
        qb, loc = table[2 * t], table[2 * t + 1]
        p = p_ref[0, t]
        dp = dot(key_block(v_ref, loc, blk), da_ref[qb], TN)
        ds = (p.astype(F32) * dp).astype(BF)
        dqa_ref[qb] += dot(key_block(k_ref, loc, blk, HEAD), ds, NN)
        dka_ref[loc] += dot(q_ref[0, qb, :HEAD], ds, NT)
        dva_ref[loc] += dot(da_ref[qb, :HEAD], p, NT)
        return c

    lax.fori_loop(0, pairs, step, 0, unroll=pairs)
    scale = 1.0 / math.sqrt(HEAD)
    for b in range(2):
        lanes = slice(b * blk, (b + 1) * blk)
        cos, sin = cos_ref[0, :, lanes] * scale, sin_ref[0, :, lanes] * scale
        for j in range(SHARE):
            dq_ref[0, j, :, lanes] = turn(dqa_ref[b, :, j * blk : (j + 1) * blk], cos, sin, 1, -1.0).astype(BF)
    n = len(order) // len(outs)
    for r, at in enumerate(order):
        out_ref = outs[at // n]
        for b in range(2):
            lanes = slice(b * blk, (b + 1) * blk)
            cos, sin = cos_ref[r, :, lanes], sin_ref[r, :, lanes]
            out_ref[at % n, 0, 0, :, lanes] = turn(dka_ref[2 * r + b], cos, sin, 1, -1.0).astype(BF)
            out_ref[at % n, 1, 0, :, lanes] = dva_ref[2 * r + b].astype(BF)


def solution(mesh):
    sizes = {name: mesh.shape[name] for name in ("dp", "ctx")}
    rows = P("dp", "ctx", None)
    grid = P("dp", "ctx")
    line = P("dp")
    return jax.shard_map(
        functools.partial(per_device, sizes),
        mesh=mesh,
        in_specs=(rows, grid, line, grid, grid, grid, grid, line, grid, grid, grid, rows),
        out_specs=(rows, rows, line, grid, grid, grid, grid, line, grid, grid, grid),
        check_vma=False,
    )
```
